32 devices in a mesh: group: 4 (over x, core), dp: 8 (over z, y).
Axes of the slice: x: 2, y: 2, z: 4, core: 2. Of those that a mesh axis runs over, the one named last changes fastest.
Arguments:
- tokens: bfloat16 [36864, 768], P(('group', 'dp')), may hold values from -6 to 6
- cotangent: bfloat16 [36864, 768], P(('group', 'dp')), may hold values from -6 to 6
- norm1_gain: bfloat16 [768], replicated, may hold values from 0.38 to 2.3
- norm1_bias: bfloat16 [768], replicated, may hold values from -1.1953125 to 1.1953125
- qkv_weight: bfloat16 [768, 2304], replicated, may hold values from -0.21875 to 0.21875
- qkv_bias: bfloat16 [2304], replicated, may hold values from -1.1953125 to 1.1953125
- rotary_freqs: float32 [2, 12, 32], replicated, may hold values from -3 to 3
- out_weight: bfloat16 [768, 768], replicated, may hold values from -0.875 to 0.875
- out_bias: bfloat16 [768], replicated, may hold values from -1.1953125 to 1.1953125
- norm2_gain: bfloat16 [768], replicated, may hold values from 0.38 to 2.3
- norm2_bias: bfloat16 [768], replicated, may hold values from -1.1953125 to 1.1953125
- up_weight: bfloat16 [768, 3072], replicated, may hold values from -0.21875 to 0.21875
- up_bias: bfloat16 [3072], replicated, may hold values from -1.1953125 to 1.1953125
- down_weight: bfloat16 [3072, 768], replicated, may hold values from -0.109375 to 0.109375
- down_bias: bfloat16 [768], replicated, may hold values from -1.1953125 to 1.1953125
- group_res: int32 [4], P('group'), may hold values from 0 to 2, as said below
- images: int32 [32], P(('group', 'dp')), may hold values from 1 to 5, as said below
Outputs:
- output: bfloat16 [36864, 768], P(('group', 'dp'))
- input_grad: bfloat16 [36864, 768], P(('group', 'dp'))
- norm1_gain_grad: float32 [768], P('dp')
- norm1_bias_grad: float32 [768], P('dp')
- qkv_weight_grad: float32 [768, 2304], P('dp')
- qkv_bias_grad: float32 [2304], P('dp')
- rotary_grad: float32 [2, 12, 32], replicated
- out_weight_grad: float32 [768, 768], P('dp')
- out_bias_grad: float32 [768], P('dp')
- norm2_gain_grad: float32 [768], P('dp')
- norm2_bias_grad: float32 [768], P('dp')
- up_weight_grad: float32 [768, 3072], P('dp')
- up_bias_grad: float32 [3072], P('dp')
- down_weight_grad: float32 [3072, 768], P('dp')
- down_bias_grad: float32 [768], P('dp')
- weight_sq: float32 [], replicated
- rotary_sq: float32 [], replicated
The draws below stay inside these ranges and needn't reach their ends.
Inputs may be any that keep to these rules, and one draw needn't show every extreme that they name: `group_res`: resolution index 0 means 224 px images of 14 x 14 patches, 1 means 320 px (20 x 20), 2 means 384 px (24 x 24); each of the three is given to at least one group. A device holds between 1 and 1152 // p whole images of its group's resolution, p its patches per image; in every group some device holds that most.
All inputs are finite; a program needn't handle non-finite values.
Results may differ from the reference program's by a relative error of at most 0.013.
The reference program's roundings to bfloat16 on the way count: a program that leaves them out, or rounds other values in their place, can miss the bound.
Values sent between devices are 32-bit elements; how exact they have to be, the bound alone decides.
No kernel may reach another device: no remote copies, remote signals or barrier semaphores. Data moves between devices by JAX's collectives and lax.ppermute only.
A program may use at most 448 MiB of HBM per device.

```python
import math
import jax
import jax.numpy as jnp
from jax import lax

D = 768
HEADS = 12
HEAD = 64
FF = 3072
SLOTS = 1152
TOKENS = 36864
N_GROUP = 4
N_DP = 8


def resolution_table(key):
    table_key = jax.random.fold_in(key, 11)
    res_order = jax.random.permutation(table_key, 3)
    extra_res = jax.random.randint(jax.random.fold_in(table_key, 1), (N_GROUP - 3,), 0, 3)
    joined = jnp.concatenate([res_order, extra_res])
    placing = jax.random.permutation(jax.random.fold_in(table_key, 2), N_GROUP)
    return joined[placing].astype(jnp.int32)


def draw_group_res(key, part):
    return resolution_table(key)


def draw_images(key, part):
    res_table = resolution_table(key)
    key = jax.random.fold_in(key, 5)
    res_rows = jnp.repeat(res_table, N_DP)
    side_len = jnp.where(res_rows == 0, 14, jnp.where(res_rows == 1, 20, 24))
    capacity = SLOTS // (side_len * side_len)
    raw_bits = jax.random.randint(key, (N_GROUP * N_DP,), 0, 1 << 20)
    counted = 1 + raw_bits % capacity
    full_pick = jax.random.randint(jax.random.fold_in(key, 1), (N_GROUP,), 0, N_DP)
    slot_index = jnp.arange(N_GROUP * N_DP)
    full_mask = slot_index == jnp.repeat(full_pick + jnp.arange(N_GROUP) * N_DP, N_DP)
    return jnp.where(full_mask, capacity, counted).astype(jnp.int32)


def gain_profile(key, lowest, highest, jitter):
    place = jnp.arange(D, dtype=jnp.float32) / jnp.float32(D - 1)
    flip_draw = jax.random.uniform(jax.random.fold_in(key, 1), (), jnp.float32)
    place = jnp.where(flip_draw < 0.5, place, 1.0 - place)
    base_line = lowest * jnp.exp(place * jnp.log(highest / lowest))
    factor = jax.random.uniform(key, (D,), jnp.float32, 1.0 - jitter, 1.0 + jitter)
    return (base_line * factor).astype(jnp.bfloat16)


def draw_norm1_gain(key, part):
    key = jax.random.fold_in(key, 21)
    return gain_profile(key, 0.5, 1.8, 0.1)


def draw_norm2_gain(key, part):
    key = jax.random.fold_in(key, 23)
    return gain_profile(key, 0.5, 1.8, 0.1)


def level_of(key, extent, cuts, smallest, top_value):
    def one(position, blocks):
        steps = jax.random.uniform(jax.random.fold_in(jax.random.fold_in(key, 6), position), (blocks,), jnp.float32, smallest / len(cuts), top_value / len(cuts))
        return jnp.repeat(jnp.exp(steps), extent[position] // blocks).reshape((-1,) + (1,) * (len(extent) - position - 1))

    gain = one(*cuts[0])
    for cut in cuts[1:]:
        gain = gain * one(*cut)
    return gain


def bell_draw(key, shape, width, bound, pieces=(), kind=jnp.bfloat16):
    values = jax.random.normal(key, shape, jnp.float32) * width
    if len(pieces) > 0:
        values = level_of(key, shape, pieces, -0.22, 0.18) * values
    return jnp.clip(values, min=-bound, max=bound).astype(kind)


def setup_inputs(seed: int = 0) -> dict:
    splits = jax.random.split(jax.random.key(seed), 18)
    tokens = bell_draw(splits[0], (TOKENS, D), 1.0, 6.0, ((0, 32),))
    cotangent = bell_draw(splits[1], (TOKENS, D), 1.0, 6.0, ((0, 32),))
    norm1_gain = draw_norm1_gain(jax.random.fold_in(splits[17], 71), 0)
    norm1_bias = bell_draw(splits[3], (D,), 0.2, 1.1953125)
    qkv_weight = bell_draw(splits[4], (D, 3 * D), D ** -0.5, 0.21875)
    qkv_bias = bell_draw(splits[5], (3 * D,), 0.2, 1.1953125)
    rotary_freqs = bell_draw(splits[6], (2, HEADS, HEAD // 2), 0.5, 3.0, (), jnp.float32)
    out_weight = bell_draw(splits[7], (D, D), (D // 16) ** -0.5, 0.875)
    out_bias = bell_draw(splits[8], (D,), 0.2, 1.1953125)
    norm2_gain = draw_norm2_gain(jax.random.fold_in(splits[17], 71), 0)
    norm2_bias = bell_draw(splits[10], (D,), 0.2, 1.1953125)
    up_weight = bell_draw(splits[11], (D, FF), D ** -0.5, 0.21875)
    up_bias = bell_draw(splits[12], (FF,), 0.2, 1.1953125)
    down_weight = bell_draw(splits[13], (FF, D), FF ** -0.5, 0.109375)
    down_bias = bell_draw(splits[14], (D,), 0.2, 1.1953125)
    group_res = draw_group_res(jax.random.fold_in(splits[17], 71), 0)
    images = draw_images(jax.random.fold_in(splits[17], 71), 0)
    return dict(tokens=tokens, cotangent=cotangent, norm1_gain=norm1_gain, norm1_bias=norm1_bias, qkv_weight=qkv_weight, qkv_bias=qkv_bias, rotary_freqs=rotary_freqs, out_weight=out_weight, out_bias=out_bias, norm2_gain=norm2_gain, norm2_bias=norm2_bias, up_weight=up_weight, up_bias=up_bias, down_weight=down_weight, down_bias=down_bias, group_res=group_res, images=images)


@jax.custom_vjp
def low(v):
    return lax.optimization_barrier(v.astype(jnp.bfloat16)).astype(jnp.float32)

@jax.custom_vjp
def low_back(v):
    return v

def low_keep(v):
    return (low(v), None)

def low_pass(kept, grad):
    return (grad,)

def back_keep(v):
    return (v, None)

def back_low(kept, grad):
    return (low(grad),)
low.defvjp(low_keep, low_pass)
low_back.defvjp(back_keep, back_low)
HIGHEST = lax.Precision.HIGHEST
NEG_FILL = -1e+30
EPSILON = 1e-06

def layout_of(resolution, images_here, slot_count):
    side_len = jnp.where(resolution == 0, 14, jnp.where(resolution == 1, 20, 24)).astype(jnp.int32)
    patches = side_len * side_len
    slot_ids = jnp.arange(slot_count, dtype=jnp.int32)
    image_ids = slot_ids // patches
    within = slot_ids - image_ids * patches
    row_ids = within // side_len
    column_ids = within - row_ids * side_len
    live_mask = slot_ids < images_here * patches
    segment = jnp.where(live_mask, image_ids, -1 - slot_ids)
    return (row_ids.astype(jnp.float32), column_ids.astype(jnp.float32), live_mask, segment)

def normalize(values, norm_gain, norm_bias):
    center = lax.optimization_barrier(jnp.mean(values, axis=-1, keepdims=True))
    shifted = values - center
    inverse = lax.rsqrt(lax.optimization_barrier(jnp.mean(shifted * shifted, axis=-1, keepdims=True)) + EPSILON)
    normed = shifted * inverse
    return normed * norm_gain + norm_bias

def rotate(values, cosine, sine_part):
    half_dim = values.shape[-1] // 2
    first_half = values[..., :half_dim]
    second_half = values[..., half_dim:]
    return jnp.concatenate([first_half * cosine - second_half * sine_part, first_half * sine_part + second_half * cosine], axis=-1)

def block_forward(token_float, params, row_pos, column_pos, segment):
    norm1_gain, norm1_bias, qkv_weight, qkv_bias, rotary_freqs, out_weight, out_bias, norm2_gain, norm2_bias, up_weight, up_bias, down_weight, down_bias = params
    slot_count = token_float.shape[0]
    first_in = low(normalize(token_float, norm1_gain, norm1_bias))
    projected = low_back(jnp.dot(first_in, qkv_weight, precision=HIGHEST) + qkv_bias)
    triple = projected.reshape(slot_count, 3, HEADS, HEAD)
    angles = row_pos[:, None, None] * rotary_freqs[0] + column_pos[:, None, None] * rotary_freqs[1]
    cosine = jnp.cos(angles)
    sine_part = jnp.sin(angles)
    query_low = low(rotate(triple[:, 0], cosine, sine_part) * (1.0 / math.sqrt(HEAD)))
    key_low = low(rotate(triple[:, 1], cosine, sine_part))
    value_low = low(triple[:, 2])
    scores = low_back(jnp.einsum('qhd,khd->hqk', query_low, key_low, precision=HIGHEST))
    same_image = segment[:, None] == segment[None, :]
    scores = jnp.where(same_image[None], scores, NEG_FILL)
    row_max = lax.optimization_barrier(jnp.max(scores, axis=-1, keepdims=True))
    exp_scores = jnp.exp(scores - row_max)
    prob_mass = low(exp_scores / lax.optimization_barrier(jnp.sum(exp_scores, axis=-1, keepdims=True)))
    attn_mix = jnp.einsum('hqk,khd->qhd', prob_mass, value_low, precision=HIGHEST).reshape(slot_count, HEADS * HEAD)
    attended = low(low_back(attn_mix))
    middle = token_float + low_back(jnp.dot(attended, out_weight, precision=HIGHEST) + out_bias)
    second_in = low(normalize(middle, norm2_gain, norm2_bias))
    hidden_pre = low_back(jnp.dot(second_in, up_weight, precision=HIGHEST) + up_bias)
    activated = low(jax.nn.gelu(hidden_pre))
    return middle + low_back(jnp.dot(activated, down_weight, precision=HIGHEST) + down_bias)

def reference(tokens, cotangent, norm1_gain, norm1_bias, qkv_weight, qkv_bias, rotary_freqs, out_weight, out_bias, norm2_gain, norm2_bias, up_weight, up_bias, down_weight, down_bias, group_res, images):
    block_total = N_GROUP * N_DP
    res_rows = jnp.repeat(group_res, N_DP).astype(jnp.int32)
    side_rows = jnp.where(res_rows == 0, 14, jnp.where(res_rows == 1, 20, 24)).astype(jnp.int32)
    patch_rows = images * side_rows * side_rows
    res_totals = jnp.stack([jnp.sum(jnp.where(res_rows == res_index, patch_rows, 0)) for res_index in range(3)]).astype(jnp.float32)
    params = (norm1_gain, norm1_bias, qkv_weight, qkv_bias, rotary_freqs, out_weight, out_bias, norm2_gain, norm2_bias, up_weight, up_bias, down_weight, down_bias)
    params = tuple((weight_arg.astype(jnp.float32) for weight_arg in params))
    zero_grads = jax.tree.map(jnp.zeros_like, params)
    token_blocks = tokens.reshape(block_total, SLOTS, D)
    cot_blocks = cotangent.reshape(block_total, SLOTS, D)

    def block_step(running, inputs):
        token_block, cot_block, resolution, images_here = inputs
        row_pos, column_pos, live_mask, segment = layout_of(resolution, images_here, SLOTS)
        token_float = token_block.astype(jnp.float32)
        output_block, pull = jax.vjp(lambda values, weights: block_forward(values, weights, row_pos, column_pos, segment), token_float, params)
        upstream = cot_block.astype(jnp.float32) * live_mask[:, None].astype(jnp.float32)
        input_block, weight_grads = pull(upstream)
        block_scale = jnp.float32(SLOTS) / (3.0 * res_totals[resolution])
        running = jax.tree.map(lambda grad_total, grad_term: grad_total + block_scale * grad_term, running, weight_grads)
        return (running, (output_block.astype(jnp.bfloat16), input_block.astype(jnp.bfloat16)))
    grads, (outputs, input_grads) = lax.scan(block_step, zero_grads, (token_blocks, cot_blocks, res_rows, images))
    weight_list = grads[:4] + grads[5:]
    weight_sq = sum((jnp.sum(grad_term * grad_term) for grad_term in weight_list))
    rotary_sq = jnp.sum(grads[4] * grads[4])
    return (outputs.reshape(N_GROUP * N_DP * SLOTS, D), input_grads.reshape(N_GROUP * N_DP * SLOTS, D), grads[0], grads[1], grads[2], grads[3], grads[4], grads[5], grads[6], grads[7], grads[8], grads[9], grads[10], grads[11], grads[12], weight_sq, rotary_sq)
```

```python
import functools
import math

import jax
import jax.numpy as jnp
import numpy as np
from jax import lax
from jax.experimental import pallas as pl
from jax.experimental.pallas import tpu as pltpu
from jax.sharding import PartitionSpec as P

EPSILON = 1e-06
NEG_FILL = -1e30
SIDES = (14, 20, 24)
F32 = jnp.float32
BF16 = jnp.bfloat16
MIB = 1 << 20


def dot(left, right, left_dim, right_dim):
    return lax.dot_general(
        left, right, (((left_dim,), (right_dim,)), ((), ())), preferred_element_type=F32
    )


def smem():
    return pl.BlockSpec(memory_space=pltpu.SMEM)


def whole(shape):
    return pl.BlockSpec(shape, lambda *_: (0,) * len(shape), pipeline_mode=pl.Buffered(1))


def array(shape, kind=BF16):
    return jax.ShapeDtypeStruct(shape, kind)


class Line:
    def __init__(self):
        self.last = []

    def call(self, name, body, grid, ins, outs, scratch=(), scalars=None, deps=(), limit=60):
        lead = 0 if scalars is None else 1
        deps = list(deps) + self.last
        first_out = lead + len(ins) + len(deps)

        def kernel(*refs):
            body(*refs[: lead + len(ins)], *refs[first_out:])

        results = pl.pallas_call(
            kernel,
            name=name,
            grid_spec=pltpu.PrefetchScalarGridSpec(
                num_scalar_prefetch=lead,
                grid=grid,
                in_specs=[spec for _, spec in ins] + [anywhere()] * len(deps),
                out_specs=[spec for _, spec in outs],
                scratch_shapes=list(scratch),
            ),
            out_shape=[shape for shape, _ in outs],
            compiler_params=pltpu.CompilerParams(vmem_limit_bytes=limit * MIB),
            cost_estimate=pl.CostEstimate(flops=1 << 20, bytes_accessed=1 << 20, transcendentals=0),
        )(*([] if scalars is None else [scalars]), *[value for value, _ in ins], *deps)
        self.last = [results[0]]
        return results


def anywhere():
    return pl.BlockSpec(memory_space=pl.ANY)


def lanes_of(ref):
    return ref[...].astype(F32).reshape(1, -1)


def clip(value, low, high):
    return jnp.minimum(jnp.maximum(value, low), high)


def position_table(slots):
    table = np.zeros((3, slots, 128), np.float32)
    index = np.arange(slots)
    for res, side in enumerate(SIDES):
        within = index % (side * side)
        for lane in (0, 64):
            table[res, index, lane + within // side] = 1
            table[res, index, lane + 32 + within % side] = 1
    return table.astype(jnp.bfloat16)


def weight_lanes():
    table = np.zeros((128, 256), np.float32)
    for index in range(32):
        table[index, :128] = index
        table[32 + index, 128:] = index
    return table.astype(jnp.bfloat16)


def for_each_image(info, slots, body):
    for res, side in enumerate(SIDES):
        patches = side * side

        @pl.when(info[0] == res)
        def _(patches=patches):
            for image in range(slots // patches):
                offset = image * patches
                start = offset // 16 * 16
                span = -(-patches // 16) * 16
                body(image, start, span, offset - start, patches)


def inside(shape, axis, offset, patches):
    index = lax.broadcasted_iota(jnp.int32, shape, axis)
    return (index >= offset) & (index < offset + patches)


def live_rows(info):
    side = jnp.where(info[0] == 0, SIDES[0], jnp.where(info[0] == 1, SIDES[1], SIDES[2]))
    return info[1] * side * side


def swap_halves(values, half):
    pieces = []
    lane = lax.broadcasted_iota(jnp.int32, (values.shape[0], 128), 1)
    first = lane % (2 * half) < half
    for at in range(0, values.shape[1], 128):
        piece = values[:, at : at + 128]
        pieces.append(
            jnp.where(first, pltpu.roll(piece, 128 - half, 1), pltpu.roll(piece, half, 1))
        )
    return pieces[0] if len(pieces) == 1 else jnp.concatenate(pieces, axis=1)


def combine_angles(trig, width):
    cos_row, sin_row = trig[:, :width], trig[:, width : 2 * width]
    cos_col, sin_col = trig[:, 2 * width : 3 * width], trig[:, 3 * width :]
    return cos_row * cos_col - sin_row * sin_col, sin_row * cos_col + cos_row * sin_col


def for_each_image(info, slots, body):
    for res, side in enumerate(SIDES):
        patches = side * side

        @pl.when(info[0] == res)
        def _(patches=patches):
            for image in range(slots // patches):
                offset = image * patches
                start = offset // 16 * 16
                span = -(-patches // 16) * 16
                body(image, start, span, offset - start, patches)


def inside(shape, axis, offset, patches):
    index = lax.broadcasted_iota(jnp.int32, shape, axis)
    return (index >= offset) & (index < offset + patches)


def live_rows(info):
    side = jnp.where(info[0] == 0, SIDES[0], jnp.where(info[0] == 1, SIDES[1], SIDES[2]))
    return info[1] * side * side


def swap_halves(values, half):
    pieces = []
    lane = lax.broadcasted_iota(jnp.int32, (values.shape[0], 128), 1)
    first = lane % (2 * half) < half
    for at in range(0, values.shape[1], 128):
        piece = values[:, at : at + 128]
        pieces.append(
            jnp.where(first, pltpu.roll(piece, 128 - half, 1), pltpu.roll(piece, half, 1))
        )
    return pieces[0] if len(pieces) == 1 else jnp.concatenate(pieces, axis=1)


def combine_angles(trig, width):
    cos_row, sin_row = trig[:, :width], trig[:, width : 2 * width]
    cos_col, sin_col = trig[:, 2 * width : 3 * width], trig[:, 3 * width :]
    return cos_row * cos_col - sin_row * sin_col, sin_row * cos_col + cos_row * sin_col


def first_kernel(
    info, pos_ref, tok_ref, gain_ref, bias_ref, w_ref, wb_ref, freq_ref, qkv_ref, in_ref, tab_ref
):
    width = tok_ref.shape[1]

    @pl.when(pl.program_id(0) == 0)
    def _():
        index = lax.broadcasted_iota(jnp.int32, (32, width), 0).astype(F32)
        lane = lax.broadcasted_iota(jnp.int32, (32, width), 1)
        sign = jnp.where(lane % 64 < 32, -1.0, 1.0).astype(F32)
        tab_ref[...] = jnp.zeros_like(tab_ref)
        for kind in range(2):
            angle = index * freq_ref[kind : kind + 1, :]
            for part, value in enumerate((jnp.cos(angle), jnp.sin(angle) * sign)):
                high = value.astype(BF16)
                low = (value - high.astype(F32)).astype(BF16)
                at = (2 * kind + part) * width
                tab_ref[32 * kind : 32 * kind + 32, at : at + width] = high
                tab_ref[64 + 32 * kind : 96 + 32 * kind, at : at + width] = low

    values = tok_ref[...].astype(F32)
    shifted = values - jnp.mean(values, axis=1, keepdims=True)
    inverse = lax.rsqrt(jnp.mean(shifted * shifted, axis=1, keepdims=True) + EPSILON)
    first_in = (
        shifted * inverse * lanes_of(gain_ref) + lanes_of(bias_ref)
    ).astype(BF16)
    in_ref[...] = first_in
    cosine, sine = combine_angles(dot(pos_ref[...], tab_ref[...], 1, 0), width)
    for part in range(3):
        cols = slice(part * width, (part + 1) * width)
        projected = dot(first_in, w_ref[:, cols], 1, 0) + wb_ref[cols].astype(F32).reshape(1, -1)
        if part < 2:
            projected = projected * cosine + swap_halves(projected, 32) * sine
        if part == 0:
            projected = projected * 0.125
        qkv_ref[:, cols] = projected.astype(BF16)


ROWS = 384


def fill_angles(table, freq_ref, width):
    index = lax.broadcasted_iota(jnp.int32, (32, width), 0).astype(F32)
    lane = lax.broadcasted_iota(jnp.int32, (32, width), 1)
    sign = jnp.where(lane % 64 < 32, -1.0, 1.0).astype(F32)
    table[...] = jnp.zeros_like(table)
    for kind in range(2):
        angle = index * freq_ref[kind : kind + 1, :]
        for part, value in enumerate((jnp.cos(angle), jnp.sin(angle) * sign)):
            high = value.astype(BF16)
            low = (value - high.astype(F32)).astype(BF16)
            at = (2 * kind + part) * width
            table[32 * kind : 32 * kind + 32, at : at + width] = high
            table[64 + 32 * kind : 96 + 32 * kind, at : at + width] = low


def normed_rows(values):
    shifted = values - jnp.mean(values, axis=1, keepdims=True)
    inverse = lax.rsqrt(jnp.mean(shifted * shifted, axis=1, keepdims=True) + EPSILON)
    return shifted * inverse, inverse


def forward_kernel(
    scal, pos_ref, tok_ref, g1_ref, b1_ref, qb_ref, freq_ref, ob_ref, g2_ref, b2_ref, ub_ref,
    w_hbm, ow_hbm, uw_hbm, cot_hbm,
    send_ref, in_ref, stat_ref, tab_hbm, qkv_hbm, att_hbm, mid_hbm, sec_hbm, act_hbm, slope_hbm,
    w_s, ow_s, uw_s, cot_s, tab_s, qkv_s, att_s, mid_s, sec_s, act_s, slope_s, load_sem, store_sem,
):
    slots, width = att_s.shape
    hidden = act_s.shape[1]
    blocks, pairs = slots // ROWS, width // 128
    first_mid, first_send = blocks + pairs, 2 * blocks + pairs
    last = first_send + hidden // width - 1
    step = pl.program_id(0)
    half = cot_s.shape[1]

    def load(at):
        source, target = (
            [(w_hbm.at[:, part * width : (part + 1) * width], w_s.at[part]) for part in range(3)]
            + [(ow_hbm, ow_s), (uw_hbm, uw_s)]
            + [(cot_hbm.at[:, pl.ds(pl.multiple_of((1 - scal[2]) * half, half), half)], cot_s)]
        )[at]
        return pltpu.make_async_copy(source, target, load_sem.at[at])

    def store(kind, block):
        rows = pl.ds(pl.multiple_of(block * ROWS, ROWS), ROWS)
        if kind == 0:
            source, target = qkv_s.at[:, rows], qkv_hbm.at[:, rows]
        elif kind < 5:
            pair = ((mid_s, mid_hbm), (sec_s, sec_hbm), (act_s, act_hbm), (slope_s, slope_hbm))
            source, target = (ref.at[rows] for ref in pair[kind - 1])
        else:
            source, target = ((tab_s, tab_hbm), (att_s, att_hbm))[kind - 5]
        return pltpu.make_async_copy(source, target, store_sem.at[kind, block])

    @pl.when(step == 0)
    def _():
        for at in range(6):
            load(at).start()
        fill_angles(tab_s, freq_ref, width)
        store(5, 0).start()

    @pl.when(step < blocks)
    def _():
        normed, _ = normed_rows(tok_ref[...].astype(F32))
        first_in = (normed * lanes_of(g1_ref) + lanes_of(b1_ref)).astype(BF16)
        in_ref[...] = first_in
        cosine, sine = combine_angles(dot(pos_ref[...], tab_s[...], 1, 0), width)
        rows = pl.ds(pl.multiple_of(step * ROWS, ROWS), ROWS)
        for part in range(3):

            @pl.when(step == 0)
            def _():
                load(part).wait()

            bias = qb_ref[part * width : (part + 1) * width].astype(F32).reshape(1, -1)
            projected = dot(first_in, w_s[part], 1, 0) + bias
            if part < 2:
                projected = projected * cosine + swap_halves(projected, 32) * sine
            if part == 0:
                projected = projected * 0.125
            projected = projected.astype(BF16)
            for pair in range(pairs):
                qkv_s[part * pairs + pair, rows, :] = projected[:, pair * 128 : pair * 128 + 128]
        store(0, step).start()

    @pl.when((step >= blocks) & (step < first_mid))
    def _():
        pair = step - blocks
        cols = pl.ds(pl.multiple_of(pair * 128, 128), 128)
        q_ref, k_ref, v_ref = (qkv_s.at[part * pairs + pair] for part in range(3))
        att_s[:, cols] = v_ref[...]
        live = live_rows(scal)

        def image_step(image, start, span, offset, patches):
            rows = slice(start, start + span)
            exact = span == patches
            turned = v_ref[rows, :].T
            mixed = []
            for head in range(2):
                lanes = slice(head * 64, head * 64 + 64)
                scores = dot(k_ref[rows, lanes], q_ref[rows, lanes], 1, 1)
                if not exact:
                    scores = jnp.where(inside(scores.shape, 0, offset, patches), scores, NEG_FILL)
                top = jnp.max(scores, axis=0, keepdims=True)
                powers = jnp.exp(scores - top)
                mass = jnp.sum(powers, axis=0, keepdims=True)
                mixed.append(dot(turned[lanes], powers.astype(BF16), 1, 0) * (1.0 / mass))
                stat_ref[image, head : head + 1, 0:span] = top + jnp.log(mass)
            result = jnp.concatenate(mixed, axis=0).T
            keep = lax.broadcasted_iota(jnp.int32, result.shape, 0) < live - start
            if not exact:
                keep = keep & inside(result.shape, 0, offset, patches)
            result = jnp.where(keep, result, att_s[rows, cols].astype(F32))
            att_s[rows, cols] = result.astype(BF16)

        for_each_image(scal, slots, image_step)

    @pl.when((step >= first_mid) & (step < first_send))
    def _():
        @pl.when(step == first_mid)
        def _():
            store(6, 0).start()
            load(3).wait()
            load(4).wait()

        block = step - first_mid
        rows = pl.ds(pl.multiple_of(block * ROWS, ROWS), ROWS)
        middle = tok_ref[...].astype(F32) + (dot(att_s[rows, :], ow_s[...], 1, 0) + lanes_of(ob_ref))
        mid_s[rows, :] = middle
        normed, _ = normed_rows(middle)
        second_in = (normed * lanes_of(g2_ref) + lanes_of(b2_ref)).astype(BF16)
        sec_s[rows, :] = second_in
        scale = math.sqrt(2.0 / math.pi)
        for at in range(0, hidden, 768):
            cols = slice(at, at + 768)
            pre = dot(second_in, uw_s[:, cols], 1, 0) + ub_ref[cols].astype(F32).reshape(1, -1)
            square = pre * pre
            bent = jnp.tanh(pre * (scale + (scale * 0.044715) * square))
            gate = 0.5 + 0.5 * bent
            act_s[rows, cols] = (pre * gate).astype(BF16)
            lean = pre * (scale + (3.0 * scale * 0.044715) * square)
            slope_s[rows, cols] = (gate * (1.0 + (1.0 - bent) * lean)).astype(BF16)
        for kind in range(1, 5):
            store(kind, block).start()

    @pl.when(step >= first_send)
    def _():
        @pl.when(step == first_send)
        def _():
            load(5).wait()
            cot_s[...] = live_cotangent(scal, cot_s, 0).astype(BF16)

        tile = pl.ds(pl.multiple_of((step - first_send) * width, width), width)
        send_ref[...] = dot(act_s[:, tile], cot_s[...], 0, 0)

    @pl.when(step == last)
    def _():
        for kind in range(5):
            for block in range(blocks):
                store(kind, block).wait()
        store(5, 0).wait()
        store(6, 0).wait()


def live_cotangent(info, cot_ref, first_row):
    row = lax.broadcasted_iota(jnp.int32, cot_ref.shape, 0) + first_row
    return jnp.where(row < live_rows(info), cot_ref[...].astype(F32), 0.0)


def hidden_kernel(
    scal, cot_ref, slope_ref, dw_hbm, sec_hbm, send_ref, sums_ref, upsum_ref, hid_hbm,
    dw_s, sec_s, hid_s, load_sem, store_sem,
):
    slots, width = sec_s.shape
    hidden = hid_s.shape[1]
    blocks, pieces = slots // ROWS, hidden // width
    step = pl.program_id(0)
    last = blocks + hidden // 2 // width - 1

    def load(at):
        if at == pieces:
            return pltpu.make_async_copy(sec_hbm, sec_s, load_sem.at[at])
        rows = slice(at * width, (at + 1) * width)
        return pltpu.make_async_copy(dw_hbm.at[rows], dw_s.at[rows], load_sem.at[at])

    def store(block):
        rows = pl.ds(pl.multiple_of(block * ROWS, ROWS), ROWS)
        return pltpu.make_async_copy(hid_s.at[rows], hid_hbm.at[rows], store_sem.at[block])

    @pl.when(step == 0)
    def _():
        for at in range(pieces + 1):
            load(at).start()
        sums_ref[...] = jnp.zeros_like(sums_ref)
        upsum_ref[...] = jnp.zeros_like(upsum_ref)

    @pl.when(step < blocks)
    def _():
        upstream = live_cotangent(scal, cot_ref, step * ROWS)
        up_low = upstream.astype(BF16)
        rows = pl.ds(pl.multiple_of(step * ROWS, ROWS), ROWS)
        for at in range(pieces):

            @pl.when(step == 0)
            def _():
                load(at).wait()

            cols = slice(at * width, (at + 1) * width)
            act_grad = dot(up_low, dw_s[cols, :], 1, 1)
            hidden_low = (slope_ref[:, cols].astype(F32) * act_grad).astype(BF16)
            hid_s[rows, cols] = hidden_low
            upsum_ref[0:1, cols] += jnp.sum(hidden_low.astype(F32), axis=0, keepdims=True)
        sums_ref[0:1, :] += jnp.sum(upstream, axis=0, keepdims=True)
        store(step).start()

    @pl.when(step >= blocks)
    def _():
        @pl.when(step == blocks)
        def _():
            load(pieces).wait()

        tile = (1 - scal[2]) * (hidden // 2) + (step - blocks) * width
        send_ref[...] = dot(sec_s[...], hid_s[:, pl.ds(pl.multiple_of(tile, width), width)], 0, 0)

    @pl.when(step == last)
    def _():
        for block in range(blocks):
            store(block).wait()


def write_pieces(term, scal, shard, one, two):
    count = term.shape[0] // shard
    if one is not None:
        for at in range(count):
            for ref, bit in ((one[0], 1 - scal[3]), (one[1], scal[3])):
                rows = pl.ds(pl.multiple_of(at * shard + bit * (shard // 2), 8), shard // 2)
                ref[at] = term[rows, one[2]]
    if two is not None:
        for at in range(count // 2):
            for ref, bit in ((two[0], 1 - scal[4]), (two[1], scal[4])):
                rows = pl.ds(pl.multiple_of((2 * at + bit) * shard, 8), shard)
                ref[at] = term[rows, two[2]]


def back_kernel(
    shard, scal, scale_ref, cot_ref, hid_ref, mid_ref, gain_ref, col_ref, got_ref, uw_hbm, ow_hbm, sec_hbm,
    branch_ref, att_ref, grad_ref, sums_ref, *rest,
):
    outs, (uw_s, ow_s, sec_s, term_s, load_sem) = rest[:-5], rest[-5:]
    slots, width = sec_s.shape
    blocks, pieces = slots // ROWS, uw_s.shape[0]
    step = pl.program_id(0)

    def load(at):
        if at < pieces:
            source, target = uw_hbm.at[:, at * width : (at + 1) * width], uw_s.at[at]
        else:
            source, target = ((ow_hbm, ow_s), (sec_hbm, sec_s))[at - pieces]
        return pltpu.make_async_copy(source, target, load_sem.at[at])

    @pl.when(step == 0)
    def _():
        for at in range(pieces + 2):
            load(at).start()
        sums_ref[...] = jnp.zeros_like(sums_ref)

    @pl.when(step < blocks)
    def _():
        upstream = live_cotangent(scal, cot_ref, step * ROWS)
        back = None
        for at in range(pieces):

            @pl.when(step == 0)
            def _():
                load(at).wait()

            term = dot(hid_ref[:, at * width : (at + 1) * width], uw_s[at], 1, 1)
            back = term if back is None else back + term
        normed, inverse = normed_rows(mid_ref[...])
        scaled = back * lanes_of(gain_ref)
        inner = (
            scaled
            - jnp.mean(scaled, axis=1, keepdims=True)
            - normed * jnp.mean(scaled * normed, axis=1, keepdims=True)
        )
        middle_grad = upstream + inverse * inner
        grad_ref[...] = middle_grad
        branch = middle_grad.astype(BF16)
        branch_ref[...] = branch

        @pl.when(step == 0)
        def _():
            load(pieces).wait()

        att_ref[...] = dot(branch, ow_s[...], 1, 1).astype(BF16)
        sums_ref[0:1, :] += jnp.sum(back * normed, axis=0, keepdims=True)
        sums_ref[1:2, :] += jnp.sum(back, axis=0, keepdims=True)
        sums_ref[2:3, :] += jnp.sum(branch.astype(F32), axis=0, keepdims=True)

    @pl.when(step >= blocks)
    def _():
        @pl.when(step == blocks)
        def _():
            load(pieces + 1).wait()

        term = dot(sec_s[...], col_ref[...], 0, 0) * scale_ref[0] + got_ref[...] * scale_ref[1]
        if len(outs) == 1:
            outs[0][...] = term
        else:
            term_s[...] = term

            @pl.when(step < blocks + 2)
            def _():
                write_pieces(term_s, scal, shard, (outs[0], outs[1], slice(None)), None)

            @pl.when(step == blocks + 2)
            def _():
                write_pieces(term_s, scal, shard, None, (outs[2], outs[3], slice(None)))


def attend_back_kernel(
    info, pos_ref, t0, t1, t2, t3, lanes_ref, q_ref, k_ref, v_ref, up_ref, stat_ref,
    gq_ref, gk_ref, gv_ref, sums_ref, dq_acc, dk_acc, dv_acc,
):
    @pl.when(info[0] < 2)
    def _():
        for acc in (dq_acc, dk_acc, dv_acc):
            acc[...] = jnp.zeros_like(acc)

    def image_step(image, start, span, offset, patches):
        rows = slice(start, start + span)
        exact = span == patches
        for head in range(2):
            lanes = slice(head * 64, head * 64 + 64)
            query, key = q_ref[rows, lanes], k_ref[rows, lanes]
            value, upstream = v_ref[rows, lanes], up_ref[rows, lanes]
            probs = jnp.exp(dot(key, query, 1, 1) - stat_ref[image, head : head + 1, 0:span])
            if not exact:
                keep = inside(probs.shape, 0, offset, patches)
                keep = keep & inside(probs.shape, 1, offset, patches)
                probs = jnp.where(keep, probs, 0.0)
            prob_grad = dot(value, upstream, 1, 1)
            inner = jnp.sum(probs * prob_grad, axis=0, keepdims=True)
            score_low = (probs * (prob_grad - inner)).astype(BF16)
            value_grad = dot(probs.astype(BF16), upstream, 1, 0)
            key_grad = dot(score_low, query, 1, 0)
            query_grad = dot(key.T, score_low, 1, 0).T
            if exact:
                dq_acc[rows, lanes] = query_grad
                dk_acc[rows, lanes] = key_grad
                dv_acc[rows, lanes] = value_grad
            else:
                dq_acc[rows, lanes] += query_grad
                dk_acc[rows, lanes] += key_grad
                dv_acc[rows, lanes] += value_grad

    for_each_image(info, q_ref.shape[0], image_step)
    pos = pos_ref[...]
    table = jnp.concatenate([t0[...], t1[...], t2[...], t3[...]], axis=1)
    cosine, sine = combine_angles(dot(pos, table, 1, 0), 128)
    places = dot(pos, lanes_ref[...], 1, 0)
    lane = lax.broadcasted_iota(jnp.int32, (1, 128), 1)
    sign = jnp.where(lane % 64 < 32, 1.0, -1.0)
    angle_grad = None
    sums_ref[...] = jnp.zeros_like(sums_ref)
    for row, (acc, low_ref, out_ref, up, down) in enumerate(
        ((dq_acc, q_ref, gq_ref, 0.125, 8.0), (dk_acc, k_ref, gk_ref, 1.0, 1.0))
    ):
        grad = acc[...] * up
        swapped = swap_halves(grad, 32)
        term = swapped * (low_ref[...].astype(F32) * down)
        angle_grad = term if angle_grad is None else angle_grad + term
        pre = (grad * cosine - swapped * sine).astype(BF16)
        out_ref[...] = pre
        sums_ref[2 + row : 3 + row, :] = jnp.sum(pre.astype(F32), axis=0, keepdims=True)
    value_low = dv_acc[...].astype(BF16)
    gv_ref[...] = value_low
    sums_ref[4:5, :] = jnp.sum(value_low.astype(F32), axis=0, keepdims=True)
    for row in range(2):
        place = places[:, row * 128 : row * 128 + 128]
        sums_ref[row : row + 1, :] = sign * jnp.sum(place * angle_grad, axis=0, keepdims=True)


def input_kernel(starts, tok_ref, gain_ref, grad_ref, w_ref, *refs):
    pieces = refs[: len(starts)]
    out_ref, sums_ref = refs[len(starts) :]

    @pl.when(pl.program_id(0) == 0)
    def _():
        sums_ref[...] = jnp.zeros_like(sums_ref)

    back = None
    for piece, start in zip(pieces, starts):
        term = dot(piece[...], w_ref[:, start : start + piece.shape[1]], 1, 1)
        back = term if back is None else back + term
    values = tok_ref[...].astype(F32)
    shifted = values - jnp.mean(values, axis=1, keepdims=True)
    inverse = lax.rsqrt(jnp.mean(shifted * shifted, axis=1, keepdims=True) + EPSILON)
    normed = shifted * inverse
    scaled = back * lanes_of(gain_ref)
    inner = (
        scaled
        - jnp.mean(scaled, axis=1, keepdims=True)
        - normed * jnp.mean(scaled * normed, axis=1, keepdims=True)
    )
    out_ref[...] = (grad_ref[...] + inverse * inner).astype(BF16)
    sums_ref[0:1, :] += jnp.sum(back * normed, axis=0, keepdims=True)
    sums_ref[1:2, :] += jnp.sum(back, axis=0, keepdims=True)


def output_kernel(act_ref, dw_ref, db_ref, mid_ref, out_ref):
    out_ref[...] = (
        mid_ref[...] + (dot(act_ref[...], dw_ref[...], 1, 0) + lanes_of(db_ref))
    ).astype(BF16)


def weight_grad(line, name, groups, scal, own, scales=None, extra=None, shard=0, mask=False, tile=768):
    slots, height = groups[0][0].shape
    tile = min(tile, height)
    plan = [(len(rights), width) for _, rights, width in groups]
    total = sum(count * width for count, width in plan)
    one_cols = total // 3 * 2
    pieces = extra is not None and shard % 16 == 0

    def kernel(scal_ref, *refs):
        rest = list(refs)
        if extra is not None:
            scale_ref, extra_ref = rest.pop(0), rest.pop(0)
        lefts_rights = [(rest.pop(0), [rest.pop(0) for _ in range(count)]) for count, _ in plan]
        target = rest[-1] if pieces else rest[0]
        at = 0
        for (left_ref, right_refs), (count, width) in zip(lefts_rights, plan):
            for right_ref in right_refs:
                right = right_ref[...]
                if mask:
                    right = live_cotangent(scal_ref, right_ref, 0).astype(BF16)
                cols = slice(at, at + width)
                term = dot(left_ref[...], right, 0, 0)
                if extra is not None:
                    term = term * scale_ref[0] + extra_ref[:, cols] * scale_ref[1]
                target[:, cols] = term
                at += width
        if pieces:
            write_pieces(
                target, scal_ref, shard,
                (rest[0], rest[1], slice(0, one_cols)), (rest[2], rest[3], slice(one_cols, total)),
            )

    ins = []
    if extra is not None:
        ins += [(scales, smem()), (extra, pl.BlockSpec((tile, total), lambda i, scal: (i, 0)))]
    for left, rights, width in groups:
        ins.append((left, pl.BlockSpec((slots, tile), lambda i, scal: (0, i))))
        for right in rights:
            ins.append((right, pl.BlockSpec(
                (slots, width), lambda i, scal: (0, scal[2] if own else 1 - scal[2]),
                pipeline_mode=pl.Buffered(1),
            )))
    if not pieces:
        outs = [(array((height, total), F32), pl.BlockSpec((tile, total), lambda i, scal: (i, 0)))]
        return line.call(name, kernel, (height // tile,), ins, outs, scalars=scal)[0]
    count = height // shard
    outs = [
        (array((count, shard // 2, one_cols), F32),
         pl.BlockSpec((tile // shard, shard // 2, one_cols), lambda i, scal: (i, 0, 0)))
    ] * 2 + [
        (array((count // 2, shard, total - one_cols), F32),
         pl.BlockSpec((tile // shard // 2, shard, total - one_cols), lambda i, scal: (i, 0, 0)))
    ] * 2
    return line.call(
        name, kernel, (height // tile,), ins, outs, [pltpu.VMEM((tile, total), F32)], scalars=scal
    )


class Place:
    def __init__(self, n_group, n_dp):
        self.n_group, self.n_dp = n_group, n_dp
        group_at, self.dp_at = lax.axis_index("group"), lax.axis_index("dp")
        self.core, self.x = lax.rem(group_at, 2), lax.div(group_at, 2)
        self.dp_bits = n_dp.bit_length() - 1
        self.dp = [lax.rem(lax.div(self.dp_at, 1 << bit), 2) for bit in range(self.dp_bits)]

    def group(self, value, mask):
        return lax.ppermute(value, "group", [(at, at ^ mask) for at in range(self.n_group)])

    def along(self, value, mask):
        return lax.ppermute(value, "dp", [(at, at ^ mask) for at in range(self.n_dp)])

    def small_stages(self):
        yield lambda v: v + (self.group(v, 1) + (self.group(v, 2) + self.group(v, 3)))
        for bit in range(0, self.dp_bits, 2):
            one = 1 << bit
            if bit + 1 < self.dp_bits:
                yield lambda v, one=one: v + (
                    self.along(v, one) + (self.along(v, 2 * one) + self.along(v, 3 * one))
                )
            else:
                yield lambda v, one=one: v + self.along(v, one)


def sum_of(terms):
    result = terms[0]
    for term in terms[1:]:
        result = result + term
    return result


class Chunk:
    def __init__(self, place, kept, rows, cols):
        self.place = place
        shard = rows // place.n_dp
        self.rows, self.fold, one_cols = shard, 1, cols // 3 * 2
        if not isinstance(kept, (list, tuple)):
            while shard * self.fold % 16:
                self.fold *= 2
            tall = shard * self.fold
            view = kept.reshape(place.n_dp, shard, cols)
            one = view[..., :one_cols].reshape(place.n_dp, 2, tall // 2, one_cols // self.fold)
            two = view[..., one_cols:].reshape(place.n_dp // 2, 2, tall, (cols - one_cols) // self.fold)
            kept = [
                lax.dynamic_index_in_dim(value, at, 1, keepdims=False)
                for value, bit in ((one, place.x), (two, place.dp[0])) for at in (1 - bit, bit)
            ]
        one_sent, self.one, two_sent, self.two = kept
        self.count, self.half, self.one_cols = one_sent.shape
        self.two_cols = two_sent.shape[2]
        self.got_one = place.group(one_sent, 2)
        self.got_two = place.along(two_sent, 1)
        self.stage = 0

    def job(self):
        place, stage = self.place, self.stage
        self.stage += 1
        half, one_cols, two_cols = self.half, self.one_cols, self.two_cols
        cols = one_cols + 2 * two_cols
        if stage == 0:
            lead = self.count // 2
            ins = [
                (value.reshape(lead, 2, half, one_cols), pl.BlockSpec(
                    (lead, None, half, one_cols), lambda i, scal: (0, 1 - scal[4], 0, 0)))
                for value in (self.one, self.got_one)
            ]

            def body(scal, ins, outs):
                outs[0][...] = ins[0][...] + ins[1][...]

            def then(sent):
                self.got = place.along(sent, 1)

            return ins, [(lead, half, one_cols)], body, then
        if stage < place.dp_bits:
            bit = 4 + stage
            if stage == 1:
                lead = self.count // 4
                ins = [
                    (value.reshape(lead, 2, 2, half, one_cols), pl.BlockSpec(
                        (lead, 2, None, half, one_cols), lambda i, scal: (0, 0, scal[4], 0, 0)))
                    for value in (self.one, self.got_one)
                ]
                ins.append((self.got.reshape(lead, 2, half, one_cols), None))
                ins += [
                    (value.reshape(lead, 2, 2 * half, two_cols), None)
                    for value in (self.two, self.got_two)
                ]

                def body(scal, ins, outs):
                    for out, at in ((outs[0], 1 - scal[bit]), (outs[1], scal[bit])):
                        out[:, :, :one_cols] = ins[0][:, at] + ins[1][:, at] + ins[2][:, at]
                        for part in range(2):
                            rows = slice(part * half, part * half + half)
                            lanes = slice(one_cols + part * two_cols, one_cols + (part + 1) * two_cols)
                            out[:, :, lanes] = ins[3][:, at, rows] + ins[4][:, at, rows]
            else:
                lead = self.both.shape[0] // 2
                ins = [(value.reshape(lead, 2, half, cols), None) for value in (self.both, self.got)]

                def body(scal, ins, outs):
                    for out, at in ((outs[0], 1 - scal[bit]), (outs[1], scal[bit])):
                        out[...] = ins[0][:, at] + ins[1][:, at]

            def then(sent, kept):
                self.both = kept
                self.got = place.along(sent, 1 << stage)

            return ins, [(lead, half, cols)] * 2, body, then
        if stage == place.dp_bits:
            ins = [(self.both.reshape(half, cols), None), (self.got.reshape(half, cols), None)]

            def body(scal, ins, outs):
                outs[0][...] = ins[0][...] + ins[1][...]

            def then(own):
                self.own, self.got = own, place.group(own, 2)

            return ins, [(half, cols)], body, then
        ins = [(self.own, None), (self.got, None)]

        def body(scal, ins, outs):
            own, got = ins
            out, square = outs
            here = pl.ds(pl.multiple_of(scal[3] * half, 8), half)
            there = pl.ds(pl.multiple_of((1 - scal[3]) * half, 8), half)
            out[here, :one_cols] = own[:, :one_cols]
            out[there, :one_cols] = got[:, :one_cols]
            for part in range(2):
                lanes = slice(one_cols + part * two_cols, one_cols + (part + 1) * two_cols)
                out[part * half : part * half + half, one_cols:] = own[:, lanes] + got[:, lanes]
            square[...] = jnp.broadcast_to(jnp.sum(out[...] * out[...]), square.shape)

        def then(mine, square):
            self.mine, self.square = mine, square
            self.theirs = place.group(mine, 1)

        return ins, [(2 * half, one_cols + two_cols), (8, 128)], body, then

    def blocks(self):
        found = []
        for value in (
            jnp.where(self.place.core == 0, self.mine, self.theirs),
            jnp.where(self.place.core == 0, self.theirs, self.mine),
        ):
            one = value[:, : self.one_cols].reshape(self.rows, -1)
            two = value[:, self.one_cols :].reshape(self.rows, -1)
            found.append((one, two))
        return found


def run_jobs(line, name, scal, jobs):
    ins = [
        (value, spec if spec is not None else whole(value.shape))
        for job in jobs for value, spec in job[0]
    ]
    outs = [
        (array(shape, F32), pl.BlockSpec(shape, functools.partial(lambda rank, *_: (0,) * rank, len(shape))))
        for job in jobs for shape in job[1]
    ]

    def kernel(scal_ref, *refs):
        at_in, at_out = 0, len(ins)
        for job_ins, job_outs, body, _ in jobs:
            body(
                scal_ref, refs[at_in : at_in + len(job_ins)], refs[at_out : at_out + len(job_outs)]
            )
            at_in += len(job_ins)
            at_out += len(job_outs)

    results = line.call(name, kernel, (1,), ins, outs, scalars=scal)
    at = 0
    for _, job_outs, _, then in jobs:
        then(*results[at : at + len(job_outs)])
        at += len(job_outs)


def local(
    n_group, n_dp, tokens, cotangent, norm1_gain, norm1_bias, qkv_weight, qkv_bias, rotary_freqs,
    out_weight, out_bias, norm2_gain, norm2_bias, up_weight, up_bias, down_weight, down_bias,
    group_res, images,
):
    slots, width = tokens.shape
    heads = rotary_freqs.shape[1]
    hidden = up_weight.shape[1]
    pairs = heads // 2
    blocks = slots // ROWS
    place = Place(n_group, n_dp)
    line = Line()
    scal = jnp.concatenate(
        [group_res, images, jnp.stack([place.core, place.x] + place.dp).astype(jnp.int32)]
    ).astype(jnp.int32)

    def rows_of(cols, first=0):
        return pl.BlockSpec((ROWS, cols), lambda i, *_: (clip(i - first, 0, blocks - 1), 0))

    def param(vector):
        return (vector, whole(vector.shape))

    def kept_sum(rows, cols):
        return (array((rows, cols), F32), pl.BlockSpec((rows, cols), lambda *_: (0, 0)))

    def in_hbm(shape, kind=BF16):
        return (array(shape, kind), anywhere())

    side = jnp.where(group_res[0] == 0, SIDES[0], jnp.where(group_res[0] == 1, SIDES[1], SIDES[2]))
    lane = lax.broadcasted_iota(jnp.int32, (2304 // n_dp, 128), 1)
    patches = (images[0] * side * side).astype(F32)
    here = jnp.where(lane == group_res[0], patches, 0.0)
    gathered = lax.all_gather(here, "dp")

    half_freqs = jnp.concatenate([rotary_freqs, rotary_freqs], axis=-1).reshape(2, width)
    pos = jnp.asarray(position_table(slots))
    stat_shape = (slots // SIDES[0] ** 2, 8, -(-(SIDES[2] ** 2) // 128) * 128)
    first_mid, first_send = blocks + pairs, 2 * blocks + pairs
    tiles = hidden // width
    down_sent, first_in, stats, trig_table, qkv, attended, middle, second_in, act, slope = line.call(
        "forward", forward_kernel, (first_send + tiles,),
        [
            (pos, pl.BlockSpec(
                (None, ROWS, 128), lambda i, scal: (scal[0], clip(i, 0, blocks - 1), 0))),
            (tokens, pl.BlockSpec((ROWS, width), lambda i, scal: (
                jnp.where(i < blocks, i, clip(i - first_mid, 0, blocks - 1)), 0))),
            param(norm1_gain), param(norm1_bias), param(qkv_bias), param(half_freqs), param(out_bias),
            param(norm2_gain), param(norm2_bias), param(up_bias),
            (qkv_weight, anywhere()), (out_weight, anywhere()), (up_weight, anywhere()),
            (cotangent, anywhere()),
        ],
        [
            (array((hidden, width // 2), F32), pl.BlockSpec(
                (width, width // 2), lambda i, scal: (clip(i - first_send, 0, tiles - 1), 0))),
            (array((slots, width)), rows_of(width)),
            (array((pairs,) + stat_shape, F32), pl.BlockSpec(
                (None,) + stat_shape, lambda i, scal: (clip(i - blocks, 0, pairs - 1), 0, 0, 0))),
            in_hbm((128, 4 * width)), in_hbm((3 * pairs, slots, 128)), in_hbm((slots, width)),
            in_hbm((slots, width), F32), in_hbm((slots, width)), in_hbm((slots, hidden)),
            in_hbm((slots, hidden)),
        ],
        [
            pltpu.VMEM((3, width, width), BF16), pltpu.VMEM((width, width), BF16),
            pltpu.VMEM((width, hidden), BF16), pltpu.VMEM((slots, width // 2), BF16),
            pltpu.VMEM((128, 4 * width), BF16), pltpu.VMEM((3 * pairs, slots, 128), BF16),
            pltpu.VMEM((slots, width), BF16), pltpu.VMEM((slots, width), F32),
            pltpu.VMEM((slots, width), BF16), pltpu.VMEM((slots, hidden), BF16),
            pltpu.VMEM((slots, hidden), BF16),
            pltpu.SemaphoreType.DMA((6,)), pltpu.SemaphoreType.DMA((7, blocks)),
        ],
        scalars=scal, limit=62,
    )
    down_got = place.group(down_sent, 1)
    totals = jnp.sum(gathered[:, :8], axis=0)
    others = [place.group(totals, mask) for mask in (1, 2, 3)]

    up_sent, down_sums, up_sums, hidden_low = line.call(
        "hidden_grad", hidden_kernel, (blocks + tiles // 2,),
        [
            (cotangent, rows_of(width)), (slope, rows_of(hidden)), (down_weight, anywhere()),
            (second_in, anywhere()),
        ],
        [
            (array((width, hidden // 2), F32), pl.BlockSpec(
                (width, width), lambda i, scal: (0, clip(i - blocks, 0, tiles // 2 - 1)))),
            kept_sum(8, width), kept_sum(8, hidden), in_hbm((slots, hidden)),
        ],
        [
            pltpu.VMEM((hidden, width), BF16), pltpu.VMEM((slots, width), BF16),
            pltpu.VMEM((slots, hidden), BF16), pltpu.SemaphoreType.DMA((tiles + 1,)),
            pltpu.SemaphoreType.DMA((blocks,)),
        ],
        scalars=scal, deps=[totals],
    )
    up_got = place.group(up_sent, 1)
    all_totals = (totals + sum_of(others))[0]
    scales = F32(slots) / (
        3.0 * jnp.stack([
            jnp.sum(jnp.where(counted[0] > 0, all_totals, 0.0)) for counted in (totals, others[0])
        ])
    )

    down_groups = [(act, [cotangent], width // 2)]
    kept = weight_grad(
        line, "down_keep", down_groups, scal, True, scales, down_got, hidden // n_dp, mask=True
    )
    down = Chunk(place, kept, hidden, width // 2)

    shard = width // n_dp
    third = hidden // 6
    if shard % 16 == 0:
        piece_outs = [
            (array((n_dp, shard // 2, 2 * third), F32), pl.BlockSpec(
                (n_dp, shard // 2, third), lambda i, scal: (0, 0, clip(i - blocks, 0, 1))))
        ] * 2 + [
            (array((n_dp // 2, shard, third), F32), pl.BlockSpec(
                (n_dp // 2, shard, third), lambda i, scal: (0, 0, 0)))
        ] * 2
    else:
        piece_outs = [(array((width, 3 * third), F32), pl.BlockSpec(
            (width, third), lambda i, scal: (0, clip(i - blocks, 0, 2))))]
    branch, att_grad, mid_grad, norm_sums, *kept = line.call(
        "back", functools.partial(back_kernel, shard), (blocks + 3,),
        [
            (scales, smem()), (cotangent, rows_of(width)), (hidden_low, rows_of(hidden)),
            (middle, rows_of(width)), param(norm2_gain),
            (hidden_low, pl.BlockSpec(
                (slots, third), lambda i, scal: (0, 3 * scal[2] + clip(i - blocks, 0, 2)))),
            (up_got, pl.BlockSpec((width, third), lambda i, scal: (0, clip(i - blocks, 0, 2)))),
            (up_weight, anywhere()), (out_weight, anywhere()), (second_in, anywhere()),
        ],
        [
            (array((slots, width)), rows_of(width)), (array((slots, width)), rows_of(width)),
            (array((slots, width), F32), rows_of(width)), kept_sum(8, width),
        ] + piece_outs,
        [
            pltpu.VMEM((tiles, width, width), BF16), pltpu.VMEM((width, width), BF16),
            pltpu.VMEM((slots, width), BF16), pltpu.VMEM((width, third), F32),
            pltpu.SemaphoreType.DMA((tiles + 2,)),
        ],
        scalars=scal, deps=[down.one],
    )
    up = Chunk(place, kept if len(kept) > 1 else kept[0], width, hidden // 2)

    lanes_table = jnp.asarray(weight_lanes())

    def attend_back(first, count):
        def head_block(part):
            return pl.BlockSpec((128, 128), lambda i, scal: (0, part * pairs + first + i))

        def qkv_block(part):
            return pl.BlockSpec((None, slots, 128), lambda i, scal: (part * pairs + first + i, 0, 0))

        out = (array((slots, count * 128)), pl.BlockSpec((slots, 128), lambda i, scal: (0, i)))
        return line.call(
            "attend_back", attend_back_kernel, (count,),
            [(pos, pl.BlockSpec((None, slots, 128), lambda i, scal: (scal[0], 0, 0)))]
            + [(trig_table, head_block(part)) for part in range(4)]
            + [param(lanes_table)]
            + [(qkv, qkv_block(part)) for part in range(3)]
            + [
                (att_grad, pl.BlockSpec((slots, 128), lambda i, scal: (0, first + i))),
                (stats, pl.BlockSpec((None,) + stat_shape, lambda i, scal: (first + i, 0, 0, 0))),
            ],
            [out] * 3
            + [(array((count, 8, 128), F32), pl.BlockSpec((None, 8, 128), lambda i, scal: (i, 0, 0)))],
            scratch=[pltpu.VMEM((slots, 128), F32)] * 3,
            scalars=scal,
        )

    def jobs(name, *chunks):
        run_jobs(line, name, scal, [chunk.job() for chunk in chunks])

    last = pairs // 3
    first = pairs - last
    part_one = attend_back(0, first)
    jobs("d0", down)
    qo_groups = [(first_in, part_one[:3], first * 64), (attended, [branch], width // 2)]
    qo_sent = weight_grad(line, "qo_send", qo_groups, scal, False)
    qo_got = place.group(qo_sent, 1)
    part_two = attend_back(first, last)
    jobs("u0", up)
    jobs("d1", down)
    kept = weight_grad(line, "qo_keep", qo_groups, scal, True, scales, qo_got, shard)
    qo = Chunk(place, kept, width, first * 192 + width // 2)
    q2_groups = [(first_in, part_two[:3], last * 64)]
    q2_sent = weight_grad(line, "q2_send", q2_groups, scal, False)
    q2_got = place.group(q2_sent, 1)
    jobs("d2", down)

    pieces, starts = [], []
    for at, parts in ((0, part_one), (first, part_two)):
        for part in range(3):
            pieces.append(parts[part])
            starts.append(part * width + at * 128)
    input_grad, sums_one = line.call(
        "input_grad", functools.partial(input_kernel, starts), (blocks,),
        [
            (tokens, rows_of(width)), param(norm1_gain), (mid_grad, rows_of(width)),
            param(qkv_weight),
        ] + [(piece, rows_of(piece.shape[1])) for piece in pieces],
        [(array((slots, width)), rows_of(width)), kept_sum(8, width)],
    )
    kept = weight_grad(line, "q2_keep", q2_groups, scal, True, scales, q2_got, shard)
    q2 = Chunk(place, kept, width, last * 192)
    jobs("u1_q0", up, qo)

    pair_all = jnp.concatenate([part_one[3], part_two[3]])
    small = jnp.concatenate(
        [
            down_sums[0],
            norm_sums[:3].reshape(-1),
            up_sums[0],
            sums_one[:2].reshape(-1),
            pair_all[:, :5].transpose(1, 0, 2).reshape(-1),
        ]
    )
    small = (small * scales[0]).reshape(-1, 128)

    (output,) = line.call(
        "output", output_kernel, (blocks,),
        [(act, rows_of(hidden)), param(down_weight), param(down_bias), (middle, rows_of(width))],
        [(array((slots, width)), rows_of(width))],
        deps=[small],
    )

    chunks = (down, up, qo, q2)
    stages = list(place.small_stages())
    tail = [q2, down, up, qo, q2, up, down, qo, q2, up, qo, q2, up, qo, q2, qo, q2]
    for at, chunk in enumerate(tail):
        if chunk.stage < place.dp_bits + 2:
            jobs(f"tail{at}", chunk)
        if at in (1, 3, 5) and stages:
            small = stages.pop(0)(small)
    for chunk in chunks:
        while chunk.stage < place.dp_bits + 2:
            jobs("rest", chunk)
    for stage in stages:
        small = stage(small)

    small = small.reshape(-1)
    at = 0

    def take(size):
        nonlocal at
        at += size
        return small[at - size : at]

    down_bias_all, gain_two_all, bias_two_all, out_bias_all = (take(width) for _ in range(4))
    up_bias_all = take(hidden)
    gain_one_all, bias_one_all = take(width), take(width)
    rotary_all = take(2 * width).reshape(2, heads, 2, -1).sum(axis=2)
    qkv_bias_all = take(3 * width)

    squares = sum_of([chunk.square for chunk in chunks])
    squares = squares + place.group(squares, 1)
    for stage in list(place.small_stages())[1:]:
        squares = stage(squares)
    vectors = (
        down_bias_all, gain_two_all, bias_two_all, out_bias_all, up_bias_all, gain_one_all,
        bias_one_all, qkv_bias_all,
    )
    weight_sq = squares[0, 0] + sum_of([jnp.sum(v * v) for v in vectors])
    rotary_sq = jnp.sum(rotary_all * rotary_all)

    def shard(vector):
        size = vector.shape[0] // n_dp
        return lax.dynamic_slice_in_dim(vector, place.dp_at * size, size)

    down_cols, up_cols, qo_cols, q2_cols = (chunk.blocks() for chunk in chunks)

    def join(cols):
        return jnp.concatenate([part for core in cols for part in core], axis=1)

    qkv_cols = []
    for part in range(3):
        for cols, size in (
            ([one for one, _ in qo_cols], first * 64),
            ([jnp.concatenate(core, axis=1) for core in q2_cols], last * 64),
        ):
            for core in cols:
                qkv_cols.append(core[:, part * size : part * size + size])
    return (
        output,
        input_grad,
        shard(gain_one_all),
        shard(bias_one_all),
        jnp.concatenate(qkv_cols, axis=1),
        shard(qkv_bias_all),
        rotary_all,
        jnp.concatenate([two for _, two in qo_cols], axis=1),
        shard(out_bias_all),
        shard(gain_two_all),
        shard(bias_two_all),
        join(up_cols),
        shard(up_bias_all),
        join(down_cols),
        shard(down_bias_all),
        weight_sq,
        rotary_sq,
    )


def solution(mesh):
    rows = P(("group", "dp"), None)
    placed = (rows, rows) + (P(),) * 13 + (P("group"), P(("group", "dp")))
    return jax.shard_map(
        functools.partial(local, mesh.shape["group"], mesh.shape["dp"]),
        mesh=mesh,
        in_specs=placed,
        out_specs=(
            rows, rows, P("dp"), P("dp"), P("dp", None), P("dp"), P(), P("dp", None), P("dp"),
            P("dp"), P("dp"), P("dp", None), P("dp"), P("dp", None), P("dp"), P(), P(),
        ),
        check_vma=False,
    )
```

```python
import functools
import math

import jax
import jax.numpy as jnp
import numpy as np
from jax import lax
from jax.experimental import pallas as pl
from jax.experimental.pallas import tpu as pltpu
from jax.sharding import PartitionSpec as P

EPSILON = 1e-06
NEG_FILL = -1e30
SIDES = (14, 20, 24)
F32 = jnp.float32
BF16 = jnp.bfloat16
MIB = 1 << 20


def dot(left, right, left_dim, right_dim):
    return lax.dot_general(
        left, right, (((left_dim,), (right_dim,)), ((), ())), preferred_element_type=F32
    )


def smem():
    return pl.BlockSpec(memory_space=pltpu.SMEM)


def whole(shape):
    return pl.BlockSpec(shape, lambda *_: (0,) * len(shape), pipeline_mode=pl.Buffered(1))


def array(shape, kind=BF16):
    return jax.ShapeDtypeStruct(shape, kind)


class Line:
    def __init__(self):
        self.last = []

    def call(
        self, name, body, grid, ins, outs, scratch=(), scalars=None, deps=(), limit=60, long=False
    ):
        lead = 0 if scalars is None else 1
        deps = list(deps) + self.last
        first_out = lead + len(ins) + len(deps)

        def kernel(*refs):
            body(*refs[: lead + len(ins)], *refs[first_out:])

        results = pl.pallas_call(
            kernel,
            name=name,
            grid_spec=pltpu.PrefetchScalarGridSpec(
                num_scalar_prefetch=lead,
                grid=grid,
                in_specs=[spec for _, spec in ins] + [anywhere()] * len(deps),
                out_specs=[spec for _, spec in outs],
                scratch_shapes=list(scratch),
            ),
            out_shape=[shape for shape, _ in outs],
            compiler_params=pltpu.CompilerParams(vmem_limit_bytes=limit * MIB),
            cost_estimate=pl.CostEstimate(
                flops=10**13 if long else 1 << 20, bytes_accessed=1 << 20, transcendentals=0
            ),
        )(*([] if scalars is None else [scalars]), *[value for value, _ in ins], *deps)
        self.last = [results[0]]
        return results


def anywhere():
    return pl.BlockSpec(memory_space=pl.ANY)


def lanes_of(ref):
    return ref[...].astype(F32).reshape(1, -1)


def clip(value, low, high):
    return jnp.minimum(jnp.maximum(value, low), high)


def position_table(slots):
    table = np.zeros((3, slots, 128), np.float32)
    index = np.arange(slots)
    for res, side in enumerate(SIDES):
        within = index % (side * side)
        for lane in (0, 64):
            table[res, index, lane + within // side] = 1
            table[res, index, lane + 32 + within % side] = 1
    return table.astype(jnp.bfloat16)


def weight_lanes():
    table = np.zeros((128, 256), np.float32)
    for index in range(32):
        table[index, :128] = index
        table[32 + index, 128:] = index
    return table.astype(jnp.bfloat16)


def for_each_image(info, slots, body):
    for res, side in enumerate(SIDES):
        patches = side * side

        @pl.when(info[0] == res)
        def _(patches=patches):
            for image in range(slots // patches):
                offset = image * patches
                start = offset // 16 * 16
                span = -(-patches // 16) * 16
                body(image, start, span, offset - start, patches)


def inside(shape, axis, offset, patches):
    index = lax.broadcasted_iota(jnp.int32, shape, axis)
    return (index >= offset) & (index < offset + patches)


def live_rows(info):
    side = jnp.where(info[0] == 0, SIDES[0], jnp.where(info[0] == 1, SIDES[1], SIDES[2]))
    return info[1] * side * side


def swap_halves(values, half):
    pieces = []
    lane = lax.broadcasted_iota(jnp.int32, (values.shape[0], 128), 1)
    first = lane % (2 * half) < half
    for at in range(0, values.shape[1], 128):
        piece = values[:, at : at + 128]
        pieces.append(
            jnp.where(first, pltpu.roll(piece, 128 - half, 1), pltpu.roll(piece, half, 1))
        )
    return pieces[0] if len(pieces) == 1 else jnp.concatenate(pieces, axis=1)


def combine_angles(trig, width):
    cos_row, sin_row = trig[:, :width], trig[:, width : 2 * width]
    cos_col, sin_col = trig[:, 2 * width : 3 * width], trig[:, 3 * width :]
    return cos_row * cos_col - sin_row * sin_col, sin_row * cos_col + cos_row * sin_col


ROWS = 384


def fill_angles(table, freq_ref, width):
    index = lax.broadcasted_iota(jnp.int32, (32, width), 0).astype(F32)
    lane = lax.broadcasted_iota(jnp.int32, (32, width), 1)
    sign = jnp.where(lane % 64 < 32, -1.0, 1.0).astype(F32)
    table[...] = jnp.zeros_like(table)
    for kind in range(2):
        angle = index * freq_ref[kind : kind + 1, :]
        for part, value in enumerate((jnp.cos(angle), jnp.sin(angle) * sign)):
            high = value.astype(BF16)
            low = (value - high.astype(F32)).astype(BF16)
            at = (2 * kind + part) * width
            table[32 * kind : 32 * kind + 32, at : at + width] = high
            table[64 + 32 * kind : 96 + 32 * kind, at : at + width] = low


def normed_rows(values):
    shifted = values - jnp.mean(values, axis=1, keepdims=True)
    inverse = lax.rsqrt(jnp.mean(shifted * shifted, axis=1, keepdims=True) + EPSILON)
    return shifted * inverse, inverse


def row_block(index):
    return pl.ds(pl.multiple_of(index * ROWS, ROWS), ROWS)


def column_half(size, which):
    return pl.ds(pl.multiple_of(which * size, size), size)


def each(count, body):
    def step(index, carry):
        body(index)
        return carry

    lax.fori_loop(0, count, step, 0)


class Outbox:
    def __init__(self, sems, first=0):
        self.sems, self.kinds, self.first = sems, [], first

    def kind(self, blocks, ends):
        self.kinds.append((blocks, ends))
        return len(self.kinds) - 1

    def copy(self, kind, block):
        source, target = self.kinds[kind][1](block)
        return pltpu.make_async_copy(source, target, self.sems.at[self.first + kind, block])

    def send(self, kind, block):
        self.copy(kind, block).start()

    def wait(self, kind):
        for block in range(self.kinds[kind][0]):
            self.copy(kind, block).wait()


def layer_kernel(
    scal, g1_ref, b1_ref, qb_ref, freq_ref, ob_ref, g2_ref, b2_ref, ub_ref,
    pos_hbm, tok_hbm, w_hbm, ow_hbm, uw_hbm, dw_hbm, cot_hbm,
    zero_ref, sums_ref, upsum_ref, dsent_hbm, down_hbm, usent_hbm, up_hbm, in_hbm, stat_hbm, tab_hbm,
    qkv_hbm, mid_hbm, act_hbm, branch_hbm, attg_hbm, grad_hbm,
    pos_s, tok_s, w_s, ow_s, uw_s, cot_s, tab_s, in_s, qkv_s, stat_s, att_s, mid_s, sec_s, act_s, slope_s,
    grad_s, tok_sem, load_sem, store_sem, grad_sem,
):
    slots, width = att_s.shape
    hidden = act_s.shape[1]
    blocks, pairs, tiles = slots // ROWS, width // 128, hidden // width
    half = width // 2

    def tokens(block):
        rows = row_block(block)
        return pltpu.make_async_copy(tok_hbm.at[rows], tok_s.at[rows], tok_sem.at[block])

    def load(at):
        source, target = (
            [(w_hbm.at[:, part * width : (part + 1) * width], w_s.at[part]) for part in range(3)]
            + [(pos_hbm.at[scal[0]], pos_s), (ow_hbm, ow_s), (uw_hbm, uw_s), (cot_hbm, cot_s)]
            + [(dw_hbm.at[part * width : (part + 1) * width], w_s.at[part]) for part in range(tiles)]
        )[at]
        return pltpu.make_async_copy(source, target, load_sem.at[at])

    out = Outbox(store_sem)

    def by_rows(source, target):
        return out.kind(blocks, lambda block: (source.at[row_block(block)], target.at[row_block(block)]))

    send_in, send_act, send_mid = (
        by_rows(source, target) for source, target in ((in_s, in_hbm), (act_s, act_hbm), (mid_s, mid_hbm))
    )
    send_qkv = out.kind(
        blocks, lambda block: (qkv_s.at[:, row_block(block)], qkv_hbm.at[:, row_block(block)])
    )
    send_tab = out.kind(1, lambda block: (tab_s, tab_hbm))
    send_stat = out.kind(1, lambda block: (stat_s, stat_hbm))
    for ref in (zero_ref, sums_ref, upsum_ref):
        ref[...] = jnp.zeros_like(ref)
    tokens(0).start()
    for at in range(4):
        load(at).start()
    for block in range(1, blocks):
        tokens(block).start()
    for at in range(4, 7):
        load(at).start()
    fill_angles(tab_s, freq_ref, width)
    out.send(send_tab, 0)
    for at in range(4):
        load(at).wait()

    def project(block):
        tokens(block).wait()
        rows = row_block(block)
        normed, _ = normed_rows(tok_s[rows, :].astype(F32))
        first_in = (normed * lanes_of(g1_ref) + lanes_of(b1_ref)).astype(BF16)
        in_s[rows, :] = first_in
        cosine, sine = combine_angles(dot(pos_s[rows, :], tab_s[...], 1, 0), width)
        for part in range(3):
            bias = qb_ref[part * width : (part + 1) * width].astype(F32).reshape(1, -1)
            projected = dot(first_in, w_s[part], 1, 0) + bias
            if part < 2:
                projected = projected * cosine + swap_halves(projected, 32) * sine
            if part == 0:
                projected = projected * 0.125
            projected = projected.astype(BF16)
            for pair in range(pairs):
                qkv_s[part * pairs + pair, rows, :] = projected[:, pair * 128 : pair * 128 + 128]
        out.send(send_in, block)
        out.send(send_qkv, block)

    each(blocks, project)

    def attend(pair):
        cols = column_half(128, pair)
        q_ref, k_ref, v_ref = (qkv_s.at[part * pairs + pair] for part in range(3))
        att_s[:, cols] = v_ref[...]
        live = live_rows(scal)

        def image_step(image, start, span, offset, patches):
            rows = slice(start, start + span)
            exact = span == patches
            turned = v_ref[rows, :].T
            mixed = []
            for head in range(2):
                lanes = slice(head * 64, head * 64 + 64)
                scores = dot(k_ref[rows, lanes], q_ref[rows, lanes], 1, 1)
                if not exact:
                    scores = jnp.where(inside(scores.shape, 0, offset, patches), scores, NEG_FILL)
                top = jnp.max(scores, axis=0, keepdims=True)
                powers = jnp.exp(scores - top)
                mass = jnp.sum(powers, axis=0, keepdims=True)
                mixed.append(dot(turned[lanes], powers.astype(BF16), 1, 0) * (1.0 / mass))
                stat_s[pair, image, head : head + 1, 0:span] = top + jnp.log(mass)
            result = jnp.concatenate(mixed, axis=0).T
            keep = lax.broadcasted_iota(jnp.int32, result.shape, 0) < live - start
            if not exact:
                keep = keep & inside(result.shape, 0, offset, patches)
            result = jnp.where(keep, result, att_s[rows, cols].astype(F32))
            att_s[rows, cols] = result.astype(BF16)

        for_each_image(scal, slots, image_step)

    for at in range(7, 7 + tiles):
        load(at).start()
    each(pairs, attend)
    out.send(send_stat, 0)
    load(4).wait()
    load(5).wait()

    def feed(block):
        rows = row_block(block)
        middle = tok_s[rows, :].astype(F32) + (dot(att_s[rows, :], ow_s[...], 1, 0) + lanes_of(ob_ref))
        mid_s[rows, :] = middle
        normed, _ = normed_rows(middle)
        second_in = (normed * lanes_of(g2_ref) + lanes_of(b2_ref)).astype(BF16)
        sec_s[rows, :] = second_in
        scale = math.sqrt(2.0 / math.pi)
        for at in range(0, hidden, 768):
            cols = slice(at, at + 768)
            pre = dot(second_in, uw_s[:, cols], 1, 0) + ub_ref[cols].astype(F32).reshape(1, -1)
            square = pre * pre
            bent = jnp.tanh(pre * (scale + (scale * 0.044715) * square))
            gate = 0.5 + 0.5 * bent
            act_s[rows, cols] = (pre * gate).astype(BF16)
            lean = pre * (scale + (3.0 * scale * 0.044715) * square)
            slope_s[rows, cols] = (gate * (1.0 + (1.0 - bent) * lean)).astype(BF16)
        for kind in (send_act, send_mid):
            out.send(kind, block)

    each(blocks, feed)
    load(6).wait()
    cot_s[...] = live_cotangent(scal, cot_s, 0).astype(BF16)

    def grad_copies(tile, slot):
        rows = pl.ds(pl.multiple_of(tile * width, width), width)
        return [
            pltpu.make_async_copy(
                grad_s.at[slot, :, column_half(half, which)], target.at[rows], grad_sem.at[slot, at])
            for at, (which, target) in enumerate(((1 - scal[2], dsent_hbm), (scal[2], down_hbm)))
        ]

    def down_grad(tile):
        slot = lax.rem(tile, 2)

        @pl.when(tile >= 2)
        def _():
            for copy in grad_copies(tile - 2, slot):
                copy.wait()

        grad_s[slot] = dot(act_s[:, column_half(width, tile)], cot_s[...], 0, 0)
        for copy in grad_copies(tile, slot):
            copy.start()

    each(tiles, down_grad)
    for kind in (send_in, send_mid):
        out.wait(kind)
    for at in range(7, 7 + tiles):
        load(at).wait()
    branch_s, attg_s = in_s, tok_s
    late = Outbox(store_sem, len(out.kinds))
    late_kinds = [
        late.kind(blocks, lambda block, source=source, target=target: (
            source.at[row_block(block)], target.at[row_block(block)]))
        for source, target in ((branch_s, branch_hbm), (attg_s, attg_hbm), (mid_s, grad_hbm))
    ]

    def back_rows(block):
        rows = row_block(block)
        up_low = cot_s[rows, :]
        upstream = up_low.astype(F32)
        for part in range(tiles):
            cols = slice(part * width, (part + 1) * width)
            act_grad = dot(up_low, w_s[part], 1, 1)
            hidden_low = (slope_s[rows, cols].astype(F32) * act_grad).astype(BF16)
            slope_s[rows, cols] = hidden_low
            upsum_ref[0:1, cols] += jnp.sum(hidden_low.astype(F32), axis=0, keepdims=True)
        back = dot(slope_s[rows, :], uw_s[...], 1, 1)
        normed, inverse = normed_rows(mid_s[rows, :])
        scaled = back * lanes_of(g2_ref)
        inner = (
            scaled
            - jnp.mean(scaled, axis=1, keepdims=True)
            - normed * jnp.mean(scaled * normed, axis=1, keepdims=True)
        )
        middle_grad = upstream + inverse * inner
        mid_s[rows, :] = middle_grad
        branch = middle_grad.astype(BF16)
        branch_s[rows, :] = branch
        attg_s[rows, :] = dot(branch, ow_s[...], 1, 1).astype(BF16)
        sums_ref[0:1, :] += jnp.sum(upstream, axis=0, keepdims=True)
        sums_ref[1:2, :] += jnp.sum(back * normed, axis=0, keepdims=True)
        sums_ref[2:3, :] += jnp.sum(back, axis=0, keepdims=True)
        sums_ref[3:4, :] += jnp.sum(branch.astype(F32), axis=0, keepdims=True)
        for kind in late_kinds:
            late.send(kind, block)

    each(blocks, back_rows)

    def up_copy(tile, slot, wait):
        for first, target in ((0, usent_hbm), (tiles // 2, up_hbm)):

            @pl.when((tile >= first) & (tile < first + tiles // 2))
            def _(first=first, target=target):
                copy = pltpu.make_async_copy(
                    grad_s.at[slot], target.at[:, column_half(width, tile - first)], grad_sem.at[slot, 0]
                )
                copy.wait() if wait else copy.start()

    def up_grad(tile):
        slot = lax.rem(tile, 2)

        @pl.when(tile < 2)
        def _():
            for copy in grad_copies(tile + tiles - 2, slot):
                copy.wait()

        @pl.when(tile >= 2)
        def _():
            up_copy(tile - 2, slot, True)

        side = jnp.where(tile < tiles // 2, 1 - scal[2], scal[2])
        place = side * (tiles // 2) + lax.rem(tile, tiles // 2)
        grad_s[slot] = dot(sec_s[...], slope_s[:, column_half(width, place)], 0, 0)
        up_copy(tile, slot, False)

    each(tiles, up_grad)
    slot = tiles % 2
    up_copy(jnp.int32(tiles - 2), slot, True)
    grad_s[slot] = dot(att_s[...], branch_s[...], 0, 0)
    copies = [
        pltpu.make_async_copy(
            grad_s.at[slot, :, column_half(half, which)],
            target.at[:, hidden // 2 : hidden // 2 + half], grad_sem.at[slot, at])
        for at, (which, target) in enumerate(((1 - scal[2], usent_hbm), (scal[2], up_hbm)))
    ]
    for copy in copies:
        copy.start()
    up_copy(jnp.int32(tiles - 1), (tiles - 1) % 2, True)
    for copy in copies:
        copy.wait()
    for kind in (send_act, send_qkv, send_tab, send_stat):
        out.wait(kind)
    for kind in late_kinds:
        late.wait(kind)


def zeros_kernel(out_ref):
    out_ref[...] = jnp.zeros_like(out_ref)


def live_cotangent(info, cot_ref, first_row):
    row = lax.broadcasted_iota(jnp.int32, cot_ref.shape, 0) + first_row
    return jnp.where(row < live_rows(info), cot_ref[...].astype(F32), 0.0)


def attend_back_kernel(
    info, pos_ref, t0, t1, t2, t3, lanes_ref, in_ref, q_ref, k_ref, v_ref, up_ref, stat_ref,
    *rest,
):
    dw_refs, (gq_ref, gk_ref, gv_ref, sums_ref, dq_acc, dk_acc, dv_acc) = rest[:-7], rest[-7:]
    @pl.when(info[0] < 2)
    def _():
        for acc in (dq_acc, dk_acc, dv_acc):
            acc[...] = jnp.zeros_like(acc)

    def image_step(image, start, span, offset, patches):
        rows = slice(start, start + span)
        exact = span == patches
        for head in range(2):
            lanes = slice(head * 64, head * 64 + 64)
            query, key = q_ref[rows, lanes], k_ref[rows, lanes]
            value, upstream = v_ref[rows, lanes], up_ref[rows, lanes]
            probs = jnp.exp(dot(key, query, 1, 1) - stat_ref[image, head : head + 1, 0:span])
            if not exact:
                keep = inside(probs.shape, 0, offset, patches)
                keep = keep & inside(probs.shape, 1, offset, patches)
                probs = jnp.where(keep, probs, 0.0)
            prob_grad = dot(value, upstream, 1, 1)
            inner = jnp.sum(probs * prob_grad, axis=0, keepdims=True)
            score_low = (probs * (prob_grad - inner)).astype(BF16)
            value_grad = dot(probs.astype(BF16), upstream, 1, 0)
            key_grad = dot(score_low, query, 1, 0)
            query_grad = dot(key.T, score_low, 1, 0).T
            if exact:
                dq_acc[rows, lanes] = query_grad
                dk_acc[rows, lanes] = key_grad
                dv_acc[rows, lanes] = value_grad
            else:
                dq_acc[rows, lanes] += query_grad
                dk_acc[rows, lanes] += key_grad
                dv_acc[rows, lanes] += value_grad

    for_each_image(info, q_ref.shape[0], image_step)
    pos = pos_ref[...]
    table = jnp.concatenate([t0[...], t1[...], t2[...], t3[...]], axis=1)
    cosine, sine = combine_angles(dot(pos, table, 1, 0), 128)
    places = dot(pos, lanes_ref[...], 1, 0)
    lane = lax.broadcasted_iota(jnp.int32, (1, 128), 1)
    sign = jnp.where(lane % 64 < 32, 1.0, -1.0)
    angle_grad = None
    sums_ref[...] = jnp.zeros_like(sums_ref)
    for row, (acc, low_ref, out_ref, up, down) in enumerate(
        ((dq_acc, q_ref, gq_ref, 0.125, 8.0), (dk_acc, k_ref, gk_ref, 1.0, 1.0))
    ):
        grad = acc[...] * up
        swapped = swap_halves(grad, 32)
        term = swapped * (low_ref[...].astype(F32) * down)
        angle_grad = term if angle_grad is None else angle_grad + term
        pre = (grad * cosine - swapped * sine).astype(BF16)
        out_ref[...] = pre
        sums_ref[2 + row : 3 + row, :] = jnp.sum(pre.astype(F32), axis=0, keepdims=True)
    value_low = dv_acc[...].astype(BF16)
    gv_ref[...] = value_low
    sums_ref[4:5, :] = jnp.sum(value_low.astype(F32), axis=0, keepdims=True)
    for row in range(2):
        place = places[:, row * 128 : row * 128 + 128]
        sums_ref[row : row + 1, :] = sign * jnp.sum(place * angle_grad, axis=0, keepdims=True)
    grads = jnp.concatenate([gq_ref[...], gk_ref[...], gv_ref[...]], axis=1)
    weight_grad = dot(in_ref[...], grads, 0, 0)
    for at, ref in enumerate(dw_refs):
        ref[...] = weight_grad[at * ref.shape[0] : (at + 1) * ref.shape[0]]


def input_kernel(
    scal, tok_ref, gain_ref, grad_ref, w_ref, down_ref, up_ref, other_ref, own_ref, *refs
):
    pieces, (out_ref, sums_ref, down_out, up_out, pair_out) = refs[:6], refs[6:]
    width, half = tok_ref.shape[1], pieces[0].shape[1]

    @pl.when(pl.program_id(0) == 0)
    def _():
        sums_ref[...] = jnp.zeros_like(sums_ref)
        down_out[...] = down_ref[...]
        up_out[...] = up_ref[...]
        count = own_ref.shape[0]
        for pair in range(count):
            pair_out[count * (1 - scal[2]) + pair] = other_ref[pair]
            pair_out[count * scal[2] + pair] = own_ref[pair]

    back = None
    for side, which in enumerate((1 - scal[2], scal[2])):
        for part in range(3):
            cols = pl.ds(pl.multiple_of(part * width + which * half, half), half)
            term = dot(pieces[3 * side + part][...], w_ref[:, cols], 1, 1)
            back = term if back is None else back + term
    values = tok_ref[...].astype(F32)
    shifted = values - jnp.mean(values, axis=1, keepdims=True)
    inverse = lax.rsqrt(jnp.mean(shifted * shifted, axis=1, keepdims=True) + EPSILON)
    normed = shifted * inverse
    scaled = back * lanes_of(gain_ref)
    inner = (
        scaled
        - jnp.mean(scaled, axis=1, keepdims=True)
        - normed * jnp.mean(scaled * normed, axis=1, keepdims=True)
    )
    out_ref[...] = (grad_ref[...] + inverse * inner).astype(BF16)
    sums_ref[0:1, :] += jnp.sum(back * normed, axis=0, keepdims=True)
    sums_ref[1:2, :] += jnp.sum(back, axis=0, keepdims=True)


def output_kernel(act_ref, dw_ref, db_ref, mid_ref, out_ref):
    out_ref[...] = (
        mid_ref[...] + (dot(act_ref[...], dw_ref[...], 1, 0) + lanes_of(db_ref))
    ).astype(BF16)


def weight_of(counted, totals, slots):
    return F32(slots) / (3.0 * jnp.sum(jnp.where(counted > 0, totals, 0.0)))


def combine(line, name, scal, counts, slots, own, got, shard, split, long=False):
    height, total = own.shape
    tile = max(2 * shard, height // 4)
    if shard % 16:
        split = None

    def kernel(scal_ref, *refs):
        first = len(counts) + 1
        counted, own_ref, got_refs, outs = (
            refs[: first - 1], refs[first - 1], refs[first : first + len(got)], refs[first + len(got) :]
        )
        totals = sum_of([ref[0:1] for ref in counted[2:]])
        mine = weight_of(counted[0][0:1], totals, slots)
        theirs = weight_of(counted[1][0:1], totals, slots)
        target = outs[-1] if split else outs[0]
        for at, got_ref in enumerate(got_refs):

            @pl.when(pl.program_id(0) // steps_each == at)
            def _(got_ref=got_ref):
                target[...] = own_ref[...] * mine + got_ref[...] * theirs

        if split:
            stride = split // 2
            for at in range(tile // shard // stride):
                sides = (scal_ref[4], 1 - scal_ref[4]) if split == 4 else (0,)
                for index, (x_bit, y_bit) in enumerate(
                    ((x, y) for y in sides for x in (scal_ref[3], 1 - scal_ref[3]))
                ):
                    rows = (stride * at + y_bit) * shard + x_bit * (shard // 2)
                    outs[index][at] = target[pl.ds(pl.multiple_of(rows, 8), shard // 2), :]

    block = pl.BlockSpec((tile, total), lambda i, scal: (i, 0))
    got = list(got) if isinstance(got, (list, tuple)) else [got]
    ins = [(count, whole(count.shape)) for count in counts] + [(own, block)]
    steps_each = height // tile // len(got)
    ins += [
        (one, pl.BlockSpec((tile, total), functools.partial(
            lambda at, i, scal: (clip(i - at * steps_each, 0, steps_each - 1), 0), at)))
        for at, one in enumerate(got)
    ]
    if split is None:
        return line.call(
            name, kernel, (height // tile,), ins, [(array((height, total), F32), block)], scalars=scal,
            long=long,
        )[0]
    count = height // shard

    shards = split // 2
    outs = [(array((count // shards, shard // 2, total), F32), pl.BlockSpec(
        (tile // shard // shards, shard // 2, total), lambda i, scal: (i, 0, 0)))] * split
    return line.call(
        name, kernel, (height // tile,), ins, outs, [pltpu.VMEM((tile, total), F32)], scalars=scal
    )


class Place:
    def __init__(self, n_group, n_dp):
        self.n_group, self.n_dp = n_group, n_dp
        group_at, self.dp_at = lax.axis_index("group"), lax.axis_index("dp")
        self.core, self.x = lax.rem(group_at, 2), lax.div(group_at, 2)
        self.dp_bits = n_dp.bit_length() - 1
        self.dp = [lax.rem(lax.div(self.dp_at, 1 << bit), 2) for bit in range(self.dp_bits)]

    def group(self, value, mask):
        return lax.ppermute(value, "group", [(at, at ^ mask) for at in range(self.n_group)])

    def along(self, value, mask):
        return lax.ppermute(value, "dp", [(at, at ^ mask) for at in range(self.n_dp)])

    def across(self, value, group_mask, dp_mask):
        pairs = [
            (at * self.n_dp + dp, (at ^ group_mask) * self.n_dp + (dp ^ dp_mask))
            for at in range(self.n_group) for dp in range(self.n_dp)
        ]
        return lax.ppermute(value, ("group", "dp"), pairs)

    def stages(self, group=True):
        if group:
            yield lambda v: [self.group(v, mask) for mask in (1, 2, 3)]
        for bit in range(0, self.dp_bits, 2):
            masks = [1 << bit] if bit + 1 == self.dp_bits else [1 << bit, 2 << bit, 3 << bit]
            yield lambda v, masks=masks: [self.along(v, mask) for mask in masks]


def sum_of(terms):
    result = terms[0]
    for term in terms[1:]:
        result = result + term
    return result


class Scatter:
    def __init__(self, place, kept, rows, cols, joint, widths=()):
        self.place, self.rows, self.widths = place, rows // place.n_dp, list(widths)
        self.bit = 1 if joint else 0
        if not isinstance(kept, (list, tuple)):
            tall, wide = self.rows, cols
            while tall % 16:
                tall, wide = 2 * tall, wide // 2
            shards = place.n_dp // 2 if joint else place.n_dp
            view = kept.reshape(shards, -1, 2, tall // 2, wide)

            def part(y, x):
                found = lax.dynamic_index_in_dim(view, y, 1, keepdims=False)
                return lax.dynamic_index_in_dim(found, x, 1, keepdims=False)

            kept = [
                part(y, x)
                for y in ((place.dp[0], 1 - place.dp[0]) if joint else (0,))
                for x in (place.x, 1 - place.x)
            ]
        masks = ((0, 0), (2, 0), (0, 1), (2, 1))
        self.terms = [[kept[0]]] + [
            [place.across(piece, *mask)] for piece, mask in zip(kept[1:], masks[1:])
        ]

    def job(self):
        place, bit = self.place, self.bit
        lead, half, cols = self.terms[0][0].shape
        counts = [len(term) for term in self.terms]

        def read(refs, at):
            refs, found = list(refs), []
            for count in counts:
                rows = [ref[:, at] for ref in (refs.pop(0) for _ in range(count))]
                found.append(rows[0] if count == 1 else jnp.concatenate(rows, axis=1))
            return sum_of(found)

        if bit < place.dp_bits:
            wide, cut = self.widths.pop(0) if self.widths else (2, 1)
            wide, cut = min(wide, place.dp_bits - bit), cut if half % (8 * cut) == 0 else 1
            size = 1 << wide
            ins = [
                (one.reshape(lead // size, size, -1, cols), None) for term in self.terms for one in term
            ]

            def body(scal, ins, outs):
                for mask in range(size):
                    at = scal[4 + bit] if not mask % 2 else 1 - scal[4 + bit]
                    if wide == 2:
                        at = at + 2 * (scal[5 + bit] if mask < 2 else 1 - scal[5 + bit])
                    value = read(ins, at)
                    if mask == 0:
                        outs[0][...] = value
                    for part in range(cut if mask else 0):
                        rows = slice(part * half // cut, (part + 1) * half // cut)
                        outs[1 + (mask - 1) * cut + part][...] = value[:, rows]

            def then(mine, *sent):
                self.terms = [[mine]] + [
                    [place.along(value, mask << bit) for value in sent[(mask - 1) * cut : mask * cut]]
                    for mask in range(1, size)
                ]

            self.bit += wide
            shapes = [(lead // size, half, cols)]
            shapes += [(lead // size, half // cut, cols)] * ((size - 1) * cut)
            return ins, shapes, body, then
        ins = [(one.reshape(1, 1, -1, cols), None) for term in self.terms for one in term]
        self.terms = []

        def body(scal, ins, outs):
            mine = read(ins, 0)[0]
            outs[0][...] = mine
            outs[1][...] = jnp.broadcast_to(jnp.sum(mine * mine), outs[1].shape)

        def then(mine, square):
            self.square = square
            over_x = place.group(mine, 2)
            self.parts = [mine, place.group(mine, 1), over_x, place.group(over_x, 1)]

        return ins, [(half, cols), (8, 128)], body, then

    def blocks(self):
        place = self.place
        mine, core, x, both = self.parts
        found = []
        for at in (0, 1):
            here = jnp.where(place.core == at, mine, core)
            there = jnp.where(place.core == at, x, both)
            low, high = jnp.where(place.x == 0, here, there), jnp.where(place.x == 0, there, here)
            found.append(jnp.concatenate([low, high]).reshape(self.rows, -1))
        return found


class Scattered:
    def __init__(self, place, kept):
        self.place = place
        self.mine = lax.psum_scatter(kept, "dp", scatter_dimension=0, tiled=True)
        self.got = None

    def job(self):
        place = self.place
        if self.got is None:

            def hand_on(scal, ins, outs):
                outs[0][...] = ins[0][...]

            def start(mine):
                self.mine, self.got = mine, place.group(mine, 2)

            return [(self.mine, None)], [self.mine.shape], hand_on, start
        ins = [(self.mine, None), (self.got, None)]

        def body(scal, ins, outs):
            outs[0][...] = ins[0][...] + ins[1][...]
            outs[1][...] = jnp.broadcast_to(jnp.sum(outs[0][...] * outs[0][...]), outs[1].shape)

        def then(mine, square):
            self.mine, self.square = mine, square
            self.theirs = place.group(mine, 1)

        return ins, [self.mine.shape, (8, 128)], body, then

    def blocks(self):
        first = self.place.core == 0
        return [jnp.where(first, self.mine, self.theirs), jnp.where(first, self.theirs, self.mine)]


def run_jobs(line, name, scal, jobs, long=False):
    ins = [
        (value, spec if spec is not None else whole(value.shape))
        for job in jobs for value, spec in job[0]
    ]
    outs = [
        (array(shape, F32), pl.BlockSpec(shape, functools.partial(lambda rank, *_: (0,) * rank, len(shape))))
        for job in jobs for shape in job[1]
    ]

    def kernel(scal_ref, *refs):
        at_in, at_out = 0, len(ins)
        for job_ins, job_outs, body, _ in jobs:
            body(
                scal_ref, refs[at_in : at_in + len(job_ins)], refs[at_out : at_out + len(job_outs)]
            )
            at_in += len(job_ins)
            at_out += len(job_outs)

    results = line.call(name, kernel, (1,), ins, outs, scalars=scal, long=long)
    at = 0
    for _, job_outs, _, then in jobs:
        then(*results[at : at + len(job_outs)])
        at += len(job_outs)


def local(
    n_group, n_dp, tokens, cotangent, norm1_gain, norm1_bias, qkv_weight, qkv_bias, rotary_freqs,
    out_weight, out_bias, norm2_gain, norm2_bias, up_weight, up_bias, down_weight, down_bias,
    group_res, images,
):
    slots, width = tokens.shape
    heads = rotary_freqs.shape[1]
    hidden = up_weight.shape[1]
    pairs = heads // 2
    blocks = slots // ROWS
    place = Place(n_group, n_dp)
    line = Line()
    scal = jnp.concatenate(
        [group_res, images, jnp.stack([place.core, place.x] + place.dp).astype(jnp.int32)]
    ).astype(jnp.int32)

    def rows_of(cols, first=0):
        return pl.BlockSpec((ROWS, cols), lambda i, *_: (clip(i - first, 0, blocks - 1), 0))

    def param(vector):
        return (vector, whole(vector.shape))

    def kept_sum(rows, cols):
        return (array((rows, cols), F32), pl.BlockSpec((rows, cols), lambda *_: (0, 0)))

    def in_hbm(shape, kind=BF16):
        return (array(shape, kind), anywhere())

    side = jnp.where(group_res[0] == 0, SIDES[0], jnp.where(group_res[0] == 1, SIDES[1], SIDES[2]))
    lane = lax.broadcasted_iota(jnp.int32, (8, 128), 1)
    patches = (images[0] * side * side).astype(F32)
    totals = jnp.where(lane == group_res[0], patches, 0.0)
    here = totals
    got = [place.group(totals, mask) for mask in (1, 2, 3)]
    beside = got[0]
    deps = [here]

    half_freqs = jnp.concatenate([rotary_freqs, rotary_freqs], axis=-1).reshape(2, width)
    pos = jnp.asarray(position_table(slots))
    stat_shape = (slots // SIDES[0] ** 2, 8, -(-(SIDES[2] ** 2) // 128) * 128)
    tiles = hidden // width
    half = width // 2

    def vmem(*shape, kind=BF16):
        return pltpu.VMEM(shape, kind)

    (
        zero, down_sums, up_sums, down_sent, down_own, up_sent, up_own, first_in, stats, trig_table, qkv,
        middle, act, branch, att_grad, mid_grad,
    ) = line.call(
        "layer", layer_kernel, (1,),
        [
            param(norm1_gain), param(norm1_bias), param(qkv_bias), param(half_freqs), param(out_bias),
            param(norm2_gain), param(norm2_bias), param(up_bias), (pos, anywhere()), (tokens, anywhere()),
            (qkv_weight, anywhere()), (out_weight, anywhere()), (up_weight, anywhere()),
            (down_weight, anywhere()), (cotangent, anywhere()),
        ],
        [
            kept_sum(8, 128), kept_sum(8, width), kept_sum(8, hidden),
            in_hbm((hidden, half), F32), in_hbm((hidden, half), F32),
            in_hbm((width, hidden // 2 + half), F32), in_hbm((width, hidden // 2 + half), F32),
            in_hbm((slots, width)), in_hbm((pairs,) + stat_shape, F32), in_hbm((128, 4 * width)),
            in_hbm((3 * pairs, slots, 128)), in_hbm((slots, width), F32), in_hbm((slots, hidden)),
            in_hbm((slots, width)), in_hbm((slots, width)), in_hbm((slots, width), F32),
        ],
        [
            vmem(slots, 128), vmem(slots, width), vmem(tiles, width, width), vmem(width, width),
            vmem(width, hidden), vmem(slots, width), vmem(128, 4 * width), vmem(slots, width),
            vmem(3 * pairs, slots, 128), vmem(pairs, *stat_shape, kind=F32), vmem(slots, width),
            vmem(slots, width, kind=F32), vmem(slots, width), vmem(slots, hidden), vmem(slots, hidden),
            vmem(2, width, width, kind=F32),
            pltpu.SemaphoreType.DMA((blocks,)), pltpu.SemaphoreType.DMA((7 + tiles,)),
            pltpu.SemaphoreType.DMA((9, blocks)), pltpu.SemaphoreType.DMA((2, 2)),
        ],
        scalars=scal, limit=63, deps=deps,
    )
    down_got = place.group(down_sent, 1)
    up_got = place.group(up_sent, 1)
    totals = sum_of([totals] + got) + zero
    stages = list(place.stages(False))
    got = stages.pop(0)(totals)
    (zero,) = line.call("mark", zeros_kernel, (1,), [], [kept_sum(8, 128)], long=True)
    for stage in stages:
        totals = sum_of([totals] + got) + zero
        got = stage(totals)
    counts = [here, beside, totals] + got
    scale = weight_of(here[0], sum_of(counts[2:])[0], slots)
    shard = width // n_dp

    def reduce(name, own, got, rows, split, long=False):
        return combine(line, name, scal, counts, slots, own, got, rows, split, long)

    down = Scattered(place, reduce("down_sum", down_own, down_got, hidden // n_dp, None))
    up = Scatter(
        place, reduce("up_sum", up_own, up_got, shard, 2), width, up_own.shape[1], False, ((1, 2),)
    )

    lanes_table = jnp.asarray(weight_lanes())

    def attend_back(own, split):
        count = pairs // 2

        def at(i, scal):
            return count * (scal[2] if own else 1 - scal[2]) + i

        def table_block(part):
            return pl.BlockSpec((128, 128), lambda i, scal: (0, part * pairs + at(i, scal)))

        def qkv_block(part):
            return pl.BlockSpec((None, slots, 128), lambda i, scal: (part * pairs + at(i, scal), 0, 0))

        out = (array((slots, count * 128)), pl.BlockSpec((slots, 128), lambda i, scal: (0, i)))
        return line.call(
            "attend_back", attend_back_kernel, (count,),
            [(pos, pl.BlockSpec((None, slots, 128), lambda i, scal: (scal[0], 0, 0)))]
            + [(trig_table, table_block(part)) for part in range(4)]
            + [param(lanes_table), param(first_in)]
            + [(qkv, qkv_block(part)) for part in range(3)]
            + [
                (att_grad, pl.BlockSpec((slots, 128), lambda i, scal: (0, at(i, scal)))),
                (stats, pl.BlockSpec(
                    (None,) + stat_shape, lambda i, scal: (at(i, scal), 0, 0, 0))),
            ],
            [(
                array((width // split, count * 384), F32),
                pl.BlockSpec((width // split, 384), lambda i, scal: (0, i)),
            )] * split
            + [out] * 3
            + [(array((count, 8, 128), F32), pl.BlockSpec((None, 8, 128), lambda i, scal: (i, 0, 0)))],
            scratch=[pltpu.VMEM((slots, 128), F32)] * 3,
            scalars=scal,
        )

    def jobs(name, *chunks, long=False):
        run_jobs(line, name, scal, [chunk.job() for chunk in chunks], long)

    *other_grads, other_sums = attend_back(False, 2)
    qkv_got = [place.group(other_grads.pop(0), 1) for _ in range(2)]
    qkv_own, *own_grads, own_sums = attend_back(True, 1)
    qkv_grad = Scatter(
        place, reduce("qkv_sum", qkv_own, qkv_got, shard, 4), width, qkv_own.shape[1], True
    )
    input_grad, sums_one, down_sums, up_sums, pair_sums = line.call(
        "input_grad", input_kernel, (blocks,),
        [
            (tokens, rows_of(width)), param(norm1_gain), (mid_grad, rows_of(width)),
            param(qkv_weight), param(down_sums), param(up_sums), param(other_sums), param(own_sums),
        ] + [(piece, rows_of(piece.shape[1])) for piece in other_grads + own_grads],
        [
            (array((slots, width)), rows_of(width)), kept_sum(8, width), kept_sum(8, width),
            kept_sum(8, hidden),
            (array((pairs, 8, 128), F32), pl.BlockSpec((pairs, 8, 128), lambda *_: (0, 0, 0))),
        ],
        scalars=scal,
    )
    pair_all = pair_sums[:, :5].transpose(1, 0, 2)
    vectors = [
        sums_one[0], sums_one[1], pair_all[2:].reshape(-1), down_sums[3], down_sums[1], down_sums[2],
        up_sums[0], down_sums[0],
    ]
    small = jnp.concatenate(
        [vector.reshape(n_dp, -1) for vector in vectors + [pair_all[:2].reshape(-1)]], axis=1
    )
    small = small * scale
    jobs("up0", up)
    (output,) = line.call(
        "output", output_kernel, (blocks,),
        [(act, rows_of(hidden)), param(down_weight), param(down_bias), (middle, rows_of(width))],
        [(array((slots, width)), rows_of(width))],
    )
    jobs("qkv0", qkv_grad)
    jobs("down_hold", down)
    jobs("up1", up)
    while qkv_grad.terms:
        jobs("qkv_rest", qkv_grad)
    while up.terms:
        jobs("up_rest", up)
    jobs("down_x", down)
    square = qkv_grad.square + up.square + 0.5 * down.square
    small = jnp.concatenate([small, jnp.broadcast_to(square[:1], (n_dp, 128))], axis=1)
    small = small + place.group(small, 1)
    for bit in range(place.dp_bits):
        small = small + place.along(small, 1 << bit)
    small = small + place.group(small, 2)

    cut = sum(vector.size for vector in vectors) // n_dp
    rotary_all = small[:, cut:-128].reshape(2, heads, 2, -1).sum(axis=2)
    rotary_sq = jnp.sum(rotary_all * rotary_all)
    weight_sq = small[0, -1] + jnp.sum(small[:, :cut] * small[:, :cut])
    here = lax.dynamic_index_in_dim(small, place.dp_at, 0, keepdims=False)
    shards, at = [], 0
    for vector in vectors:
        size = vector.size // n_dp
        shards.append(here[at : at + size])
        at += size
    gain_one, bias_one, qkv_vector, out_vector, gain_two, bias_two, up_vector, down_vector = shards

    qkv_cols = [
        block.reshape(-1, pairs // 2, 3, 128).transpose(0, 2, 1, 3) for block in qkv_grad.blocks()
    ]
    qkv_all = jnp.concatenate(qkv_cols, axis=2).reshape(-1, 3 * width)
    up_cols = up.blocks()
    split = hidden // 2
    return (
        output,
        input_grad,
        gain_one,
        bias_one,
        qkv_all,
        qkv_vector,
        rotary_all,
        jnp.concatenate([block[:, split:] for block in up_cols], axis=1),
        out_vector,
        gain_two,
        bias_two,
        jnp.concatenate([block[:, :split] for block in up_cols], axis=1),
        up_vector,
        jnp.concatenate(down.blocks(), axis=1),
        down_vector,
        weight_sq,
        rotary_sq,
    )


def solution(mesh):
    rows = P(("group", "dp"), None)
    placed = (rows, rows) + (P(),) * 13 + (P("group"), P(("group", "dp")))
    return jax.shard_map(
        functools.partial(local, mesh.shape["group"], mesh.shape["dp"]),
        mesh=mesh,
        in_specs=placed,
        out_specs=(
            rows, rows, P("dp"), P("dp"), P("dp", None), P("dp"), P(), P("dp", None), P("dp"),
            P("dp"), P("dp"), P("dp", None), P("dp"), P("dp", None), P("dp"), P(), P(),
        ),
        check_vma=False,
    )
```

```python
import functools
import math

import jax
import jax.numpy as jnp
import numpy as np
from jax import lax
from jax.experimental import pallas as pl
from jax.experimental.pallas import tpu as pltpu
from jax.sharding import PartitionSpec as P

EPSILON = 1e-06
NEG_FILL = -1e30
SIDES = (14, 20, 24)
F32 = jnp.float32
BF16 = jnp.bfloat16
MIB = 1 << 20


def dot(left, right, left_dim, right_dim):
    return lax.dot_general(
        left, right, (((left_dim,), (right_dim,)), ((), ())), preferred_element_type=F32
    )


def smem():
    return pl.BlockSpec(memory_space=pltpu.SMEM)


def whole(shape):
    return pl.BlockSpec(shape, lambda *_: (0,) * len(shape), pipeline_mode=pl.Buffered(1))


def array(shape, kind=BF16):
    return jax.ShapeDtypeStruct(shape, kind)


class Line:
    def __init__(self):
        self.last = []

    def call(
        self, name, body, grid, ins, outs, scratch=(), scalars=None, deps=(), limit=60, long=False
    ):
        lead = 0 if scalars is None else 1
        deps = list(deps) + self.last
        first_out = lead + len(ins) + len(deps)

        def kernel(*refs):
            body(*refs[: lead + len(ins)], *refs[first_out:])

        results = pl.pallas_call(
            kernel,
            name=name,
            grid_spec=pltpu.PrefetchScalarGridSpec(
                num_scalar_prefetch=lead,
                grid=grid,
                in_specs=[spec for _, spec in ins] + [anywhere()] * len(deps),
                out_specs=[spec for _, spec in outs],
                scratch_shapes=list(scratch),
            ),
            out_shape=[shape for shape, _ in outs],
            compiler_params=pltpu.CompilerParams(vmem_limit_bytes=limit * MIB),
            cost_estimate=pl.CostEstimate(
                flops=10**13 if long else 1 << 20, bytes_accessed=1 << 20, transcendentals=0
            ),
        )(*([] if scalars is None else [scalars]), *[value for value, _ in ins], *deps)
        self.last = [results[0]]
        return results


def anywhere():
    return pl.BlockSpec(memory_space=pl.ANY)


def lanes_of(ref):
    return ref[...].astype(F32).reshape(1, -1)


def clip(value, low, high):
    return jnp.minimum(jnp.maximum(value, low), high)


def position_table(slots):
    table = np.zeros((3, slots, 128), np.float32)
    index = np.arange(slots)
    for res, side in enumerate(SIDES):
        within = index % (side * side)
        for lane in (0, 64):
            table[res, index, lane + within // side] = 1
            table[res, index, lane + 32 + within % side] = 1
    return table.astype(jnp.bfloat16)


def weight_lanes():
    table = np.zeros((128, 256), np.float32)
    for index in range(32):
        table[index, :128] = index
        table[32 + index, 128:] = index
    return table.astype(jnp.bfloat16)


def for_each_image(info, slots, body):
    for res, side in enumerate(SIDES):
        patches = side * side

        @pl.when(info[0] == res)
        def _(patches=patches):
            for image in range(slots // patches):
                offset = image * patches
                start = offset // 16 * 16
                span = -(-patches // 16) * 16
                body(image, start, span, offset - start, patches)


def inside(shape, axis, offset, patches):
    index = lax.broadcasted_iota(jnp.int32, shape, axis)
    return (index >= offset) & (index < offset + patches)


def live_rows(info):
    side = jnp.where(info[0] == 0, SIDES[0], jnp.where(info[0] == 1, SIDES[1], SIDES[2]))
    return info[1] * side * side


def swap_halves(values, half):
    pieces = []
    lane = lax.broadcasted_iota(jnp.int32, (values.shape[0], 128), 1)
    first = lane % (2 * half) < half
    for at in range(0, values.shape[1], 128):
        piece = values[:, at : at + 128]
        pieces.append(
            jnp.where(first, pltpu.roll(piece, 128 - half, 1), pltpu.roll(piece, half, 1))
        )
    return pieces[0] if len(pieces) == 1 else jnp.concatenate(pieces, axis=1)


def combine_angles(trig, width):
    cos_row, sin_row = trig[:, :width], trig[:, width : 2 * width]
    cos_col, sin_col = trig[:, 2 * width : 3 * width], trig[:, 3 * width :]
    return cos_row * cos_col - sin_row * sin_col, sin_row * cos_col + cos_row * sin_col


ROWS = 384


def fill_angles(table, freq_ref, width):
    index = lax.broadcasted_iota(jnp.int32, (32, width), 0).astype(F32)
    lane = lax.broadcasted_iota(jnp.int32, (32, width), 1)
    sign = jnp.where(lane % 64 < 32, -1.0, 1.0).astype(F32)
    table[...] = jnp.zeros_like(table)
    for kind in range(2):
        angle = index * freq_ref[kind : kind + 1, :]
        for part, value in enumerate((jnp.cos(angle), jnp.sin(angle) * sign)):
            high = value.astype(BF16)
            low = (value - high.astype(F32)).astype(BF16)
            at = (2 * kind + part) * width
            table[32 * kind : 32 * kind + 32, at : at + width] = high
            table[64 + 32 * kind : 96 + 32 * kind, at : at + width] = low


def normed_rows(values):
    shifted = values - jnp.mean(values, axis=1, keepdims=True)
    inverse = lax.rsqrt(jnp.mean(shifted * shifted, axis=1, keepdims=True) + EPSILON)
    return shifted * inverse, inverse


def row_block(index):
    return pl.ds(pl.multiple_of(index * ROWS, ROWS), ROWS)


def column_half(size, which):
    return pl.ds(pl.multiple_of(which * size, size), size)


def each(count, body):
    def step(index, carry):
        body(index)
        return carry

    lax.fori_loop(0, count, step, 0)


class Outbox:
    def __init__(self, sems, first=0):
        self.sems, self.kinds, self.first = sems, [], first

    def kind(self, blocks, ends):
        self.kinds.append((blocks, ends))
        return len(self.kinds) - 1

    def copy(self, kind, block):
        source, target = self.kinds[kind][1](block)
        return pltpu.make_async_copy(source, target, self.sems.at[self.first + kind, block])

    def send(self, kind, block):
        self.copy(kind, block).start()

    def wait(self, kind):
        for block in range(self.kinds[kind][0]):
            self.copy(kind, block).wait()


def layer_kernel(
    scal, g1_ref, b1_ref, qb_ref, freq_ref, ob_ref, g2_ref, b2_ref, ub_ref,
    pos_hbm, tok_hbm, w_hbm, ow_hbm, uw_hbm, dw_hbm, cot_hbm,
    zero_ref, sums_ref, upsum_ref, dsent_hbm, down_hbm, usent_hbm, up_hbm, in_hbm, stat_hbm, tab_hbm,
    qkv_hbm, mid_hbm, act_hbm, branch_hbm, attg_hbm, grad_hbm,
    pos_s, tok_s, w_s, ow_s, uw_s, cot_s, tab_s, in_s, qkv_s, stat_s, att_s, mid_s, sec_s, act_s, slope_s,
    grad_s, tok_sem, load_sem, store_sem, grad_sem,
):
    slots, width = att_s.shape
    hidden = act_s.shape[1]
    blocks, pairs, tiles = slots // ROWS, width // 128, hidden // width
    half = width // 2

    def tokens(block):
        rows = row_block(block)
        return pltpu.make_async_copy(tok_hbm.at[rows], tok_s.at[rows], tok_sem.at[block])

    def load(at):
        source, target = (
            [(w_hbm.at[:, part * width : (part + 1) * width], w_s.at[part]) for part in range(3)]
            + [(pos_hbm.at[scal[0]], pos_s), (ow_hbm, ow_s), (uw_hbm, uw_s), (cot_hbm, cot_s)]
            + [(dw_hbm.at[part * width : (part + 1) * width], w_s.at[part]) for part in range(tiles)]
        )[at]
        return pltpu.make_async_copy(source, target, load_sem.at[at])

    out = Outbox(store_sem)

    def by_rows(source, target):
        return out.kind(blocks, lambda block: (source.at[row_block(block)], target.at[row_block(block)]))

    send_in, send_act, send_mid = (
        by_rows(source, target) for source, target in ((in_s, in_hbm), (act_s, act_hbm), (mid_s, mid_hbm))
    )
    send_qkv = out.kind(
        blocks, lambda block: (qkv_s.at[:, row_block(block)], qkv_hbm.at[:, row_block(block)])
    )
    send_tab = out.kind(1, lambda block: (tab_s, tab_hbm))
    send_stat = out.kind(1, lambda block: (stat_s, stat_hbm))
    for ref in (zero_ref, sums_ref, upsum_ref):
        ref[...] = jnp.zeros_like(ref)
    tokens(0).start()
    for at in range(4):
        load(at).start()
    for block in range(1, blocks):
        tokens(block).start()
    for at in range(4, 7):
        load(at).start()
    fill_angles(tab_s, freq_ref, width)
    out.send(send_tab, 0)
    for at in range(4):
        load(at).wait()

    def project(block):
        tokens(block).wait()
        rows = row_block(block)
        normed, _ = normed_rows(tok_s[rows, :].astype(F32))
        first_in = (normed * lanes_of(g1_ref) + lanes_of(b1_ref)).astype(BF16)
        in_s[rows, :] = first_in
        cosine, sine = combine_angles(dot(pos_s[rows, :], tab_s[...], 1, 0), width)
        for part in range(3):
            bias = qb_ref[part * width : (part + 1) * width].astype(F32).reshape(1, -1)
            projected = dot(first_in, w_s[part], 1, 0) + bias
            if part < 2:
                projected = projected * cosine + swap_halves(projected, 32) * sine
            if part == 0:
                projected = projected * 0.125
            projected = projected.astype(BF16)
            for pair in range(pairs):
                qkv_s[part * pairs + pair, rows, :] = projected[:, pair * 128 : pair * 128 + 128]
        out.send(send_in, block)
        out.send(send_qkv, block)

    each(blocks, project)

    def attend(pair):
        cols = column_half(128, pair)
        q_ref, k_ref, v_ref = (qkv_s.at[part * pairs + pair] for part in range(3))
        att_s[:, cols] = v_ref[...]
        live = live_rows(scal)

        def image_step(image, start, span, offset, patches):
            rows = slice(start, start + span)
            exact = span == patches
            turned = v_ref[rows, :].T
            mixed = []
            for head in range(2):
                lanes = slice(head * 64, head * 64 + 64)
                scores = dot(k_ref[rows, lanes], q_ref[rows, lanes], 1, 1)
                if not exact:
                    scores = jnp.where(inside(scores.shape, 0, offset, patches), scores, NEG_FILL)
                top = jnp.max(scores, axis=0, keepdims=True)
                powers = jnp.exp(scores - top)
                mass = jnp.sum(powers, axis=0, keepdims=True)
                mixed.append(dot(turned[lanes], powers.astype(BF16), 1, 0) * (1.0 / mass))
                stat_s[pair, image, head : head + 1, 0:span] = top + jnp.log(mass)
            result = jnp.concatenate(mixed, axis=0).T
            keep = lax.broadcasted_iota(jnp.int32, result.shape, 0) < live - start
            if not exact:
                keep = keep & inside(result.shape, 0, offset, patches)
            result = jnp.where(keep, result, att_s[rows, cols].astype(F32))
            att_s[rows, cols] = result.astype(BF16)

        for_each_image(scal, slots, image_step)

    for at in range(7, 7 + tiles):
        load(at).start()
    each(pairs, attend)
    out.send(send_stat, 0)
    load(4).wait()
    load(5).wait()

    def feed(block):
        rows = row_block(block)
        middle = tok_s[rows, :].astype(F32) + (dot(att_s[rows, :], ow_s[...], 1, 0) + lanes_of(ob_ref))
        mid_s[rows, :] = middle
        normed, _ = normed_rows(middle)
        second_in = (normed * lanes_of(g2_ref) + lanes_of(b2_ref)).astype(BF16)
        sec_s[rows, :] = second_in
        scale = math.sqrt(2.0 / math.pi)
        for at in range(0, hidden, 768):
            cols = slice(at, at + 768)
            pre = dot(second_in, uw_s[:, cols], 1, 0) + ub_ref[cols].astype(F32).reshape(1, -1)
            square = pre * pre
            bent = jnp.tanh(pre * (scale + (scale * 0.044715) * square))
            gate = 0.5 + 0.5 * bent
            act_s[rows, cols] = (pre * gate).astype(BF16)
            lean = pre * (scale + (3.0 * scale * 0.044715) * square)
            slope_s[rows, cols] = (gate * (1.0 + (1.0 - bent) * lean)).astype(BF16)
        for kind in (send_act, send_mid):
            out.send(kind, block)

    each(blocks, feed)
    load(6).wait()
    cot_s[...] = live_cotangent(scal, cot_s, 0).astype(BF16)

    def grad_copies(tile, slot):
        rows = pl.ds(pl.multiple_of(tile * width, width), width)
        return [
            pltpu.make_async_copy(
                grad_s.at[slot, :, column_half(half, which)], target.at[rows], grad_sem.at[slot, at])
            for at, (which, target) in enumerate(((1 - scal[2], dsent_hbm), (scal[2], down_hbm)))
        ]

    def down_grad(tile):
        slot = lax.rem(tile, 2)

        @pl.when(tile >= 2)
        def _():
            for copy in grad_copies(tile - 2, slot):
                copy.wait()

        grad_s[slot] = dot(act_s[:, column_half(width, tile)], cot_s[...], 0, 0)
        for copy in grad_copies(tile, slot):
            copy.start()

    each(tiles, down_grad)
    for kind in (send_in, send_mid):
        out.wait(kind)
    for at in range(7, 7 + tiles):
        load(at).wait()
    branch_s, attg_s = in_s, tok_s
    late = Outbox(store_sem, len(out.kinds))
    late_kinds = [
        late.kind(blocks, lambda block, source=source, target=target: (
            source.at[row_block(block)], target.at[row_block(block)]))
        for source, target in ((branch_s, branch_hbm), (attg_s, attg_hbm), (mid_s, grad_hbm))
    ]

    def back_rows(block):
        rows = row_block(block)
        up_low = cot_s[rows, :]
        upstream = up_low.astype(F32)
        for part in range(tiles):
            cols = slice(part * width, (part + 1) * width)
            act_grad = dot(up_low, w_s[part], 1, 1)
            hidden_low = (slope_s[rows, cols].astype(F32) * act_grad).astype(BF16)
            slope_s[rows, cols] = hidden_low
            upsum_ref[0:1, cols] += jnp.sum(hidden_low.astype(F32), axis=0, keepdims=True)
        back = dot(slope_s[rows, :], uw_s[...], 1, 1)
        normed, inverse = normed_rows(mid_s[rows, :])
        scaled = back * lanes_of(g2_ref)
        inner = (
            scaled
            - jnp.mean(scaled, axis=1, keepdims=True)
            - normed * jnp.mean(scaled * normed, axis=1, keepdims=True)
        )
        middle_grad = upstream + inverse * inner
        mid_s[rows, :] = middle_grad
        branch = middle_grad.astype(BF16)
        branch_s[rows, :] = branch
        attg_s[rows, :] = dot(branch, ow_s[...], 1, 1).astype(BF16)
        sums_ref[0:1, :] += jnp.sum(upstream, axis=0, keepdims=True)
        sums_ref[1:2, :] += jnp.sum(back * normed, axis=0, keepdims=True)
        sums_ref[2:3, :] += jnp.sum(back, axis=0, keepdims=True)
        sums_ref[3:4, :] += jnp.sum(branch.astype(F32), axis=0, keepdims=True)
        for kind in late_kinds:
            late.send(kind, block)

    each(blocks, back_rows)

    def up_copy(tile, slot, wait):
        for first, target in ((0, usent_hbm), (tiles // 2, up_hbm)):

            @pl.when((tile >= first) & (tile < first + tiles // 2))
            def _(first=first, target=target):
                copy = pltpu.make_async_copy(
                    grad_s.at[slot], target.at[:, column_half(width, tile - first)], grad_sem.at[slot, 0]
                )
                copy.wait() if wait else copy.start()

    def up_grad(tile):
        slot = lax.rem(tile, 2)

        @pl.when(tile < 2)
        def _():
            for copy in grad_copies(tile + tiles - 2, slot):
                copy.wait()

        @pl.when(tile >= 2)
        def _():
            up_copy(tile - 2, slot, True)

        side = jnp.where(tile < tiles // 2, 1 - scal[2], scal[2])
        place = side * (tiles // 2) + lax.rem(tile, tiles // 2)
        grad_s[slot] = dot(sec_s[...], slope_s[:, column_half(width, place)], 0, 0)
        up_copy(tile, slot, False)

    each(tiles, up_grad)
    slot = tiles % 2
    up_copy(jnp.int32(tiles - 2), slot, True)
    grad_s[slot] = dot(att_s[...], branch_s[...], 0, 0)
    copies = [
        pltpu.make_async_copy(
            grad_s.at[slot, :, column_half(half, which)],
            target.at[:, hidden // 2 : hidden // 2 + half], grad_sem.at[slot, at])
        for at, (which, target) in enumerate(((1 - scal[2], usent_hbm), (scal[2], up_hbm)))
    ]
    for copy in copies:
        copy.start()
    up_copy(jnp.int32(tiles - 1), (tiles - 1) % 2, True)
    for copy in copies:
        copy.wait()
    for kind in (send_act, send_qkv, send_tab, send_stat):
        out.wait(kind)
    for kind in late_kinds:
        late.wait(kind)


def zeros_kernel(out_ref):
    out_ref[...] = jnp.zeros_like(out_ref)


def live_cotangent(info, cot_ref, first_row):
    row = lax.broadcasted_iota(jnp.int32, cot_ref.shape, 0) + first_row
    return jnp.where(row < live_rows(info), cot_ref[...].astype(F32), 0.0)


def attend_back_kernel(
    info, pos_ref, t0, t1, t2, t3, lanes_ref, in_ref, q_ref, k_ref, v_ref, up_ref, stat_ref,
    *rest,
):
    dw_refs, (gq_ref, gk_ref, gv_ref, sums_ref, dq_acc, dk_acc, dv_acc) = rest[:-7], rest[-7:]
    @pl.when(info[0] < 2)
    def _():
        for acc in (dq_acc, dk_acc, dv_acc):
            acc[...] = jnp.zeros_like(acc)

    def image_step(image, start, span, offset, patches):
        rows = slice(start, start + span)
        exact = span == patches
        for head in range(2):
            lanes = slice(head * 64, head * 64 + 64)
            query, key = q_ref[rows, lanes], k_ref[rows, lanes]
            value, upstream = v_ref[rows, lanes], up_ref[rows, lanes]
            probs = jnp.exp(dot(key, query, 1, 1) - stat_ref[image, head : head + 1, 0:span])
            if not exact:
                keep = inside(probs.shape, 0, offset, patches)
                keep = keep & inside(probs.shape, 1, offset, patches)
                probs = jnp.where(keep, probs, 0.0)
            prob_grad = dot(value, upstream, 1, 1)
            inner = jnp.sum(probs * prob_grad, axis=0, keepdims=True)
            score_low = (probs * (prob_grad - inner)).astype(BF16)
            value_grad = dot(probs.astype(BF16), upstream, 1, 0)
            key_grad = dot(score_low, query, 1, 0)
            query_grad = dot(key.T, score_low, 1, 0).T
            if exact:
                dq_acc[rows, lanes] = query_grad
                dk_acc[rows, lanes] = key_grad
                dv_acc[rows, lanes] = value_grad
            else:
                dq_acc[rows, lanes] += query_grad
                dk_acc[rows, lanes] += key_grad
                dv_acc[rows, lanes] += value_grad

    for_each_image(info, q_ref.shape[0], image_step)
    pos = pos_ref[...]
    table = jnp.concatenate([t0[...], t1[...], t2[...], t3[...]], axis=1)
    cosine, sine = combine_angles(dot(pos, table, 1, 0), 128)
    places = dot(pos, lanes_ref[...], 1, 0)
    lane = lax.broadcasted_iota(jnp.int32, (1, 128), 1)
    sign = jnp.where(lane % 64 < 32, 1.0, -1.0)
    angle_grad = None
    sums_ref[...] = jnp.zeros_like(sums_ref)
    for row, (acc, low_ref, out_ref, up, down) in enumerate(
        ((dq_acc, q_ref, gq_ref, 0.125, 8.0), (dk_acc, k_ref, gk_ref, 1.0, 1.0))
    ):
        grad = acc[...] * up
        swapped = swap_halves(grad, 32)
        term = swapped * (low_ref[...].astype(F32) * down)
        angle_grad = term if angle_grad is None else angle_grad + term
        pre = (grad * cosine - swapped * sine).astype(BF16)
        out_ref[...] = pre
        sums_ref[2 + row : 3 + row, :] = jnp.sum(pre.astype(F32), axis=0, keepdims=True)
    value_low = dv_acc[...].astype(BF16)
    gv_ref[...] = value_low
    sums_ref[4:5, :] = jnp.sum(value_low.astype(F32), axis=0, keepdims=True)
    for row in range(2):
        place = places[:, row * 128 : row * 128 + 128]
        sums_ref[row : row + 1, :] = sign * jnp.sum(place * angle_grad, axis=0, keepdims=True)
    grads = jnp.concatenate([gq_ref[...], gk_ref[...], gv_ref[...]], axis=1)
    weight_grad = dot(in_ref[...], grads, 0, 0)
    if len(dw_refs) == 1:
        dw_refs[0][...] = weight_grad
    else:
        for at, ref in enumerate(dw_refs):

            @pl.when(pl.program_id(0) == at)
            def _(ref=ref):
                ref[...] = weight_grad


def input_kernel(
    scal, tok_ref, gain_ref, grad_ref, w_ref, down_ref, up_ref, other_ref, own_ref, *refs
):
    pieces, (out_ref, sums_ref, down_out, up_out, pair_out) = refs[:6], refs[6:]
    width, half = tok_ref.shape[1], pieces[0].shape[1]

    @pl.when(pl.program_id(0) == 0)
    def _():
        sums_ref[...] = jnp.zeros_like(sums_ref)
        down_out[...] = down_ref[...]
        up_out[...] = up_ref[...]
        count = own_ref.shape[0]
        for pair in range(count):
            pair_out[count * (1 - scal[2]) + pair] = other_ref[pair]
            pair_out[count * scal[2] + pair] = own_ref[pair]

    back = None
    for side, which in enumerate((1 - scal[2], scal[2])):
        for part in range(3):
            cols = pl.ds(pl.multiple_of(part * width + which * half, half), half)
            term = dot(pieces[3 * side + part][...], w_ref[:, cols], 1, 1)
            back = term if back is None else back + term
    values = tok_ref[...].astype(F32)
    shifted = values - jnp.mean(values, axis=1, keepdims=True)
    inverse = lax.rsqrt(jnp.mean(shifted * shifted, axis=1, keepdims=True) + EPSILON)
    normed = shifted * inverse
    scaled = back * lanes_of(gain_ref)
    inner = (
        scaled
        - jnp.mean(scaled, axis=1, keepdims=True)
        - normed * jnp.mean(scaled * normed, axis=1, keepdims=True)
    )
    out_ref[...] = (grad_ref[...] + inverse * inner).astype(BF16)
    sums_ref[0:1, :] += jnp.sum(back * normed, axis=0, keepdims=True)
    sums_ref[1:2, :] += jnp.sum(back, axis=0, keepdims=True)


def output_kernel(act_ref, dw_ref, db_ref, mid_ref, out_ref):
    out_ref[...] = (
        mid_ref[...] + (dot(act_ref[...], dw_ref[...], 1, 0) + lanes_of(db_ref))
    ).astype(BF16)


def weight_of(counted, totals, slots):
    return F32(slots) / (3.0 * jnp.sum(jnp.where(counted > 0, totals, 0.0)))


def cross_part(cols):
    return (cols // 2 + 127) // 128 * 128


def combine(line, name, scal, counts, slots, own, got, shard, split, long=False):
    height, total = own.shape
    tile = max(2 * shard, height // 4)
    if shard % 16:
        split = None

    def kernel(scal_ref, *refs):
        first = len(counts) + 1
        counted, own_ref, got_refs, outs = (
            refs[: first - 1], refs[first - 1], refs[first : first + len(got)], refs[first + len(got) :]
        )
        totals = sum_of([ref[0:1] for ref in counted[2:]])
        mine = weight_of(counted[0][0:1], totals, slots)
        theirs = weight_of(counted[1][0:1], totals, slots)
        target = outs[-1] if split else outs[0]
        at = 0
        for got_ref in got_refs:
            cols = slice(at, at + got_ref.shape[1])
            target[:, cols] = own_ref[:, cols] * mine + got_ref[...] * theirs
            at += got_ref.shape[1]
        if split == "cross":
            first = cross_part(total)
            for at in range(tile // shard):
                for out, x_bit in ((outs[0], scal_ref[3]), (outs[1], 1 - scal_ref[3])):
                    rows = pl.ds(pl.multiple_of(at * shard + x_bit * (shard // 2), 8), shard // 2)
                    out[at] = target[rows, :first]
            for at in range(tile // shard // 2):
                for out, y_bit in ((outs[2], scal_ref[4]), (outs[3], 1 - scal_ref[4])):
                    rows = pl.ds(pl.multiple_of((2 * at + y_bit) * shard, 8), shard)
                    out[at] = target[rows, first:]
            return
        if split:
            stride = split // 2
            for at in range(tile // shard // stride):
                sides = (scal_ref[4], 1 - scal_ref[4]) if split == 4 else (0,)
                for index, (x_bit, y_bit) in enumerate(
                    ((x, y) for y in sides for x in (scal_ref[3], 1 - scal_ref[3]))
                ):
                    rows = (stride * at + y_bit) * shard + x_bit * (shard // 2)
                    outs[index][at] = target[pl.ds(pl.multiple_of(rows, 8), shard // 2), :]

    block = pl.BlockSpec((tile, total), lambda i, scal: (i, 0))
    got = list(got) if isinstance(got, (list, tuple)) else [got]
    ins = [(count, whole(count.shape)) for count in counts] + [(own, block)]
    ins += [(one, pl.BlockSpec((tile, one.shape[1]), lambda i, scal: (i, 0))) for one in got]
    if split is None:
        return line.call(
            name, kernel, (height // tile,), ins, [(array((height, total), F32), block)], scalars=scal,
            long=long,
        )[0]
    count = height // shard

    if split == "cross":
        first = cross_part(total)
        outs = [
            (array((count // shards, high, cols), F32), pl.BlockSpec(
                (tile // shard // shards, high, cols), lambda i, scal: (i, 0, 0)))
            for shards, high, cols in ((1, shard // 2, first), (2, shard, total - first)) for _ in range(2)
        ]
        return line.call(
            name, kernel, (height // tile,), ins, outs, [pltpu.VMEM((tile, total), F32)], scalars=scal
        )
    shards = split // 2
    outs = [(array((count // shards, shard // 2, total), F32), pl.BlockSpec(
        (tile // shard // shards, shard // 2, total), lambda i, scal: (i, 0, 0)))] * split
    return line.call(
        name, kernel, (height // tile,), ins, outs, [pltpu.VMEM((tile, total), F32)], scalars=scal
    )


class Place:
    def __init__(self, n_group, n_dp):
        self.n_group, self.n_dp = n_group, n_dp
        group_at, self.dp_at = lax.axis_index("group"), lax.axis_index("dp")
        self.core, self.x = lax.rem(group_at, 2), lax.div(group_at, 2)
        self.dp_bits = n_dp.bit_length() - 1
        self.dp = [lax.rem(lax.div(self.dp_at, 1 << bit), 2) for bit in range(self.dp_bits)]

    def group(self, value, mask):
        return lax.ppermute(value, "group", [(at, at ^ mask) for at in range(self.n_group)])

    def along(self, value, mask):
        return lax.ppermute(value, "dp", [(at, at ^ mask) for at in range(self.n_dp)])

    def across(self, value, group_mask, dp_mask):
        pairs = [
            (at * self.n_dp + dp, (at ^ group_mask) * self.n_dp + (dp ^ dp_mask))
            for at in range(self.n_group) for dp in range(self.n_dp)
        ]
        return lax.ppermute(value, ("group", "dp"), pairs)

    def stages(self):
        for bit in range(0, self.dp_bits, 2):
            masks = [1 << bit] if bit + 1 == self.dp_bits else [1 << bit, 2 << bit, 3 << bit]
            yield lambda v, masks=masks: [self.along(v, mask) for mask in masks]
        yield lambda v: [self.group(v, mask) for mask in (1, 2, 3)]


def sum_of(terms):
    result = terms[0]
    for term in terms[1:]:
        result = result + term
    return result


class Scatter:
    def __init__(self, place, kept, rows, cols, joint, widths=()):
        self.place, self.rows, self.widths = place, rows // place.n_dp, list(widths)
        self.first, self.terms, self.at_once = None, [None], joint is True
        self.bit = 0 if joint is False else 1
        if joint is None and not isinstance(kept, (list, tuple)):
            tall, fold = self.rows, 1
            while tall % 16:
                tall, fold = 2 * tall, 2 * fold
            first = cross_part(cols)
            view = kept.reshape(place.n_dp, self.rows, cols)
            one = view[..., :first].reshape(place.n_dp, 2, tall // 2, first // fold)
            two = view[..., first:].reshape(place.n_dp // 2, 2, tall, (cols - first) // fold)
            self.first = first // fold
            kept = [
                lax.dynamic_index_in_dim(value, at, 1, keepdims=False)
                for value, bit in ((one, place.x), (two, place.dp[0])) for at in (bit, 1 - bit)
            ]
        elif not isinstance(kept, (list, tuple)):
            tall, wide = self.rows, cols
            while tall % 16:
                tall, wide = 2 * tall, wide // 2
            shards = place.n_dp // 2 if joint else place.n_dp
            view = kept.reshape(shards, -1, 2, tall // 2, wide)

            def part(y, x):
                found = lax.dynamic_index_in_dim(view, y, 1, keepdims=False)
                return lax.dynamic_index_in_dim(found, x, 1, keepdims=False)

            kept = [
                part(y, x)
                for y in ((place.dp[0], 1 - place.dp[0]) if joint else (0,))
                for x in (place.x, 1 - place.x)
            ]
        self.cross = None
        if joint is None:
            self.cross = [kept[0], place.group(kept[1], 2), kept[2], place.along(kept[3], 1)]
            return
        masks = ((0, 0), (2, 0), (0, 1), (2, 1))
        self.terms = [[kept[0]]] + [
            [place.across(piece, *mask)] for piece, mask in zip(kept[1:], masks[1:])
        ]

    def job(self):
        place, bit = self.place, self.bit
        if self.cross is not None:
            (count, half, first), (_, shard, second) = self.cross[0].shape, self.cross[2].shape
            lead = count // 2
            ins = [(one.reshape(lead, 2, half, first), None) for one in self.cross[:2]]
            ins += [(one.reshape(lead, 2, half, second), None) for one in self.cross[2:]]

            def cross(scal, ins, outs):
                mine, over_y, over_x = outs
                y, x = scal[4], scal[3]
                mine[:, :, :first] = ins[0][:, y] + ins[1][:, y]
                mine[:, :, first:] = ins[2][:, x] + ins[3][:, x]
                over_y[...] = ins[0][:, 1 - y] + ins[1][:, 1 - y]
                over_x[...] = ins[2][:, 1 - x] + ins[3][:, 1 - x]

            def crossed(mine, over_y, over_x):
                self.terms = [[mine], [place.along(over_y, 1), place.group(over_x, 2)]]
                self.cross = None

            return ins, [
                (lead, half, first + second), (lead, half, first), (lead, half, second)
            ], cross, crossed
        lead, half, cols = self.terms[0][0].shape
        counts = [len(term) for term in self.terms]

        def read(refs, at):
            refs, found = list(refs), []
            for count in counts:
                rows = [ref[:, at] for ref in (refs.pop(0) for _ in range(count))]
                by_rows = rows[0].shape[-1] == cols
                found.append(rows[0] if count == 1 else jnp.concatenate(rows, axis=1 if by_rows else 2))
            return sum_of(found)

        if bit < place.dp_bits:
            wide, cut = self.widths.pop(0) if self.widths else (2, 1)
            wide, cut = min(wide, place.dp_bits - bit), cut if half % (8 * cut) == 0 else 1
            size = 1 << wide
            ins = [
                (one.reshape((lead // size, size) + one.shape[1:]), None)
                for term in self.terms for one in term
            ]

            def body(scal, ins, outs):
                for mask in range(size):
                    at = scal[4 + bit] if not mask % 2 else 1 - scal[4 + bit]
                    if wide == 2:
                        at = at + 2 * (scal[5 + bit] if mask < 2 else 1 - scal[5 + bit])
                    value = read(ins, at)
                    if mask == 0:
                        outs[0][...] = value
                    for part in range(cut if mask else 0):
                        rows = slice(part * half // cut, (part + 1) * half // cut)
                        outs[1 + (mask - 1) * cut + part][...] = value[:, rows]

            def then(mine, *sent):
                self.terms = [[mine]] + [
                    [place.along(value, mask << bit) for value in sent[(mask - 1) * cut : mask * cut]]
                    for mask in range(1, size)
                ]

            self.bit += wide
            shapes = [(lead // size, half, cols)]
            shapes += [(lead // size, half // cut, cols)] * ((size - 1) * cut)
            return ins, shapes, body, then
        ins = [(one.reshape((1, 1) + one.shape[1:]), None) for term in self.terms for one in term]
        self.terms = []

        def body(scal, ins, outs):
            mine = read(ins, 0)[0]
            outs[0][...] = mine
            outs[1][...] = jnp.broadcast_to(jnp.sum(mine * mine), outs[1].shape)

        def then(mine, square):
            self.square = square
            over_x = place.group(mine, 2)
            last = place.group(mine, 3) if self.at_once else place.group(over_x, 1)
            self.parts = [mine, place.group(mine, 1), over_x, last]

        return ins, [(half, cols), (8, 128)], body, then

    def blocks(self):
        place = self.place
        mine, core, x, both = self.parts
        found = []
        for at in (0, 1):
            here = jnp.where(place.core == at, mine, core)
            there = jnp.where(place.core == at, x, both)
            low, high = jnp.where(place.x == 0, here, there), jnp.where(place.x == 0, there, here)
            both_halves = jnp.concatenate([low, high])
            if both_halves.shape[0] != self.rows and self.first is not None:
                both_halves = [both_halves[:, : self.first], both_halves[:, self.first :]]
                found.append(jnp.concatenate([one.reshape(self.rows, -1) for one in both_halves], axis=1))
                continue
            found.append(both_halves.reshape(self.rows, -1))
        return found


class Scattered:
    def __init__(self, place, kept):
        self.place, self.got = place, None
        groups = [list(range(bit, place.n_dp, 2)) for bit in range(2)]
        self.mine = lax.psum_scatter(
            kept, "dp", scatter_dimension=0, tiled=True, axis_index_groups=groups
        )
        self.stage = 0

    def job(self):
        place, stage = self.place, self.stage
        self.stage += 1
        if stage == 0:
            rows, cols = self.mine.shape[0] // 2, self.mine.shape[1]

            def split(scal, ins, outs):
                for out, bit in zip(outs, (scal[4], 1 - scal[4])):
                    out[...] = ins[0][pl.ds(pl.multiple_of(bit * rows, 8), rows), :]

            def start(mine, sent):
                self.mine, self.got = mine, place.along(sent, 1)

            return [(self.mine, None)], [(rows, cols)] * 2, split, start
        ins = [(self.mine, None), (self.got, None)]

        def body(scal, ins, outs):
            mine = ins[0][...] + ins[1][...]
            outs[0][...] = mine
            outs[1][...] = jnp.broadcast_to(jnp.sum(mine * mine), outs[1].shape)

        def then(mine, square):
            self.mine, self.square = mine, square
            if stage == 1:
                self.got = place.group(mine, 2)
            else:
                self.theirs = place.group(mine, 1)

        return ins, [self.mine.shape, (8, 128)], body, then

    def blocks(self):
        first = self.place.core == 0
        return [jnp.where(first, self.mine, self.theirs), jnp.where(first, self.theirs, self.mine)]


def run_jobs(line, name, scal, jobs, long=False):
    ins = [
        (value, spec if spec is not None else whole(value.shape))
        for job in jobs for value, spec in job[0]
    ]
    outs = [
        (array(shape, F32), pl.BlockSpec(shape, functools.partial(lambda rank, *_: (0,) * rank, len(shape))))
        for job in jobs for shape in job[1]
    ]

    def kernel(scal_ref, *refs):
        at_in, at_out = 0, len(ins)
        for job_ins, job_outs, body, _ in jobs:
            body(
                scal_ref, refs[at_in : at_in + len(job_ins)], refs[at_out : at_out + len(job_outs)]
            )
            at_in += len(job_ins)
            at_out += len(job_outs)

    results = line.call(name, kernel, (1,), ins, outs, scalars=scal, long=long)
    at = 0
    for _, job_outs, _, then in jobs:
        then(*results[at : at + len(job_outs)])
        at += len(job_outs)


def local(
    n_group, n_dp, tokens, cotangent, norm1_gain, norm1_bias, qkv_weight, qkv_bias, rotary_freqs,
    out_weight, out_bias, norm2_gain, norm2_bias, up_weight, up_bias, down_weight, down_bias,
    group_res, images,
):
    slots, width = tokens.shape
    heads = rotary_freqs.shape[1]
    hidden = up_weight.shape[1]
    pairs = heads // 2
    blocks = slots // ROWS
    place = Place(n_group, n_dp)
    line = Line()
    scal = jnp.concatenate(
        [group_res, images, jnp.stack([place.core, place.x] + place.dp).astype(jnp.int32)]
    ).astype(jnp.int32)

    def rows_of(cols, first=0):
        return pl.BlockSpec((ROWS, cols), lambda i, *_: (clip(i - first, 0, blocks - 1), 0))

    def param(vector):
        return (vector, whole(vector.shape))

    def kept_sum(rows, cols):
        return (array((rows, cols), F32), pl.BlockSpec((rows, cols), lambda *_: (0, 0)))

    def in_hbm(shape, kind=BF16):
        return (array(shape, kind), anywhere())

    side = jnp.where(group_res[0] == 0, SIDES[0], jnp.where(group_res[0] == 1, SIDES[1], SIDES[2]))
    lane = lax.broadcasted_iota(jnp.int32, (8, 128), 1)
    patches = (images[0] * side * side).astype(F32)
    totals = jnp.where(lane == group_res[0], patches, 0.0)
    here = totals
    got = [place.group(totals, mask) for mask in (1, 2, 3)]
    beside = got[0]
    spread = jnp.broadcast_to(sum_of([totals] + got)[:1], (96 * n_dp, 128))
    totals = lax.psum_scatter(spread, "dp", scatter_dimension=0, tiled=True)[:8]

    half_freqs = jnp.concatenate([rotary_freqs, rotary_freqs], axis=-1).reshape(2, width)
    pos = jnp.asarray(position_table(slots))
    stat_shape = (slots // SIDES[0] ** 2, 8, -(-(SIDES[2] ** 2) // 128) * 128)
    tiles = hidden // width
    half = width // 2

    def vmem(*shape, kind=BF16):
        return pltpu.VMEM(shape, kind)

    (
        zero, down_sums, up_sums, down_sent, down_own, up_sent, up_own, first_in, stats, trig_table, qkv,
        middle, act, branch, att_grad, mid_grad,
    ) = line.call(
        "layer", layer_kernel, (1,),
        [
            param(norm1_gain), param(norm1_bias), param(qkv_bias), param(half_freqs), param(out_bias),
            param(norm2_gain), param(norm2_bias), param(up_bias), (pos, anywhere()), (tokens, anywhere()),
            (qkv_weight, anywhere()), (out_weight, anywhere()), (up_weight, anywhere()),
            (down_weight, anywhere()), (cotangent, anywhere()),
        ],
        [
            kept_sum(8, 128), kept_sum(8, width), kept_sum(8, hidden),
            in_hbm((hidden, half), F32), in_hbm((hidden, half), F32),
            in_hbm((width, hidden // 2 + half), F32), in_hbm((width, hidden // 2 + half), F32),
            in_hbm((slots, width)), in_hbm((pairs,) + stat_shape, F32), in_hbm((128, 4 * width)),
            in_hbm((3 * pairs, slots, 128)), in_hbm((slots, width), F32), in_hbm((slots, hidden)),
            in_hbm((slots, width)), in_hbm((slots, width)), in_hbm((slots, width), F32),
        ],
        [
            vmem(slots, 128), vmem(slots, width), vmem(tiles, width, width), vmem(width, width),
            vmem(width, hidden), vmem(slots, width), vmem(128, 4 * width), vmem(slots, width),
            vmem(3 * pairs, slots, 128), vmem(pairs, *stat_shape, kind=F32), vmem(slots, width),
            vmem(slots, width, kind=F32), vmem(slots, width), vmem(slots, hidden), vmem(slots, hidden),
            vmem(2, width, width, kind=F32),
            pltpu.SemaphoreType.DMA((blocks,)), pltpu.SemaphoreType.DMA((7 + tiles,)),
            pltpu.SemaphoreType.DMA((9, blocks)), pltpu.SemaphoreType.DMA((2, 2)),
        ],
        scalars=scal, limit=63, deps=[spread],
    )
    down_got = place.group(down_sent, 1)
    up_got = place.group(up_sent, 1)
    counts = [here, beside, totals + zero]
    line.call("mark", zeros_kernel, (1,), [], [kept_sum(8, 128)], long=True)
    scale = weight_of(here[0], counts[2][0], slots)
    shard = width // n_dp

    def reduce(name, own, got, rows, split, long=False):
        return combine(line, name, scal, counts, slots, own, got, rows, split, long)

    lanes_table = jnp.asarray(weight_lanes())

    def attend_back(own):
        count = pairs // 2

        def at(i, scal):
            return count * (scal[2] if own else 1 - scal[2]) + i

        def table_block(part):
            return pl.BlockSpec((128, 128), lambda i, scal: (0, part * pairs + at(i, scal)))

        def qkv_block(part):
            return pl.BlockSpec((None, slots, 128), lambda i, scal: (part * pairs + at(i, scal), 0, 0))

        out = (array((slots, count * 128)), pl.BlockSpec((slots, 128), lambda i, scal: (0, i)))
        return line.call(
            "attend_back", attend_back_kernel, (count,),
            [(pos, pl.BlockSpec((None, slots, 128), lambda i, scal: (scal[0], 0, 0)))]
            + [(trig_table, table_block(part)) for part in range(4)]
            + [param(lanes_table), param(first_in)]
            + [(qkv, qkv_block(part)) for part in range(3)]
            + [
                (att_grad, pl.BlockSpec((slots, 128), lambda i, scal: (0, at(i, scal)))),
                (stats, pl.BlockSpec(
                    (None,) + stat_shape, lambda i, scal: (at(i, scal), 0, 0, 0))),
            ],
            (
                [(array((width, count * 384), F32), pl.BlockSpec((width, 384), lambda i, scal: (0, i)))]
                if own else [kept_sum(width, 384)] * count
            )
            + [out] * 3
            + [(array((count, 8, 128), F32), pl.BlockSpec((None, 8, 128), lambda i, scal: (i, 0, 0)))],
            scratch=[pltpu.VMEM((slots, 128), F32)] * 3,
            scalars=scal,
        )

    def jobs(name, *chunks, long=False):
        run_jobs(line, name, scal, [chunk.job() for chunk in chunks], long)

    *other_grads, other_sums = attend_back(False)
    qkv_got = [place.group(other_grads.pop(0), 1) for _ in range(pairs // 2)]
    up = Scatter(
        place, reduce("up_sum", up_own, up_got, shard, "cross"), width, up_own.shape[1], None,
        ((1, 1), (1, 1)),
    )
    down = Scattered(place, reduce("down_sum", down_own, down_got, hidden // n_dp, None))
    qkv_own, *own_grads, own_sums = attend_back(True)
    jobs("up0", up)
    qkv_grad = Scatter(
        place, reduce("qkv_sum", qkv_own, qkv_got, shard, 4), width, qkv_own.shape[1], True
    )
    input_grad, sums_one, down_sums, up_sums, pair_sums = line.call(
        "input_grad", input_kernel, (blocks,),
        [
            (tokens, rows_of(width)), param(norm1_gain), (mid_grad, rows_of(width)),
            param(qkv_weight), param(down_sums), param(up_sums), param(other_sums), param(own_sums),
        ] + [(piece, rows_of(piece.shape[1])) for piece in other_grads + own_grads],
        [
            (array((slots, width)), rows_of(width)), kept_sum(8, width), kept_sum(8, width),
            kept_sum(8, hidden),
            (array((pairs, 8, 128), F32), pl.BlockSpec((pairs, 8, 128), lambda *_: (0, 0, 0))),
        ],
        scalars=scal,
    )
    pair_all = pair_sums[:, :5].transpose(1, 0, 2)
    vectors = [
        sums_one[0], sums_one[1], pair_all[2:].reshape(-1), down_sums[3], down_sums[1], down_sums[2],
        up_sums[0], down_sums[0],
    ]
    small = jnp.concatenate(
        [vector.reshape(n_dp, -1) for vector in vectors + [pair_all[:2].reshape(-1)]], axis=1
    )
    small = small * scale
    (output,) = line.call(
        "output", output_kernel, (blocks,),
        [(act, rows_of(hidden)), param(down_weight), param(down_bias), (middle, rows_of(width))],
        [(array((slots, width)), rows_of(width))],
    )
    jobs("up1", up)
    jobs("down0", down)
    jobs("qkv0", qkv_grad)
    jobs("up2", up)
    while qkv_grad.terms:
        jobs("qkv_rest", qkv_grad)
    jobs("down1", down)
    while up.terms:
        jobs("up_rest", up)
    jobs("down_x", down)
    square = qkv_grad.square + up.square + 0.5 * down.square
    small = jnp.concatenate([small, jnp.broadcast_to(square[:1], (n_dp, 128))], axis=1)
    for stage in place.stages():
        small = sum_of([small] + stage(small))

    cut = sum(vector.size for vector in vectors) // n_dp
    rotary_all = small[:, cut:-128].reshape(2, heads, 2, -1).sum(axis=2)
    rotary_sq = jnp.sum(rotary_all * rotary_all)
    weight_sq = small[0, -1] + jnp.sum(small[:, :cut] * small[:, :cut])
    here = lax.dynamic_index_in_dim(small, place.dp_at, 0, keepdims=False)
    shards, at = [], 0
    for vector in vectors:
        size = vector.size // n_dp
        shards.append(here[at : at + size])
        at += size
    gain_one, bias_one, qkv_vector, out_vector, gain_two, bias_two, up_vector, down_vector = shards

    qkv_cols = [
        block.reshape(-1, pairs // 2, 3, 128).transpose(0, 2, 1, 3) for block in qkv_grad.blocks()
    ]
    qkv_all = jnp.concatenate(qkv_cols, axis=2).reshape(-1, 3 * width)
    up_cols = up.blocks()
    split = hidden // 2
    return (
        output,
        input_grad,
        gain_one,
        bias_one,
        qkv_all,
        qkv_vector,
        rotary_all,
        jnp.concatenate([block[:, split:] for block in up_cols], axis=1),
        out_vector,
        gain_two,
        bias_two,
        jnp.concatenate([block[:, :split] for block in up_cols], axis=1),
        up_vector,
        jnp.concatenate(down.blocks(), axis=1),
        down_vector,
        weight_sq,
        rotary_sq,
    )


def solution(mesh):
    rows = P(("group", "dp"), None)
    placed = (rows, rows) + (P(),) * 13 + (P("group"), P(("group", "dp")))
    return jax.shard_map(
        functools.partial(local, mesh.shape["group"], mesh.shape["dp"]),
        mesh=mesh,
        in_specs=placed,
        out_specs=(
            rows, rows, P("dp"), P("dp"), P("dp", None), P("dp"), P(), P("dp", None), P("dp"),
            P("dp"), P("dp"), P("dp", None), P("dp"), P("dp", None), P("dp"), P(), P(),
        ),
        check_vma=False,
    )
```

```python
import functools
import math

import jax
import jax.numpy as jnp
import numpy as np
from jax import lax
from jax.experimental import pallas as pl
from jax.experimental.pallas import tpu as pltpu
from jax.sharding import PartitionSpec as P

EPSILON = 1e-06
NEG_FILL = -1e30
SIDES = (14, 20, 24)
F32 = jnp.float32
BF16 = jnp.bfloat16
MIB = 1 << 20


def dot(left, right, left_dim, right_dim):
    return lax.dot_general(
        left, right, (((left_dim,), (right_dim,)), ((), ())), preferred_element_type=F32
    )


def smem():
    return pl.BlockSpec(memory_space=pltpu.SMEM)


def whole(shape):
    return pl.BlockSpec(shape, lambda *_: (0,) * len(shape), pipeline_mode=pl.Buffered(1))


def array(shape, kind=BF16):
    return jax.ShapeDtypeStruct(shape, kind)


class Line:
    def __init__(self):
        self.last = []

    def call(
        self, name, body, grid, ins, outs, scratch=(), scalars=None, deps=(), limit=60, long=False
    ):
        lead = 0 if scalars is None else 1
        deps = list(deps) + self.last
        first_out = lead + len(ins) + len(deps)

        def kernel(*refs):
            body(*refs[: lead + len(ins)], *refs[first_out:])

        results = pl.pallas_call(
            kernel,
            name=name,
            grid_spec=pltpu.PrefetchScalarGridSpec(
                num_scalar_prefetch=lead,
                grid=grid,
                in_specs=[spec for _, spec in ins] + [anywhere()] * len(deps),
                out_specs=[spec for _, spec in outs],
                scratch_shapes=list(scratch),
            ),
            out_shape=[shape for shape, _ in outs],
            compiler_params=pltpu.CompilerParams(vmem_limit_bytes=limit * MIB),
            cost_estimate=pl.CostEstimate(
                flops=10**13 if long else 1 << 20, bytes_accessed=1 << 20, transcendentals=0
            ),
        )(*([] if scalars is None else [scalars]), *[value for value, _ in ins], *deps)
        self.last = [results[0]]
        return results


def anywhere():
    return pl.BlockSpec(memory_space=pl.ANY)


def lanes_of(ref):
    return ref[...].astype(F32).reshape(1, -1)


def clip(value, low, high):
    return jnp.minimum(jnp.maximum(value, low), high)


def position_table(slots):
    table = np.zeros((3, slots, 128), np.float32)
    index = np.arange(slots)
    for res, side in enumerate(SIDES):
        within = index % (side * side)
        for lane in (0, 64):
            table[res, index, lane + within // side] = 1
            table[res, index, lane + 32 + within % side] = 1
    return table.astype(jnp.bfloat16)


def weight_lanes():
    table = np.zeros((128, 256), np.float32)
    for index in range(32):
        table[index, :128] = index
        table[32 + index, 128:] = index
    return table.astype(jnp.bfloat16)


def for_each_image(info, slots, body):
    for res, side in enumerate(SIDES):
        patches = side * side

        @pl.when(info[0] == res)
        def _(patches=patches):
            for image in range(slots // patches):
                offset = image * patches
                start = offset // 16 * 16
                span = -(-patches // 16) * 16
                body(image, start, span, offset - start, patches)


def inside(shape, axis, offset, patches):
    index = lax.broadcasted_iota(jnp.int32, shape, axis)
    return (index >= offset) & (index < offset + patches)


def live_rows(info):
    side = jnp.where(info[0] == 0, SIDES[0], jnp.where(info[0] == 1, SIDES[1], SIDES[2]))
    return info[1] * side * side


def swap_halves(values, half):
    pieces = []
    lane = lax.broadcasted_iota(jnp.int32, (values.shape[0], 128), 1)
    first = lane % (2 * half) < half
    for at in range(0, values.shape[1], 128):
        piece = values[:, at : at + 128]
        pieces.append(
            jnp.where(first, pltpu.roll(piece, 128 - half, 1), pltpu.roll(piece, half, 1))
        )
    return pieces[0] if len(pieces) == 1 else jnp.concatenate(pieces, axis=1)


def combine_angles(trig, width):
    cos_row, sin_row = trig[:, :width], trig[:, width : 2 * width]
    cos_col, sin_col = trig[:, 2 * width : 3 * width], trig[:, 3 * width :]
    return cos_row * cos_col - sin_row * sin_col, sin_row * cos_col + cos_row * sin_col


ROWS = 384


def fill_angles(table, freq_ref, width):
    index = lax.broadcasted_iota(jnp.int32, (32, width), 0).astype(F32)
    lane = lax.broadcasted_iota(jnp.int32, (32, width), 1)
    sign = jnp.where(lane % 64 < 32, -1.0, 1.0).astype(F32)
    table[...] = jnp.zeros_like(table)
    for kind in range(2):
        angle = index * freq_ref[kind : kind + 1, :]
        for part, value in enumerate((jnp.cos(angle), jnp.sin(angle) * sign)):
            high = value.astype(BF16)
            low = (value - high.astype(F32)).astype(BF16)
            at = (2 * kind + part) * width
            table[32 * kind : 32 * kind + 32, at : at + width] = high
            table[64 + 32 * kind : 96 + 32 * kind, at : at + width] = low


def normed_rows(values):
    shifted = values - jnp.mean(values, axis=1, keepdims=True)
    inverse = lax.rsqrt(jnp.mean(shifted * shifted, axis=1, keepdims=True) + EPSILON)
    return shifted * inverse, inverse


def row_block(index):
    return pl.ds(pl.multiple_of(index * ROWS, ROWS), ROWS)


def column_half(size, which):
    return pl.ds(pl.multiple_of(which * size, size), size)


def each(count, body):
    def step(index, carry):
        body(index)
        return carry

    lax.fori_loop(0, count, step, 0)


class Outbox:
    def __init__(self, sems, first=0):
        self.sems, self.kinds, self.first = sems, [], first

    def kind(self, blocks, ends):
        self.kinds.append((blocks, ends))
        return len(self.kinds) - 1

    def copy(self, kind, block):
        source, target = self.kinds[kind][1](block)
        return pltpu.make_async_copy(source, target, self.sems.at[self.first + kind, block])

    def send(self, kind, block):
        self.copy(kind, block).start()

    def wait(self, kind):
        for block in range(self.kinds[kind][0]):
            self.copy(kind, block).wait()


def layer_kernel(
    scal, g1_ref, b1_ref, qb_ref, freq_ref, ob_ref, g2_ref, b2_ref, ub_ref,
    pos_hbm, tok_hbm, w_hbm, ow_hbm, uw_hbm, dw_hbm, cot_hbm,
    zero_ref, sums_ref, upsum_ref, dsent_hbm, down_hbm, usent_hbm, up_hbm, in_hbm, stat_hbm, tab_hbm,
    qkv_hbm, mid_hbm, act_hbm, branch_hbm, attg_hbm, grad_hbm,
    pos_s, tok_s, w_s, ow_s, uw_s, cot_s, tab_s, in_s, qkv_s, stat_s, att_s, mid_s, sec_s, act_s, slope_s,
    grad_s, tok_sem, load_sem, store_sem, grad_sem,
):
    slots, width = att_s.shape
    hidden = act_s.shape[1]
    blocks, pairs, tiles = slots // ROWS, width // 128, hidden // width
    half = width // 2

    def tokens(block):
        rows = row_block(block)
        return pltpu.make_async_copy(tok_hbm.at[rows], tok_s.at[rows], tok_sem.at[block])

    def load(at):
        source, target = (
            [(w_hbm.at[:, part * width : (part + 1) * width], w_s.at[part]) for part in range(3)]
            + [(pos_hbm.at[scal[0]], pos_s), (ow_hbm, ow_s), (uw_hbm, uw_s), (cot_hbm, cot_s)]
            + [(dw_hbm.at[part * width : (part + 1) * width], w_s.at[part]) for part in range(tiles)]
        )[at]
        return pltpu.make_async_copy(source, target, load_sem.at[at])

    out = Outbox(store_sem)

    def by_rows(source, target):
        return out.kind(blocks, lambda block: (source.at[row_block(block)], target.at[row_block(block)]))

    send_in, send_act, send_mid = (
        by_rows(source, target) for source, target in ((in_s, in_hbm), (act_s, act_hbm), (mid_s, mid_hbm))
    )
    send_qkv = out.kind(
        blocks, lambda block: (qkv_s.at[:, row_block(block)], qkv_hbm.at[:, row_block(block)])
    )
    send_tab = out.kind(1, lambda block: (tab_s, tab_hbm))
    send_stat = out.kind(1, lambda block: (stat_s, stat_hbm))
    for ref in (zero_ref, sums_ref, upsum_ref):
        ref[...] = jnp.zeros_like(ref)
    tokens(0).start()
    for at in range(4):
        load(at).start()
    for block in range(1, blocks):
        tokens(block).start()
    for at in range(4, 7):
        load(at).start()
    fill_angles(tab_s, freq_ref, width)
    out.send(send_tab, 0)
    for at in range(4):
        load(at).wait()

    def project(block):
        tokens(block).wait()
        rows = row_block(block)
        normed, _ = normed_rows(tok_s[rows, :].astype(F32))
        first_in = (normed * lanes_of(g1_ref) + lanes_of(b1_ref)).astype(BF16)
        in_s[rows, :] = first_in
        cosine, sine = combine_angles(dot(pos_s[rows, :], tab_s[...], 1, 0), width)
        for part in range(3):
            bias = qb_ref[part * width : (part + 1) * width].astype(F32).reshape(1, -1)
            projected = dot(first_in, w_s[part], 1, 0) + bias
            if part < 2:
                projected = projected * cosine + swap_halves(projected, 32) * sine
            if part == 0:
                projected = projected * 0.125
            projected = projected.astype(BF16)
            for pair in range(pairs):
                qkv_s[part * pairs + pair, rows, :] = projected[:, pair * 128 : pair * 128 + 128]
        out.send(send_in, block)
        out.send(send_qkv, block)

    each(blocks, project)

    def attend(pair):
        cols = column_half(128, pair)
        q_ref, k_ref, v_ref = (qkv_s.at[part * pairs + pair] for part in range(3))
        att_s[:, cols] = v_ref[...]
        live = live_rows(scal)

        def image_step(image, start, span, offset, patches):
            rows = slice(start, start + span)
            exact = span == patches
            turned = v_ref[rows, :].T
            mixed = []
            for head in range(2):
                lanes = slice(head * 64, head * 64 + 64)
                scores = dot(k_ref[rows, lanes], q_ref[rows, lanes], 1, 1)
                if not exact:
                    scores = jnp.where(inside(scores.shape, 0, offset, patches), scores, NEG_FILL)
                top = jnp.max(scores, axis=0, keepdims=True)
                powers = jnp.exp(scores - top)
                mass = jnp.sum(powers, axis=0, keepdims=True)
                mixed.append(dot(turned[lanes], powers.astype(BF16), 1, 0) * (1.0 / mass))
                stat_s[pair, image, head : head + 1, 0:span] = top + jnp.log(mass)
            result = jnp.concatenate(mixed, axis=0).T
            keep = lax.broadcasted_iota(jnp.int32, result.shape, 0) < live - start
            if not exact:
                keep = keep & inside(result.shape, 0, offset, patches)
            result = jnp.where(keep, result, att_s[rows, cols].astype(F32))
            att_s[rows, cols] = result.astype(BF16)

        for_each_image(scal, slots, image_step)

    for at in range(7, 7 + tiles):
        load(at).start()
    each(pairs, attend)
    out.send(send_stat, 0)
    load(4).wait()
    load(5).wait()

    def feed(block):
        rows = row_block(block)
        middle = tok_s[rows, :].astype(F32) + (dot(att_s[rows, :], ow_s[...], 1, 0) + lanes_of(ob_ref))
        mid_s[rows, :] = middle
        normed, _ = normed_rows(middle)
        second_in = (normed * lanes_of(g2_ref) + lanes_of(b2_ref)).astype(BF16)
        sec_s[rows, :] = second_in
        scale = math.sqrt(2.0 / math.pi)
        for at in range(0, hidden, 768):
            cols = slice(at, at + 768)
            pre = dot(second_in, uw_s[:, cols], 1, 0) + ub_ref[cols].astype(F32).reshape(1, -1)
            square = pre * pre
            bent = jnp.tanh(pre * (scale + (scale * 0.044715) * square))
            gate = 0.5 + 0.5 * bent
            act_s[rows, cols] = (pre * gate).astype(BF16)
            lean = pre * (scale + (3.0 * scale * 0.044715) * square)
            slope_s[rows, cols] = (gate * (1.0 + (1.0 - bent) * lean)).astype(BF16)
        for kind in (send_act, send_mid):
            out.send(kind, block)

    each(blocks, feed)
    load(6).wait()
    cot_s[...] = live_cotangent(scal, cot_s, 0).astype(BF16)

    def grad_copies(tile, slot):
        rows = pl.ds(pl.multiple_of(tile * width, width), width)
        return [
            pltpu.make_async_copy(
                grad_s.at[slot, :, column_half(half, which)], target.at[rows], grad_sem.at[slot, at])
            for at, (which, target) in enumerate(((1 - scal[2], dsent_hbm), (scal[2], down_hbm)))
        ]

    def down_grad(tile):
        slot = lax.rem(tile, 2)

        @pl.when(tile >= 2)
        def _():
            for copy in grad_copies(tile - 2, slot):
                copy.wait()

        grad_s[slot] = dot(act_s[:, column_half(width, tile)], cot_s[...], 0, 0)
        for copy in grad_copies(tile, slot):
            copy.start()

    each(tiles, down_grad)
    for kind in (send_in, send_mid):
        out.wait(kind)
    for at in range(7, 7 + tiles):
        load(at).wait()
    branch_s, attg_s = in_s, tok_s
    late = Outbox(store_sem, len(out.kinds))
    late_kinds = [
        late.kind(blocks, lambda block, source=source, target=target: (
            source.at[row_block(block)], target.at[row_block(block)]))
        for source, target in ((branch_s, branch_hbm), (attg_s, attg_hbm), (mid_s, grad_hbm))
    ]

    def back_rows(block):
        rows = row_block(block)
        up_low = cot_s[rows, :]
        upstream = up_low.astype(F32)
        for part in range(tiles):
            cols = slice(part * width, (part + 1) * width)
            act_grad = dot(up_low, w_s[part], 1, 1)
            hidden_low = (slope_s[rows, cols].astype(F32) * act_grad).astype(BF16)
            slope_s[rows, cols] = hidden_low
            upsum_ref[0:1, cols] += jnp.sum(hidden_low.astype(F32), axis=0, keepdims=True)
        back = dot(slope_s[rows, :], uw_s[...], 1, 1)
        normed, inverse = normed_rows(mid_s[rows, :])
        scaled = back * lanes_of(g2_ref)
        inner = (
            scaled
            - jnp.mean(scaled, axis=1, keepdims=True)
            - normed * jnp.mean(scaled * normed, axis=1, keepdims=True)
        )
        middle_grad = upstream + inverse * inner
        mid_s[rows, :] = middle_grad
        branch = middle_grad.astype(BF16)
        branch_s[rows, :] = branch
        attg_s[rows, :] = dot(branch, ow_s[...], 1, 1).astype(BF16)
        sums_ref[0:1, :] += jnp.sum(upstream, axis=0, keepdims=True)
        sums_ref[1:2, :] += jnp.sum(back * normed, axis=0, keepdims=True)
        sums_ref[2:3, :] += jnp.sum(back, axis=0, keepdims=True)
        sums_ref[3:4, :] += jnp.sum(branch.astype(F32), axis=0, keepdims=True)
        for kind in late_kinds:
            late.send(kind, block)

    each(blocks, back_rows)

    def up_copy(tile, slot, wait):
        for first, target in ((0, usent_hbm), (tiles // 2, up_hbm)):

            @pl.when((tile >= first) & (tile < first + tiles // 2))
            def _(first=first, target=target):
                copy = pltpu.make_async_copy(
                    grad_s.at[slot], target.at[:, column_half(width, tile - first)], grad_sem.at[slot, 0]
                )
                copy.wait() if wait else copy.start()

    def up_grad(tile):
        slot = lax.rem(tile, 2)

        @pl.when(tile < 2)
        def _():
            for copy in grad_copies(tile + tiles - 2, slot):
                copy.wait()

        @pl.when(tile >= 2)
        def _():
            up_copy(tile - 2, slot, True)

        side = jnp.where(tile < tiles // 2, 1 - scal[2], scal[2])
        place = side * (tiles // 2) + lax.rem(tile, tiles // 2)
        grad_s[slot] = dot(sec_s[...], slope_s[:, column_half(width, place)], 0, 0)
        up_copy(tile, slot, False)

    each(tiles, up_grad)
    slot = tiles % 2
    up_copy(jnp.int32(tiles - 2), slot, True)
    grad_s[slot] = dot(att_s[...], branch_s[...], 0, 0)
    copies = [
        pltpu.make_async_copy(
            grad_s.at[slot, :, column_half(half, which)],
            target.at[:, hidden // 2 : hidden // 2 + half], grad_sem.at[slot, at])
        for at, (which, target) in enumerate(((1 - scal[2], usent_hbm), (scal[2], up_hbm)))
    ]
    for copy in copies:
        copy.start()
    up_copy(jnp.int32(tiles - 1), (tiles - 1) % 2, True)
    for copy in copies:
        copy.wait()
    for kind in (send_act, send_qkv, send_tab, send_stat):
        out.wait(kind)
    for kind in late_kinds:
        late.wait(kind)


def zeros_kernel(out_ref):
    out_ref[...] = jnp.zeros_like(out_ref)


def live_cotangent(info, cot_ref, first_row):
    row = lax.broadcasted_iota(jnp.int32, cot_ref.shape, 0) + first_row
    return jnp.where(row < live_rows(info), cot_ref[...].astype(F32), 0.0)


def attend_back_kernel(
    info, pos_ref, t0, t1, t2, t3, lanes_ref, in_ref, q_ref, k_ref, v_ref, up_ref, stat_ref,
    *rest,
):
    dw_refs, (gq_ref, gk_ref, gv_ref, sums_ref, dq_acc, dk_acc, dv_acc) = rest[:-7], rest[-7:]
    @pl.when(info[0] < 2)
    def _():
        for acc in (dq_acc, dk_acc, dv_acc):
            acc[...] = jnp.zeros_like(acc)

    def image_step(image, start, span, offset, patches):
        rows = slice(start, start + span)
        exact = span == patches
        for head in range(2):
            lanes = slice(head * 64, head * 64 + 64)
            query, key = q_ref[rows, lanes], k_ref[rows, lanes]
            value, upstream = v_ref[rows, lanes], up_ref[rows, lanes]
            probs = jnp.exp(dot(key, query, 1, 1) - stat_ref[image, head : head + 1, 0:span])
            if not exact:
                keep = inside(probs.shape, 0, offset, patches)
                keep = keep & inside(probs.shape, 1, offset, patches)
                probs = jnp.where(keep, probs, 0.0)
            prob_grad = dot(value, upstream, 1, 1)
            inner = jnp.sum(probs * prob_grad, axis=0, keepdims=True)
            score_low = (probs * (prob_grad - inner)).astype(BF16)
            value_grad = dot(probs.astype(BF16), upstream, 1, 0)
            key_grad = dot(score_low, query, 1, 0)
            query_grad = dot(key.T, score_low, 1, 0).T
            if exact:
                dq_acc[rows, lanes] = query_grad
                dk_acc[rows, lanes] = key_grad
                dv_acc[rows, lanes] = value_grad
            else:
                dq_acc[rows, lanes] += query_grad
                dk_acc[rows, lanes] += key_grad
                dv_acc[rows, lanes] += value_grad

    for_each_image(info, q_ref.shape[0], image_step)
    pos = pos_ref[...]
    table = jnp.concatenate([t0[...], t1[...], t2[...], t3[...]], axis=1)
    cosine, sine = combine_angles(dot(pos, table, 1, 0), 128)
    places = dot(pos, lanes_ref[...], 1, 0)
    lane = lax.broadcasted_iota(jnp.int32, (1, 128), 1)
    sign = jnp.where(lane % 64 < 32, 1.0, -1.0)
    angle_grad = None
    sums_ref[...] = jnp.zeros_like(sums_ref)
    for row, (acc, low_ref, out_ref, up, down) in enumerate(
        ((dq_acc, q_ref, gq_ref, 0.125, 8.0), (dk_acc, k_ref, gk_ref, 1.0, 1.0))
    ):
        grad = acc[...] * up
        swapped = swap_halves(grad, 32)
        term = swapped * (low_ref[...].astype(F32) * down)
        angle_grad = term if angle_grad is None else angle_grad + term
        pre = (grad * cosine - swapped * sine).astype(BF16)
        out_ref[...] = pre
        sums_ref[2 + row : 3 + row, :] = jnp.sum(pre.astype(F32), axis=0, keepdims=True)
    value_low = dv_acc[...].astype(BF16)
    gv_ref[...] = value_low
    sums_ref[4:5, :] = jnp.sum(value_low.astype(F32), axis=0, keepdims=True)
    for row in range(2):
        place = places[:, row * 128 : row * 128 + 128]
        sums_ref[row : row + 1, :] = sign * jnp.sum(place * angle_grad, axis=0, keepdims=True)
    grads = jnp.concatenate([gq_ref[...], gk_ref[...], gv_ref[...]], axis=1)
    weight_grad = dot(in_ref[...], grads, 0, 0)
    if len(dw_refs) == 1:
        dw_refs[0][...] = weight_grad
    else:
        for at, ref in enumerate(dw_refs):

            @pl.when(pl.program_id(0) == at)
            def _(ref=ref):
                ref[...] = weight_grad


def input_kernel(
    scal, tok_ref, gain_ref, grad_ref, w_ref, down_ref, up_ref, other_ref, own_ref, *refs
):
    pieces, (out_ref, sums_ref, down_out, up_out, pair_out) = refs[:6], refs[6:]
    width, half = tok_ref.shape[1], pieces[0].shape[1]

    @pl.when(pl.program_id(0) == 0)
    def _():
        sums_ref[...] = jnp.zeros_like(sums_ref)
        down_out[...] = down_ref[...]
        up_out[...] = up_ref[...]
        count = own_ref.shape[0]
        for pair in range(count):
            pair_out[count * (1 - scal[2]) + pair] = other_ref[pair]
            pair_out[count * scal[2] + pair] = own_ref[pair]

    back = None
    for side, which in enumerate((1 - scal[2], scal[2])):
        for part in range(3):
            cols = pl.ds(pl.multiple_of(part * width + which * half, half), half)
            term = dot(pieces[3 * side + part][...], w_ref[:, cols], 1, 1)
            back = term if back is None else back + term
    values = tok_ref[...].astype(F32)
    shifted = values - jnp.mean(values, axis=1, keepdims=True)
    inverse = lax.rsqrt(jnp.mean(shifted * shifted, axis=1, keepdims=True) + EPSILON)
    normed = shifted * inverse
    scaled = back * lanes_of(gain_ref)
    inner = (
        scaled
        - jnp.mean(scaled, axis=1, keepdims=True)
        - normed * jnp.mean(scaled * normed, axis=1, keepdims=True)
    )
    out_ref[...] = (grad_ref[...] + inverse * inner).astype(BF16)
    sums_ref[0:1, :] += jnp.sum(back * normed, axis=0, keepdims=True)
    sums_ref[1:2, :] += jnp.sum(back, axis=0, keepdims=True)


def output_kernel(act_ref, dw_ref, db_ref, mid_ref, out_ref):
    out_ref[...] = (
        mid_ref[...] + (dot(act_ref[...], dw_ref[...], 1, 0) + lanes_of(db_ref))
    ).astype(BF16)


def weight_of(counted, totals, slots):
    return F32(slots) / (3.0 * jnp.sum(jnp.where(counted > 0, totals, 0.0)))


def cross_part(cols):
    return (cols // 2 + 127) // 128 * 128


def combine(line, name, scal, counts, slots, own, got, shard, split, long=False):
    height, total = own.shape
    tile = max(2 * shard, height // 4)
    if shard % 16:
        split = None

    def kernel(scal_ref, *refs):
        first = len(counts) + 1
        counted, own_ref, got_refs, outs = (
            refs[: first - 1], refs[first - 1], refs[first : first + len(got)], refs[first + len(got) :]
        )
        totals = sum_of([ref[0:1] for ref in counted[2:]])
        mine = weight_of(counted[0][0:1], totals, slots)
        theirs = weight_of(counted[1][0:1], totals, slots)
        target = outs[-1] if split else outs[0]
        at = 0
        for got_ref in got_refs:
            cols = slice(at, at + got_ref.shape[1])
            target[:, cols] = own_ref[:, cols] * mine + got_ref[...] * theirs
            at += got_ref.shape[1]
        if split == "cross":
            first = cross_part(total)
            for at in range(tile // shard):
                for out, x_bit in ((outs[0], scal_ref[3]), (outs[1], 1 - scal_ref[3])):
                    rows = pl.ds(pl.multiple_of(at * shard + x_bit * (shard // 2), 8), shard // 2)
                    out[at] = target[rows, :first]
            for at in range(tile // shard // 2):
                for out, y_bit in ((outs[2], scal_ref[4]), (outs[3], 1 - scal_ref[4])):
                    rows = pl.ds(pl.multiple_of((2 * at + y_bit) * shard, 8), shard)
                    out[at] = target[rows, first:]
            return
        if split:
            stride = split // 2
            for at in range(tile // shard // stride):
                sides = (scal_ref[4], 1 - scal_ref[4]) if split == 4 else (0,)
                for index, (x_bit, y_bit) in enumerate(
                    ((x, y) for y in sides for x in (scal_ref[3], 1 - scal_ref[3]))
                ):
                    rows = (stride * at + y_bit) * shard + x_bit * (shard // 2)
                    outs[index][at] = target[pl.ds(pl.multiple_of(rows, 8), shard // 2), :]

    block = pl.BlockSpec((tile, total), lambda i, scal: (i, 0))
    got = list(got) if isinstance(got, (list, tuple)) else [got]
    ins = [(count, whole(count.shape)) for count in counts] + [(own, block)]
    ins += [(one, pl.BlockSpec((tile, one.shape[1]), lambda i, scal: (i, 0))) for one in got]
    if split is None:
        return line.call(
            name, kernel, (height // tile,), ins, [(array((height, total), F32), block)], scalars=scal,
            long=long,
        )[0]
    count = height // shard

    if split == "cross":
        first = cross_part(total)
        outs = [
            (array((count // shards, high, cols), F32), pl.BlockSpec(
                (tile // shard // shards, high, cols), lambda i, scal: (i, 0, 0)))
            for shards, high, cols in ((1, shard // 2, first), (2, shard, total - first)) for _ in range(2)
        ]
        return line.call(
            name, kernel, (height // tile,), ins, outs, [pltpu.VMEM((tile, total), F32)], scalars=scal
        )
    shards = split // 2
    outs = [(array((count // shards, shard // 2, total), F32), pl.BlockSpec(
        (tile // shard // shards, shard // 2, total), lambda i, scal: (i, 0, 0)))] * split
    return line.call(
        name, kernel, (height // tile,), ins, outs, [pltpu.VMEM((tile, total), F32)], scalars=scal
    )


class Place:
    def __init__(self, n_group, n_dp):
        self.n_group, self.n_dp = n_group, n_dp
        group_at, self.dp_at = lax.axis_index("group"), lax.axis_index("dp")
        self.core, self.x = lax.rem(group_at, 2), lax.div(group_at, 2)
        self.dp_bits = n_dp.bit_length() - 1
        self.dp = [lax.rem(lax.div(self.dp_at, 1 << bit), 2) for bit in range(self.dp_bits)]

    def group(self, value, mask):
        return lax.ppermute(value, "group", [(at, at ^ mask) for at in range(self.n_group)])

    def along(self, value, mask):
        return lax.ppermute(value, "dp", [(at, at ^ mask) for at in range(self.n_dp)])

    def across(self, value, group_mask, dp_mask):
        pairs = [
            (at * self.n_dp + dp, (at ^ group_mask) * self.n_dp + (dp ^ dp_mask))
            for at in range(self.n_group) for dp in range(self.n_dp)
        ]
        return lax.ppermute(value, ("group", "dp"), pairs)

    def stages(self):
        for bit in range(0, self.dp_bits, 2):
            masks = [1 << bit] if bit + 1 == self.dp_bits else [1 << bit, 2 << bit, 3 << bit]
            yield lambda v, masks=masks: [self.along(v, mask) for mask in masks]
        yield lambda v: [self.group(v, mask) for mask in (1, 2, 3)]


def sum_of(terms):
    result = terms[0]
    for term in terms[1:]:
        result = result + term
    return result


class Scatter:
    def __init__(self, place, kept, rows, cols, joint, widths=()):
        self.place, self.rows, self.widths = place, rows // place.n_dp, list(widths)
        self.first, self.terms, self.at_once = None, [None], joint is True
        self.bit = 0 if joint is False else 1
        if joint is None and not isinstance(kept, (list, tuple)):
            tall, fold = self.rows, 1
            while tall % 16:
                tall, fold = 2 * tall, 2 * fold
            first = cross_part(cols)
            view = kept.reshape(place.n_dp, self.rows, cols)
            one = view[..., :first].reshape(place.n_dp, 2, tall // 2, first // fold)
            two = view[..., first:].reshape(place.n_dp // 2, 2, tall, (cols - first) // fold)
            self.first = first // fold
            kept = [
                lax.dynamic_index_in_dim(value, at, 1, keepdims=False)
                for value, bit in ((one, place.x), (two, place.dp[0])) for at in (bit, 1 - bit)
            ]
        elif not isinstance(kept, (list, tuple)):
            tall, wide = self.rows, cols
            while tall % 16:
                tall, wide = 2 * tall, wide // 2
            shards = place.n_dp // 2 if joint else place.n_dp
            view = kept.reshape(shards, -1, 2, tall // 2, wide)

            def part(y, x):
                found = lax.dynamic_index_in_dim(view, y, 1, keepdims=False)
                return lax.dynamic_index_in_dim(found, x, 1, keepdims=False)

            kept = [
                part(y, x)
                for y in ((place.dp[0], 1 - place.dp[0]) if joint else (0,))
                for x in (place.x, 1 - place.x)
            ]
        self.cross = None
        if joint is None:
            self.cross = [kept[0], place.group(kept[1], 2), kept[2], place.along(kept[3], 1)]
            return
        masks = ((0, 0), (2, 0), (0, 1), (2, 1))
        self.terms = [[kept[0]]] + [
            [place.across(piece, *mask)] for piece, mask in zip(kept[1:], masks[1:])
        ]

    def job(self):
        place, bit = self.place, self.bit
        if self.cross is not None:
            (count, half, first), (_, shard, second) = self.cross[0].shape, self.cross[2].shape
            lead = count // 2
            ins = [(one.reshape(lead, 2, half, first), None) for one in self.cross[:2]]
            ins += [(one.reshape(lead, 2, half, second), None) for one in self.cross[2:]]

            def cross(scal, ins, outs):
                mine, over_y, over_x = outs
                y, x = scal[4], scal[3]
                mine[:, :, :first] = ins[0][:, y] + ins[1][:, y]
                mine[:, :, first:] = ins[2][:, x] + ins[3][:, x]
                over_y[...] = ins[0][:, 1 - y] + ins[1][:, 1 - y]
                over_x[...] = ins[2][:, 1 - x] + ins[3][:, 1 - x]

            def crossed(mine, over_y, over_x):
                self.terms = [[mine], [place.along(over_y, 1), place.group(over_x, 2)]]
                self.cross = None

            return ins, [
                (lead, half, first + second), (lead, half, first), (lead, half, second)
            ], cross, crossed
        lead, half, cols = self.terms[0][0].shape
        counts = [len(term) for term in self.terms]

        def read(refs, at):
            refs, found = list(refs), []
            for count in counts:
                rows = [ref[:, at] for ref in (refs.pop(0) for _ in range(count))]
                by_rows = rows[0].shape[-1] == cols
                found.append(rows[0] if count == 1 else jnp.concatenate(rows, axis=1 if by_rows else 2))
            return sum_of(found)

        if bit < place.dp_bits:
            wide, cut = self.widths.pop(0) if self.widths else (2, 1)
            wide, cut = min(wide, place.dp_bits - bit), cut if half % (8 * cut) == 0 else 1
            size = 1 << wide
            ins = [
                (one.reshape((lead // size, size) + one.shape[1:]), None)
                for term in self.terms for one in term
            ]

            def body(scal, ins, outs):
                for mask in range(size):
                    at = scal[4 + bit] if not mask % 2 else 1 - scal[4 + bit]
                    if wide == 2:
                        at = at + 2 * (scal[5 + bit] if mask < 2 else 1 - scal[5 + bit])
                    value = read(ins, at)
                    if mask == 0:
                        outs[0][...] = value
                    for part in range(cut if mask else 0):
                        rows = slice(part * half // cut, (part + 1) * half // cut)
                        outs[1 + (mask - 1) * cut + part][...] = value[:, rows]

            def then(mine, *sent):
                self.terms = [[mine]] + [
                    [place.along(value, mask << bit) for value in sent[(mask - 1) * cut : mask * cut]]
                    for mask in range(1, size)
                ]

            self.bit += wide
            shapes = [(lead // size, half, cols)]
            shapes += [(lead // size, half // cut, cols)] * ((size - 1) * cut)
            return ins, shapes, body, then
        ins = [(one.reshape((1, 1) + one.shape[1:]), None) for term in self.terms for one in term]
        self.terms = []

        def body(scal, ins, outs):
            mine = read(ins, 0)[0]
            outs[0][...] = mine
            outs[1][...] = jnp.broadcast_to(jnp.sum(mine * mine), outs[1].shape)

        def then(mine, square):
            self.square = square
            over_x = place.group(mine, 2)
            last = place.group(mine, 3) if self.at_once else place.group(over_x, 1)
            self.parts = [mine, place.group(mine, 1), over_x, last]

        return ins, [(half, cols), (8, 128)], body, then

    def blocks(self):
        place = self.place
        mine, core, x, both = self.parts
        found = []
        for at in (0, 1):
            here = jnp.where(place.core == at, mine, core)
            there = jnp.where(place.core == at, x, both)
            low, high = jnp.where(place.x == 0, here, there), jnp.where(place.x == 0, there, here)
            both_halves = jnp.concatenate([low, high])
            if both_halves.shape[0] != self.rows and self.first is not None:
                both_halves = [both_halves[:, : self.first], both_halves[:, self.first :]]
                found.append(jnp.concatenate([one.reshape(self.rows, -1) for one in both_halves], axis=1))
                continue
            found.append(both_halves.reshape(self.rows, -1))
        return found


class Scattered:
    def __init__(self, place, kept):
        self.place, self.got = place, None
        groups = [list(range(bit, place.n_dp, 2)) for bit in range(2)]
        self.mine = lax.psum_scatter(
            kept, "dp", scatter_dimension=0, tiled=True, axis_index_groups=groups
        )
        self.stage = 0

    def job(self):
        place, stage = self.place, self.stage
        self.stage += 1
        if stage == 0:
            rows, cols = self.mine.shape[0] // 2, self.mine.shape[1]

            def split(scal, ins, outs):
                for out, bit in zip(outs, (scal[4], 1 - scal[4])):
                    out[...] = ins[0][pl.ds(pl.multiple_of(bit * rows, 8), rows), :]

            def start(mine, sent):
                self.mine, self.got = mine, place.along(sent, 1)

            return [(self.mine, None)], [(rows, cols)] * 2, split, start
        if stage == 1:
            rows, cols = self.mine.shape[0] // 2, self.mine.shape[1]

            def halves(scal, ins, outs):
                for at, out in enumerate(outs):
                    part = slice(at * rows, (at + 1) * rows)
                    out[...] = ins[0][part] + ins[1][part]

            def exchange(*mine):
                self.mine, self.got = mine, [place.group(one, 2) for one in mine]

            return [(self.mine, None), (self.got, None)], [(rows, cols)] * 2, halves, exchange
        (rows, cols) = self.mine[0].shape
        ins = [(one, None) for one in (*self.mine, *self.got)]

        def body(scal, ins, outs):
            for at in range(2):
                outs[0][at * rows : (at + 1) * rows] = ins[at][...] + ins[2 + at][...]
            outs[1][...] = jnp.broadcast_to(jnp.sum(outs[0][...] * outs[0][...]), outs[1].shape)

        def then(mine, square):
            self.mine, self.square = mine, square
            self.theirs = place.group(mine, 1)

        return ins, [(2 * rows, cols), (8, 128)], body, then

    def blocks(self):
        first = self.place.core == 0
        return [jnp.where(first, self.mine, self.theirs), jnp.where(first, self.theirs, self.mine)]


def run_jobs(line, name, scal, jobs, long=False):
    ins = [
        (value, spec if spec is not None else whole(value.shape))
        for job in jobs for value, spec in job[0]
    ]
    outs = [
        (array(shape, F32), pl.BlockSpec(shape, functools.partial(lambda rank, *_: (0,) * rank, len(shape))))
        for job in jobs for shape in job[1]
    ]

    def kernel(scal_ref, *refs):
        at_in, at_out = 0, len(ins)
        for job_ins, job_outs, body, _ in jobs:
            body(
                scal_ref, refs[at_in : at_in + len(job_ins)], refs[at_out : at_out + len(job_outs)]
            )
            at_in += len(job_ins)
            at_out += len(job_outs)

    results = line.call(name, kernel, (1,), ins, outs, scalars=scal, long=long)
    at = 0
    for _, job_outs, _, then in jobs:
        then(*results[at : at + len(job_outs)])
        at += len(job_outs)


def local(
    n_group, n_dp, tokens, cotangent, norm1_gain, norm1_bias, qkv_weight, qkv_bias, rotary_freqs,
    out_weight, out_bias, norm2_gain, norm2_bias, up_weight, up_bias, down_weight, down_bias,
    group_res, images,
):
    slots, width = tokens.shape
    heads = rotary_freqs.shape[1]
    hidden = up_weight.shape[1]
    pairs = heads // 2
    blocks = slots // ROWS
    place = Place(n_group, n_dp)
    line = Line()
    scal = jnp.concatenate(
        [group_res, images, jnp.stack([place.core, place.x] + place.dp).astype(jnp.int32)]
    ).astype(jnp.int32)

    def rows_of(cols, first=0):
        return pl.BlockSpec((ROWS, cols), lambda i, *_: (clip(i - first, 0, blocks - 1), 0))

    def param(vector):
        return (vector, whole(vector.shape))

    def kept_sum(rows, cols):
        return (array((rows, cols), F32), pl.BlockSpec((rows, cols), lambda *_: (0, 0)))

    def in_hbm(shape, kind=BF16):
        return (array(shape, kind), anywhere())

    side = jnp.where(group_res[0] == 0, SIDES[0], jnp.where(group_res[0] == 1, SIDES[1], SIDES[2]))
    lane = lax.broadcasted_iota(jnp.int32, (8, 128), 1)
    patches = (images[0] * side * side).astype(F32)
    totals = jnp.where(lane == group_res[0], patches, 0.0)
    here = totals
    got = [place.group(totals, mask) for mask in (1, 2, 3)]
    beside = got[0]
    spread = jnp.broadcast_to(sum_of([totals] + got)[:1], (96 * n_dp, 128))
    totals = lax.psum_scatter(spread, "dp", scatter_dimension=0, tiled=True)[:8]

    half_freqs = jnp.concatenate([rotary_freqs, rotary_freqs], axis=-1).reshape(2, width)
    pos = jnp.asarray(position_table(slots))
    stat_shape = (slots // SIDES[0] ** 2, 8, -(-(SIDES[2] ** 2) // 128) * 128)
    tiles = hidden // width
    half = width // 2

    def vmem(*shape, kind=BF16):
        return pltpu.VMEM(shape, kind)

    (
        zero, down_sums, up_sums, down_sent, down_own, up_sent, up_own, first_in, stats, trig_table, qkv,
        middle, act, branch, att_grad, mid_grad,
    ) = line.call(
        "layer", layer_kernel, (1,),
        [
            param(norm1_gain), param(norm1_bias), param(qkv_bias), param(half_freqs), param(out_bias),
            param(norm2_gain), param(norm2_bias), param(up_bias), (pos, anywhere()), (tokens, anywhere()),
            (qkv_weight, anywhere()), (out_weight, anywhere()), (up_weight, anywhere()),
            (down_weight, anywhere()), (cotangent, anywhere()),
        ],
        [
            kept_sum(8, 128), kept_sum(8, width), kept_sum(8, hidden),
            in_hbm((hidden, half), F32), in_hbm((hidden, half), F32),
            in_hbm((width, hidden // 2 + half), F32), in_hbm((width, hidden // 2 + half), F32),
            in_hbm((slots, width)), in_hbm((pairs,) + stat_shape, F32), in_hbm((128, 4 * width)),
            in_hbm((3 * pairs, slots, 128)), in_hbm((slots, width), F32), in_hbm((slots, hidden)),
            in_hbm((slots, width)), in_hbm((slots, width)), in_hbm((slots, width), F32),
        ],
        [
            vmem(slots, 128), vmem(slots, width), vmem(tiles, width, width), vmem(width, width),
            vmem(width, hidden), vmem(slots, width), vmem(128, 4 * width), vmem(slots, width),
            vmem(3 * pairs, slots, 128), vmem(pairs, *stat_shape, kind=F32), vmem(slots, width),
            vmem(slots, width, kind=F32), vmem(slots, width), vmem(slots, hidden), vmem(slots, hidden),
            vmem(2, width, width, kind=F32),
            pltpu.SemaphoreType.DMA((blocks,)), pltpu.SemaphoreType.DMA((7 + tiles,)),
            pltpu.SemaphoreType.DMA((9, blocks)), pltpu.SemaphoreType.DMA((2, 2)),
        ],
        scalars=scal, limit=63, deps=[spread],
    )
    down_got = place.group(down_sent, 1)
    up_got = place.group(up_sent, 1)
    counts = [here, beside, totals + zero]
    line.call("mark", zeros_kernel, (1,), [], [kept_sum(8, 128)], long=True)
    scale = weight_of(here[0], counts[2][0], slots)
    shard = width // n_dp

    def reduce(name, own, got, rows, split, long=False):
        return combine(line, name, scal, counts, slots, own, got, rows, split, long)

    lanes_table = jnp.asarray(weight_lanes())

    def attend_back(own):
        count = pairs // 2

        def at(i, scal):
            return count * (scal[2] if own else 1 - scal[2]) + i

        def table_block(part):
            return pl.BlockSpec((128, 128), lambda i, scal: (0, part * pairs + at(i, scal)))

        def qkv_block(part):
            return pl.BlockSpec((None, slots, 128), lambda i, scal: (part * pairs + at(i, scal), 0, 0))

        out = (array((slots, count * 128)), pl.BlockSpec((slots, 128), lambda i, scal: (0, i)))
        return line.call(
            "attend_back", attend_back_kernel, (count,),
            [(pos, pl.BlockSpec((None, slots, 128), lambda i, scal: (scal[0], 0, 0)))]
            + [(trig_table, table_block(part)) for part in range(4)]
            + [param(lanes_table), param(first_in)]
            + [(qkv, qkv_block(part)) for part in range(3)]
            + [
                (att_grad, pl.BlockSpec((slots, 128), lambda i, scal: (0, at(i, scal)))),
                (stats, pl.BlockSpec(
                    (None,) + stat_shape, lambda i, scal: (at(i, scal), 0, 0, 0))),
            ],
            (
                [(array((width, count * 384), F32), pl.BlockSpec((width, 384), lambda i, scal: (0, i)))]
                if own else [kept_sum(width, 384)] * count
            )
            + [out] * 3
            + [(array((count, 8, 128), F32), pl.BlockSpec((None, 8, 128), lambda i, scal: (i, 0, 0)))],
            scratch=[pltpu.VMEM((slots, 128), F32)] * 3,
            scalars=scal,
        )

    def jobs(name, *chunks, long=False):
        run_jobs(line, name, scal, [chunk.job() for chunk in chunks], long)

    *other_grads, other_sums = attend_back(False)
    qkv_got = [place.group(other_grads.pop(0), 1) for _ in range(pairs // 2)]
    up = Scatter(
        place, reduce("up_sum", up_own, up_got, shard, "cross"), width, up_own.shape[1], None,
        ((1, 1), (1, 1)),
    )
    down = Scattered(place, reduce("down_sum", down_own, down_got, hidden // n_dp, None))
    qkv_own, *own_grads, own_sums = attend_back(True)
    jobs("up0", up)
    qkv_grad = Scatter(
        place, reduce("qkv_sum", qkv_own, qkv_got, shard, 4), width, qkv_own.shape[1], True
    )
    input_grad, sums_one, down_sums, up_sums, pair_sums = line.call(
        "input_grad", input_kernel, (blocks,),
        [
            (tokens, rows_of(width)), param(norm1_gain), (mid_grad, rows_of(width)),
            param(qkv_weight), param(down_sums), param(up_sums), param(other_sums), param(own_sums),
        ] + [(piece, rows_of(piece.shape[1])) for piece in other_grads + own_grads],
        [
            (array((slots, width)), rows_of(width)), kept_sum(8, width), kept_sum(8, width),
            kept_sum(8, hidden),
            (array((pairs, 8, 128), F32), pl.BlockSpec((pairs, 8, 128), lambda *_: (0, 0, 0))),
        ],
        scalars=scal,
    )
    pair_all = pair_sums[:, :5].transpose(1, 0, 2)
    vectors = [
        sums_one[0], sums_one[1], pair_all[2:].reshape(-1), down_sums[3], down_sums[1], down_sums[2],
        up_sums[0], down_sums[0],
    ]
    small = jnp.concatenate(
        [vector.reshape(n_dp, -1) for vector in vectors + [pair_all[:2].reshape(-1)]], axis=1
    )
    small = small * scale
    (output,) = line.call(
        "output", output_kernel, (blocks,),
        [(act, rows_of(hidden)), param(down_weight), param(down_bias), (middle, rows_of(width))],
        [(array((slots, width)), rows_of(width))],
    )
    jobs("up1", up)
    jobs("down0", down)
    jobs("qkv0", qkv_grad)
    jobs("up2", up)
    while qkv_grad.terms:
        jobs("qkv_rest", qkv_grad)
    jobs("down1", down)
    while up.terms:
        jobs("up_rest", up)
    jobs("down_x", down)
    square = qkv_grad.square + up.square + 0.5 * down.square
    small = jnp.concatenate([small, jnp.broadcast_to(square[:1], (n_dp, 128))], axis=1)
    for stage in place.stages():
        small = sum_of([small] + stage(small))

    cut = sum(vector.size for vector in vectors) // n_dp
    rotary_all = small[:, cut:-128].reshape(2, heads, 2, -1).sum(axis=2)
    rotary_sq = jnp.sum(rotary_all * rotary_all)
    weight_sq = small[0, -1] + jnp.sum(small[:, :cut] * small[:, :cut])
    here = lax.dynamic_index_in_dim(small, place.dp_at, 0, keepdims=False)
    shards, at = [], 0
    for vector in vectors:
        size = vector.size // n_dp
        shards.append(here[at : at + size])
        at += size
    gain_one, bias_one, qkv_vector, out_vector, gain_two, bias_two, up_vector, down_vector = shards

    qkv_cols = [
        block.reshape(-1, pairs // 2, 3, 128).transpose(0, 2, 1, 3) for block in qkv_grad.blocks()
    ]
    qkv_all = jnp.concatenate(qkv_cols, axis=2).reshape(-1, 3 * width)
    up_cols = up.blocks()
    split = hidden // 2
    return (
        output,
        input_grad,
        gain_one,
        bias_one,
        qkv_all,
        qkv_vector,
        rotary_all,
        jnp.concatenate([block[:, split:] for block in up_cols], axis=1),
        out_vector,
        gain_two,
        bias_two,
        jnp.concatenate([block[:, :split] for block in up_cols], axis=1),
        up_vector,
        jnp.concatenate(down.blocks(), axis=1),
        down_vector,
        weight_sq,
        rotary_sq,
    )


def solution(mesh):
    rows = P(("group", "dp"), None)
    placed = (rows, rows) + (P(),) * 13 + (P("group"), P(("group", "dp")))
    return jax.shard_map(
        functools.partial(local, mesh.shape["group"], mesh.shape["dp"]),
        mesh=mesh,
        in_specs=placed,
        out_specs=(
            rows, rows, P("dp"), P("dp"), P("dp", None), P("dp"), P(), P("dp", None), P("dp"),
            P("dp"), P("dp"), P("dp", None), P("dp"), P("dp", None), P("dp"), P(), P(),
        ),
        check_vma=False,
    )
```
